128 devices in a mesh: dp: 64 (over y_lo, x, z, core), tensor: 2 (over y_hi).
Axes of the slice: x: 4, y: 4 (y_hi: 2, y_lo: 2; y = y_hi * 2 + y_lo), z: 4, core: 2. Of those that a mesh axis runs over, the one named last changes fastest.
Arguments:
- tokens: bfloat16 [16384, 1024], P(('dp', 'tensor')), may hold values from -6 to 6
- routes: int32 [16384, 8], P('dp'), may hold values from 0 to 31, all different within a row; in each aligned block of 256 rows (0 to 255, 256 to 511, ...) at most 80 rows name the same one
- cotangent: bfloat16 [16384, 1024], P(('dp', 'tensor')), may hold values from -6 to 6
- attn_gain: bfloat16 [1024], P('dp'), may hold values from 0.5 to 1.5
- query_weight: bfloat16 [1024, 1024], P('dp', 'tensor'), may hold values from -0.1875 to 0.1875
- key_weight: bfloat16 [1024, 512], P('dp', 'tensor'), may hold values from -0.1875 to 0.1875
- value_weight: bfloat16 [1024, 512], P('dp', 'tensor'), may hold values from -0.1875 to 0.1875
- out_weight: bfloat16 [1024, 1024], P('dp', 'tensor'), may hold values from -0.75 to 0.75
- moe_gain: bfloat16 [1024], P('dp'), may hold values from 0.5 to 1.5
- router_weight: bfloat16 [1024, 32], P('dp'), may hold values from -0.09375 to 0.09375
- expert_gate: bfloat16 [1024, 32, 512], P('dp', None, 'tensor'), may hold values from -0.1875 to 0.1875
- expert_up: bfloat16 [1024, 32, 512], P('dp', None, 'tensor'), may hold values from -0.1875 to 0.1875
- expert_down: bfloat16 [1024, 32, 512], P('dp', None, 'tensor'), may hold values from -1 to 1
Outputs:
- output: bfloat16 [16384, 1024], P(('dp', 'tensor'))
- input_grad: bfloat16 [16384, 1024], P(('dp', 'tensor'))
- attn_gain_grad: float32 [1024], P('dp')
- query_weight_grad: float32 [1024, 1024], P('dp', 'tensor')
- key_weight_grad: float32 [1024, 512], P('dp', 'tensor')
- value_weight_grad: float32 [1024, 512], P('dp', 'tensor')
- out_weight_grad: float32 [1024, 1024], P('dp', 'tensor')
- moe_gain_grad: float32 [1024], P('dp')
- router_weight_grad: float32 [1024, 32], P('dp')
- expert_gate_grad: float32 [1024, 32, 512], P('dp', None, 'tensor')
- expert_up_grad: float32 [1024, 32, 512], P('dp', None, 'tensor')
- expert_down_grad: float32 [1024, 32, 512], P('dp', None, 'tensor')
The draws below stay inside these ranges and needn't reach their ends.
Inputs may be any that keep to these rules, and one draw needn't show every extreme that they name: `routes`: each row names 8 different experts. Within each sequence (each aligned block of 256 rows) no expert is named by more than 80 rows, and in some sequence one expert is named by exactly 80 rows.
All inputs are finite; a program needn't handle non-finite values.
Results may differ from the reference program's by a relative error of at most 0.018.
Values may be sent and summed in bfloat16 or wider, within the bound.
No kernel may reach another device: no remote copies, remote signals or barrier semaphores. Data moves between devices by JAX's collectives and lax.ppermute only.
A program may use at most 320 MiB of HBM per device.

```python
import math
import jax
import jax.numpy as jnp
import numpy as np
from jax import lax

D = 1024
HEADS = 16
KVH = 8
HDIM = 64
FF_E = 512
EXPERTS = 32
TOPK = 8
SEQ = 256
TOKENS = 16384
CAP = 80
N_DP = 64


def level_of(rng, shape, cuts, low, largest):
    level = 1.0
    for axis_at, blocks in cuts:
        heights = jax.random.uniform(jax.random.fold_in(jax.random.fold_in(rng, 6), axis_at), (blocks,), jnp.float32, low / len(cuts), largest / len(cuts))
        level = level * jnp.repeat(jnp.exp(heights), shape[axis_at] // blocks).reshape((-1,) + (1,) * (len(shape) - 1 - axis_at))
    return level


def deal_out(own_key, own, number, rows, number_of, top, reach, lean):
    ranking = jax.random.permutation(own_key, number_of)
    heavy_load, usual = portions_of(number_of, rows * top, reach, lean, True), portions_of(number_of, rows * top, reach, lean, False)
    places = jnp.arange(number_of)

    def named(lengths, turn):
        used = int((lengths > 0).sum())
        fixed = max(1, used // 4)
        passed = fixed + (places - fixed + turn * (used - fixed)) % max(1, number_of - fixed)
        return jnp.zeros((number_of,), jnp.int32).at[ranking[jnp.where(places < fixed, places, passed)]].set(jnp.asarray(lengths, jnp.int32))

    lengths = jnp.where(number % 4 == 0, named(heavy_load, number // 4), named(usual, number - number // 4 - 1))
    mixed = jax.random.permutation(jax.random.fold_in(own, 3), number_of)
    source_of, sink = mixed[0:number_of // 2 * 2:2], mixed[1:number_of // 2 * 2:2]
    margin = jnp.minimum(lengths[source_of] - 1, reach - lengths[sink]) // 2
    margin = jnp.where((source_of == ranking[0]) | (sink == ranking[0]) | (lengths[sink] == 0), 0, jnp.maximum(margin, 0))
    passed = jax.random.randint(jax.random.fold_in(own, 4), (number_of // 2,), 0, 1 << 20) % (margin + 1)
    lengths = lengths.at[source_of].add(-passed).at[sink].add(passed)
    items = jnp.searchsorted(jnp.cumsum(lengths), jnp.arange(rows * top), side="right").astype(jnp.int32)
    listing = items.reshape(top, rows).T
    listing = listing[jax.random.permutation(jax.random.fold_in(own, 1), rows)]
    turn = jax.random.randint(jax.random.fold_in(own, 2), (rows, 1), 0, top)
    return jnp.take_along_axis(listing, (jnp.arange(top)[None, :] + turn) % top, axis=1)


def portions_of(amount, total, bound, lean, full):
    portions = [(1 << 20) // math.isqrt(grade ** lean) + 1 for grade in range(1, amount + 1)]
    largest = bound if full else min(bound, max(-(-total // amount), total * portions[0] // sum(portions)))
    least = 1 if total - largest >= amount - 1 else 0
    given, spare = [largest] + [least] * (amount - 1), total - largest - least * (amount - 1)
    while spare > 0:
        candidates = [i for i in range(1, amount) if given[i] < largest] or [i for i in range(1, amount) if given[i] < bound]
        pool, budget = sum([portions[i] for i in candidates]), spare
        for i in candidates:
            addition = min(bound - given[i], max(1, budget * portions[i] // pool), spare)
            given[i] = given[i] + addition
            spare = spare - addition
    return np.array(given)


def normal_values(stream_key, extent, scale, bound, cuts=(), kind=jnp.bfloat16):
    values = scale * jax.random.normal(stream_key, extent, jnp.float32)
    if cuts:
        values = values * level_of(stream_key, extent, cuts, -0.22, 0.18)
    return jnp.clip(values, -bound, bound).astype(kind)


def setup_inputs(seed: int = 0) -> dict:
    splits = jax.random.split(jax.random.key(seed), 14)
    tokens = normal_values(splits[0], (TOKENS, D), 1.0, 6.0, ((0, 128),))
    routes_keys = jax.random.split(jax.random.fold_in(splits[1], 1), TOKENS // SEQ)
    routes_turns = jax.random.permutation(jax.random.fold_in(splits[1], 3), TOKENS // SEQ)
    routes = jax.vmap(lambda own, number: deal_out(jax.random.fold_in(splits[1], 2), own, number, SEQ, EXPERTS, TOPK, CAP, 1))(routes_keys, routes_turns).reshape((TOKENS, TOPK))
    cotangent = normal_values(splits[2], (TOKENS, D), 1.0, 6.0, ((0, 128),))
    attn_gain = jnp.clip(1.0 + 0.1 * jax.random.normal(splits[3], (D,), jnp.float32), 0.5, 1.5).astype(jnp.bfloat16)
    query_weight = normal_values(splits[4], (D, HEADS * HDIM), D ** -0.5, 0.1875, ((0, 64), (1, 2)))
    key_weight = normal_values(splits[5], (D, KVH * HDIM), D ** -0.5, 0.1875, ((0, 64), (1, 2)))
    value_weight = normal_values(splits[6], (D, KVH * HDIM), D ** -0.5, 0.1875, ((0, 64), (1, 2)))
    out_weight = normal_values(splits[7], (D, HEADS * HDIM), (HEADS * HDIM // 16) ** -0.5, 0.75, ((0, 64), (1, 2)))
    moe_gain = jnp.clip(1.0 + 0.1 * jax.random.normal(splits[8], (D,), jnp.float32), 0.5, 1.5).astype(jnp.bfloat16)
    router_weight = normal_values(splits[9], (D, EXPERTS), (4 * D) ** -0.5, 0.09375, ((0, 64),))
    expert_gate = normal_values(splits[10], (D, EXPERTS, FF_E), D ** -0.5, 0.1875, ((0, 64), (2, 2)))
    expert_up = normal_values(splits[11], (D, EXPERTS, FF_E), D ** -0.5, 0.1875, ((0, 64), (2, 2)))
    expert_down = normal_values(splits[12], (D, EXPERTS, FF_E), (FF_E // 16) ** -0.5, 1.0, ((0, 64), (2, 2)))
    return {"tokens": tokens, "routes": routes, "cotangent": cotangent, "attn_gain": attn_gain, "query_weight": query_weight, "key_weight": key_weight, "value_weight": value_weight, "out_weight": out_weight, "moe_gain": moe_gain, "router_weight": router_weight, "expert_gate": expert_gate, "expert_up": expert_up, "expert_down": expert_down}


@jax.custom_vjp
def low(v):
    return lax.optimization_barrier(v.astype(jnp.bfloat16)).astype(jnp.float32)

@jax.custom_vjp
def low_back(v):
    return v

def low_keep(v):
    return (low(v), None)

def low_pass(kept, grad):
    return (grad,)

def back_keep(v):
    return (v, None)

def back_low(kept, grad):
    return (low(grad),)
low.defvjp(low_keep, low_pass)
low_back.defvjp(back_keep, back_low)
exact_mode = lax.Precision.HIGHEST
norm_eps = 1e-06
rope_base = 10000.0

def rms_scale(values):
    return values * lax.rsqrt(lax.optimization_barrier(jnp.mean(values * values, axis=1, keepdims=True)) + norm_eps)

def rotary_tables(length):
    half_dim = HDIM // 2
    frequency = rope_base ** (-(jnp.arange(half_dim, dtype=jnp.float32) * 2.0 / HDIM))
    angles = jnp.arange(length, dtype=jnp.float32)[:, None] * frequency[None, :]
    angles = jnp.concatenate([angles, angles], axis=1)
    return (jnp.cos(angles), jnp.sin(angles))

def rotate(values, cos_tab, sin_tab):
    half_dim = values.shape[-1] // 2
    turned = jnp.concatenate([-values[..., half_dim:], values[..., :half_dim]], axis=-1)
    return values * cos_tab[:, None, :] + turned * sin_tab[:, None, :]

def slot_tables(route_rows):
    count = SEQ * TOPK
    flat_routes = route_rows.reshape(count)
    onehot = (flat_routes[:, None] == jnp.arange(EXPERTS, dtype=jnp.int32)[None, :]).astype(jnp.int32)
    before = jnp.cumsum(onehot, axis=0) - onehot
    places = lax.optimization_barrier(jnp.sum(before * onehot, axis=1))
    slot_of = flat_routes * CAP + places
    order = jnp.arange(count, dtype=jnp.int32)
    route_of = jnp.zeros((EXPERTS * CAP,), jnp.int32).at[slot_of].set(order)
    filled = jnp.zeros((EXPERTS * CAP,), jnp.float32).at[slot_of].set(1.0)
    return (slot_of, route_of // TOPK, filled)

def sequence_layer(rows, route_rows, attn_gain, query_weight, key_weight, value_weight, out_weight, moe_gain, router_weight, expert_gate, expert_up, expert_down):
    group = HEADS // KVH
    cos_tab, sin_tab = rotary_tables(SEQ)
    attn_in = low(rms_scale(rows) * attn_gain)
    query_lin = low_back(jnp.dot(attn_in, query_weight, precision=exact_mode))
    key_lin = low_back(jnp.dot(attn_in, key_weight, precision=exact_mode))
    values = low(low_back(jnp.dot(attn_in, value_weight, precision=exact_mode))).reshape(SEQ, KVH, HDIM)
    queries = low(rotate(query_lin.reshape(SEQ, HEADS, HDIM), cos_tab, sin_tab)).reshape(SEQ, KVH, group, HDIM)
    keys_rot = low(rotate(key_lin.reshape(SEQ, KVH, HDIM), cos_tab, sin_tab))
    scores = low_back(jnp.einsum('qngd,knd->ngqk', queries, keys_rot, precision=exact_mode) * (1.0 / math.sqrt(HDIM)))
    allowed = jnp.arange(SEQ)[:, None] >= jnp.arange(SEQ)[None, :]
    scores = jnp.where(allowed[None, None], scores, -1e+30)
    log_total = jax.nn.logsumexp(scores, axis=3, keepdims=True)
    attn_probs = low(jnp.exp(scores - log_total))
    context = low(low_back(jnp.einsum('ngqk,knd->qngd', attn_probs, values, precision=exact_mode))).reshape(SEQ, HEADS * HDIM)
    middle = rows + low_back(jnp.dot(context, out_weight.T, precision=exact_mode))
    moe_in = low(rms_scale(middle) * moe_gain)
    logits = jnp.dot(moe_in, router_weight, precision=exact_mode)
    route_gates = jax.nn.softmax(jnp.take_along_axis(logits, route_rows, axis=1), axis=1)
    slot_of, token_of, filled = slot_tables(route_rows)
    dispatched = (moe_in[token_of] * filled[:, None]).reshape(EXPERTS, CAP, D)
    gate_e = low_back(jnp.einsum('ecd,def->ecf', dispatched, expert_gate, precision=exact_mode))
    up_e = low_back(jnp.einsum('ecd,def->ecf', dispatched, expert_up, precision=exact_mode))
    hidden_e = low(jax.nn.silu(gate_e) * up_e)
    slot_out = low_back(jnp.einsum('ecf,def->ecd', hidden_e, expert_down, precision=exact_mode)).reshape(EXPERTS * CAP, D)
    routed_rows = slot_out[slot_of].reshape(SEQ, TOPK, D)
    return middle + lax.optimization_barrier(jnp.sum(route_gates[:, :, None] * routed_rows, axis=1))

def reference(tokens, routes, cotangent, attn_gain, query_weight, key_weight, value_weight, out_weight, moe_gain, router_weight, expert_gate, expert_up, expert_down):
    params = tuple((item.astype(jnp.float32) for item in (attn_gain, query_weight, key_weight, value_weight, out_weight, moe_gain, router_weight, expert_gate, expert_up, expert_down)))

    def forward(rows, *weights):

        def one_sequence(paired):
            return sequence_layer(paired[0], paired[1], *weights)
        blocks = (rows.reshape(N_DP, SEQ, D), routes.reshape(N_DP, SEQ, TOPK))
        return lax.map(jax.checkpoint(one_sequence), blocks).reshape(TOKENS, D)
    result, pullback = jax.vjp(forward, tokens.astype(jnp.float32), *params)
    grads = pullback(cotangent.astype(jnp.float32))
    return (result.astype(jnp.bfloat16), grads[0].astype(jnp.bfloat16), grads[1], grads[2], grads[3], grads[4], grads[5], grads[6], grads[7], grads[8], grads[9], grads[10])
```

```python
import functools

import jax
import jax.numpy as jnp
from jax import lax
from jax.experimental import pallas as pl
from jax.experimental.pallas import tpu as pltpu
from jax.sharding import Mesh, PartitionSpec as P

bf16 = jnp.bfloat16
f32 = jnp.float32

D = 1024
HDIM = 64
SEQ = 256
HALF = 128
EXPERTS = 32
CAP = 80
SLOTS = 16 * CAP
EXT = D + 128
PACK = 1664
NORM_EPS = 1e-06
ROPE_BASE = 10000.0
SCALE = 0.125
PLANE = ("x", "z")
CHIPS = ("yl", "x", "z")
NT = (((1,), (1,)), ((), ()))
TN = (((0,), (0,)), ((), ()))
VMEM_BYTES = 56 * 1024 * 1024


def mo(value, by):
    return pl.multiple_of(value, by)


def dot(a, b, dims=(((1,), (0,)), ((), ()))):
    return lax.dot_general(a, b, dims, preferred_element_type=f32)


def split(value):
    high = value.astype(bf16)
    return high, (value - high.astype(f32)).astype(bf16)


def iota(shape, dim):
    return lax.broadcasted_iota(jnp.int32, shape, dim)


def call(kernel, outs, args, scratch=(), grid=None, in_specs=None, out_specs=None, flops=0):
    smem = pl.BlockSpec(memory_space=pltpu.SMEM)
    params = pltpu.CompilerParams(vmem_limit_bytes=VMEM_BYTES)
    out_shape = [jax.ShapeDtypeStruct(shape, kind) for shape, kind in outs]
    nbytes = sum(a.size * a.dtype.itemsize for a in args) + sum(
        o.size * jnp.dtype(o.dtype).itemsize for o in out_shape
    )
    cost = pl.CostEstimate(flops=flops, bytes_accessed=nbytes, transcendentals=0)
    if grid is None:
        vmem = pl.BlockSpec(memory_space=pltpu.VMEM)
        in_specs = [smem] + [vmem] * (len(args) - 1)
        out_specs = [vmem] * len(outs)
        return pl.pallas_call(
            kernel,
            out_shape=out_shape,
            in_specs=in_specs,
            out_specs=out_specs,
            scratch_shapes=scratch,
            compiler_params=params,
            cost_estimate=cost,
        )(*args)
    return pl.pallas_call(
        kernel,
        grid=grid,
        out_shape=out_shape,
        in_specs=[smem] + in_specs,
        out_specs=out_specs,
        scratch_shapes=scratch,
        compiler_params=params,
        cost_estimate=cost,
    )(*args)


def route_kernel(pos, routes, cot_own, cot_oth, tab, mask_out, grad, sent, turned):
    half = pos[0]
    named = routes[...]
    lane = iota((SEQ, 128), 1)
    mask = jnp.zeros((SEQ, 128), f32)
    for k in range(named.shape[1]):
        mask = mask + jnp.where(named[:, k : k + 1] == lane, 1.0, 0.0)
    mask_out[...] = mask
    below = jnp.where(iota((SEQ, SEQ), 0) > iota((SEQ, SEQ), 1), 1.0, 0.0).astype(bf16)
    place = dot(below, mask.astype(bf16))
    turned[...] = jnp.where(mask > 0.0, place, -1.0).T
    slot = iota((CAP, SEQ), 0).astype(f32)
    for i in range(16):
        row = turned[pl.ds(half * 16 + i, 1), :]
        tab[i * CAP : (i + 1) * CAP, :] = jnp.where(slot == row, 1.0, 0.0).astype(bf16)
    grad[pl.ds(mo(half * HALF, HALF), HALF), :] = cot_own[...]
    grad[pl.ds(mo((1 - half) * HALF, HALF), HALF), :] = cot_oth[...]
    for n in range(4):
        cols = slice(n * 256, (n + 1) * 256)
        sent[:, cols] = dot(tab[...], grad[:, cols]).astype(bf16)


def swap_halves(u, low):
    return jnp.where(low, pltpu.roll(u, 224, 1), pltpu.roll(u, 32, 1))


def doubled(tile, low, which):
    other = pltpu.roll(tile, 64, 1)
    return jnp.where(low, tile, other) if which == 0 else jnp.where(low, other, tile)


def stacked(tile, low):
    zero = jnp.zeros_like(tile)
    return jnp.concatenate([jnp.where(low, tile, zero), jnp.where(low, zero, tile)], axis=0)


def attn_kernel(
    pos, tok_own, tok_oth, w_mine, w_oth, cos, sin,
    rows, w, aux, attn_in, q_out, k_out, v_out, ctx, lse_out, part,
):
    half, core = pos[0], pos[1]
    rows[pl.ds(mo(half * HALF, HALF), HALF), :] = tok_own[...]
    rows[pl.ds(mo((1 - half) * HALF, HALF), HALF), :] = tok_oth[...]
    for i in range(32):
        w[pl.ds(mo(i * 32 + core * 16, 16), 16), :] = w_mine[i]
        w[pl.ds(mo(i * 32 + (1 - core) * 16, 16), 16), :] = w_oth[i]
    aux[...] = w[:, 1536:PACK].astype(f32).T
    x = rows[...].astype(f32)
    factor = lax.rsqrt(jnp.mean(x * x, axis=1, keepdims=True) + NORM_EPS)
    attn_in[...] = (x * factor * aux[32:33, :]).astype(bf16)
    low32 = iota((SEQ, 256), 1) % 64 < 32
    low = iota((SEQ, 128), 1) < 64
    for n in range(4):
        lin = dot(attn_in[...], w[:, n * 256 : (n + 1) * 256])
        if n < 3:
            lin = lin * cos[...] + swap_halves(lin, low32) * sin[...]
        if n < 2:
            q_out[:, n * 256 : (n + 1) * 256] = lin.astype(bf16)
        else:
            dst = k_out if n == 2 else v_out
            for m in range(4):
                tile = lin[:, (m // 2) * 128 : (m // 2) * 128 + 128]
                dst[:, m * 128 : (m + 1) * 128] = doubled(tile, low, m % 2).astype(bf16)
    allowed = iota((2 * SEQ, SEQ), 0) % SEQ >= iota((2 * SEQ, SEQ), 1)
    for m in range(4):
        cols = slice(m * 128, (m + 1) * 128)
        scores = dot(stacked(q_out[:, cols], low), k_out[:, cols], NT) * SCALE
        scores = jnp.where(allowed, scores, -1e30)
        peak = jnp.max(scores, axis=1, keepdims=True)
        raised = jnp.exp(scores - peak)
        total = jnp.sum(raised, axis=1, keepdims=True)
        lse_out[m] = jnp.broadcast_to(peak + jnp.log(total), (2 * SEQ, 128))
        probs = (raised * (1.0 / total)).astype(bf16)
        both = dot(probs, v_out[:, cols])
        ctx[:, cols] = jnp.where(low, both[:SEQ], both[SEQ:]).astype(bf16)
    for n in range(4):
        outs = slice(n * 256, (n + 1) * 256)
        part[:, outs] = dot(ctx[...], w[outs, 1024:1536], NT).astype(bf16)


def mid_kernel(pos, rows, part_own, part_oth, aux, tab, mask, middle, moe_in, gates_out, sent):
    value = rows[...].astype(f32) + (part_own[...].astype(f32) + part_oth[...].astype(f32))
    middle[...] = value
    factor = lax.rsqrt(jnp.mean(value * value, axis=1, keepdims=True) + NORM_EPS)
    moe_in[...] = (value * factor * aux[33:34, :]).astype(bf16)
    logits = dot(moe_in[...], aux[...].astype(bf16), NT)
    chosen = jnp.where(mask[...] > 0.0, logits, -1e30)
    raised = jnp.exp(chosen - jnp.max(chosen, axis=1, keepdims=True)) * mask[...]
    gates = raised / jnp.sum(raised, axis=1, keepdims=True)
    gates_out[...] = gates
    high = gates.astype(bf16).astype(f32)
    extra = (high + pltpu.roll(gates - high, 32, 1)).astype(bf16)
    for n in range(4):
        cols = slice(n * 256, (n + 1) * 256)
        sent[:, cols] = dot(tab[...], moe_in[:, cols]).astype(bf16)
    sent[:, D:EXT] = dot(tab[...], extra).astype(bf16)


def expert_kernel(pos, x, c, w_a, w_b, w_c, w_d, dx, gate_g, up_g, scaled, w_down, w_gate, w_up):
    core, late, expert = pos[1], pos[2], pos[3]

    @pl.when(pl.program_id(0) == 0)
    def _():
        for src, at_late, at_core in (
            (w_a, late, core),
            (w_b, 1 - late, core),
            (w_c, late, 1 - core),
            (w_d, 1 - late, 1 - core),
        ):
            for i in range(16):
                rows = pl.ds(mo((at_late * 16 + i) * 32 + at_core * 16, 16), 16)
                for f in range(2):
                    for j, dst in enumerate((w_gate, w_up, w_down)):
                        dst[rows, f * 256 : (f + 1) * 256] = src[f, i, :, j * 256 : (j + 1) * 256]

    ext = x[:, D:EXT].astype(f32)
    lane = iota(ext.shape, 1)
    here, here_low = lane == expert, lane == expert + EXPERTS
    gate = jnp.sum(jnp.where(here | here_low, ext, 0.0), axis=1, keepdims=True)
    g = dot(x[:, :D], w_gate[...])
    u = dot(x[:, :D], w_up[...])
    sig = jax.nn.sigmoid(g)
    silu = g * sig
    hidden = (silu * u).astype(bf16).astype(f32)
    raw = dot(c[...], w_down[...])
    gate_grad = jnp.sum(hidden * raw, axis=1, keepdims=True)
    back = gate * raw
    gate_g[...] = (back * u * sig * (1.0 + g * (1.0 - sig))).astype(bf16)
    up_g[...] = (back * silu).astype(bf16)
    scaled[...] = (gate * hidden).astype(bf16)
    for n in range(4):
        cols = slice(n * 256, (n + 1) * 256)
        dx[:, cols] = (dot(gate_g[...], w_gate[cols, :], NT) + dot(up_g[...], w_up[cols, :], NT)).astype(bf16)
    high = gate_grad.astype(bf16).astype(f32)
    dx[:, D:EXT] = jnp.where(here, high, jnp.where(here_low, gate_grad - high, 0.0)).astype(bf16)


def expert_grad_kernel(pos, x, c, gate_g, up_g, scaled, w_down, y, mine, sent, held):
    core = pos[1]
    y[...] = dot(scaled[...], w_down[...], NT).astype(bf16)
    for j, (lhs, rhs) in enumerate(((x, gate_g), (x, up_g), (c, scaled))):
        held[...] = dot(lhs[...], rhs[...], TN).astype(bf16)
        for i in range(8):
            cols = slice(j * 512, (j + 1) * 512)
            mine[i, :, cols] = held[pl.ds(mo(i * 32 + core * 16, 16), 16), :]
            sent[i, :, cols] = held[pl.ds(mo(i * 32 + (1 - core) * 16, 16), 16), :]


def combine_kernel(pos, tab, got, out):
    for start in range(0, EXT, 256):
        cols = slice(start, min(start + 256, EXT))
        out[:, cols] = dot(tab[...], got[:, cols], TN).astype(bf16)


def finish_kernel(pos, tab, got, middle, own, sent, held):
    half = pos[0]
    for n in range(4):
        cols = slice(n * 256, (n + 1) * 256)
        held[:, cols] = dot(tab[...], got[:, cols], TN)
    mine = pl.ds(mo(half * HALF, HALF), HALF)
    own[...] = middle[mine, :] + held[mine, :]
    sent[...] = held[pl.ds(mo((1 - half) * HALF, HALF), HALF), :].astype(bf16)


def back_kernel(
    pos, comb_own, comb_oth, middle, moe_in, gates, aux, grad, rows, attn_in, w, q, k, v, ctx, lse, cos, sin,
    mg_own, part_own, part_sent, mine, sent, mg, dlin, cgrad, aog, apart, pack,
):
    half, core = pos[0], pos[1]
    low32 = iota((SEQ, 256), 1) % 64 < 32
    low = iota((SEQ, 128), 1) < 64
    gg = comb_own[:, D:EXT].astype(f32) + comb_oth[:, D:EXT].astype(f32)
    gg = gg + pltpu.roll(gg, 96, 1)
    gate = gates[...]
    logit_grad = gate * (gg - jnp.sum(gate * gg, axis=1, keepdims=True))
    lg_high, lg_low = split(logit_grad)
    router_t = aux[...].astype(bf16)
    moe_grad = comb_own[:, :D].astype(f32) + comb_oth[:, :D].astype(f32)
    moe_grad = moe_grad + dot(lg_high, router_t) + dot(lg_low, router_t)
    router_grad = dot(lg_high, moe_in[...], TN) + dot(lg_low, moe_in[...], TN)
    value = middle[...]
    factor = lax.rsqrt(jnp.mean(value * value, axis=1, keepdims=True) + NORM_EPS)
    normed = value * factor
    gain_two = jnp.sum(moe_grad * normed, axis=0, keepdims=True)
    inner = moe_grad * aux[33:34, :]
    mg[...] = grad[...].astype(f32) + factor * (
        inner - normed * jnp.mean(inner * normed, axis=1, keepdims=True)
    )
    mg_own[...] = mg[pl.ds(mo(half * HALF, HALF), HALF), :]
    aog[...] = mg[...].astype(bf16)
    for n in range(2):
        cols = slice(n * 256, (n + 1) * 256)
        cgrad[:, cols] = dot(aog[...], w[:, 1024 + n * 256 : 1280 + n * 256]).astype(bf16)
        pack[:, 1024 + n * 256 : 1280 + n * 256] = dot(aog[...], ctx[:, cols], TN).astype(bf16)
    allowed = iota((2 * SEQ, SEQ), 0) % SEQ >= iota((2 * SEQ, SEQ), 1)
    for m in range(4):
        cols = slice(m * 128, (m + 1) * 128)
        qs = stacked(q[:, cols], low)
        cs = stacked(cgrad[:, cols], low)
        scores = dot(qs, k[:, cols], NT) * SCALE
        probs = jnp.where(allowed, jnp.exp(scores - lse[m][:, :1]), 0.0)
        back = dot(cs, v[:, cols], NT)
        spread = jnp.sum(probs * back, axis=1, keepdims=True)
        sg = (probs * (back - spread)).astype(bf16)
        dq = dot(sg, k[:, cols])
        dlin[:, cols] = jnp.where(low, dq[:SEQ], dq[SEQ:]) * SCALE
        dk = dot(sg, qs, TN) * SCALE
        dv = dot(probs.astype(bf16), cs, TN)
        dk = dk + pltpu.roll(dk, 64, 1)
        dv = dv + pltpu.roll(dv, 64, 1)
        for base, val in ((512, dk), (768, dv)):
            at = slice(base + (m // 2) * 128, base + (m // 2) * 128 + 128)
            if m % 2 == 0:
                dlin[:, at] = val
            else:
                dlin[:, at] = jnp.where(low, dlin[:, at], val)
    lows = []
    for n in range(4):
        cols = slice(n * 256, (n + 1) * 256)
        lin = dlin[:, cols]
        if n < 3:
            lin = lin * cos[...] - swap_halves(lin, low32) * sin[...]
        lin = lin.astype(bf16)
        lows.append(lin)
        pack[:, cols] = dot(attn_in[...], lin, TN).astype(bf16)
    lows = jnp.concatenate(lows, axis=1)
    for n in range(4):
        cols = slice(n * 256, (n + 1) * 256)
        apart[:, cols] = dot(lows, w[cols, :1024], NT)
    part_own[...] = apart[pl.ds(mo(half * HALF, HALF), HALF), :]
    part_sent[...] = apart[pl.ds(mo((1 - half) * HALF, HALF), HALF), :].astype(bf16)
    x = rows[...].astype(f32)
    normed_one = x * lax.rsqrt(jnp.mean(x * x, axis=1, keepdims=True) + NORM_EPS)
    gain_one = jnp.sum(apart[...] * normed_one, axis=0, keepdims=True)
    at_row = iota((128, D), 0)
    small = jnp.where(at_row == 32, gain_one, jnp.where(at_row == 33, gain_two, router_grad))
    pack[:, 1536:PACK] = small.T.astype(bf16)
    for i in range(32):
        mine[i] = pack[pl.ds(mo(i * 32 + core * 16, 16), 16), :]
        sent[i] = pack[pl.ds(mo(i * 32 + (1 - core) * 16, 16), 16), :]


def input_kernel(pos, tok, aux, mg, part_own, part_oth, out):
    x = tok[...].astype(f32)
    factor = lax.rsqrt(jnp.mean(x * x, axis=1, keepdims=True) + NORM_EPS)
    normed = x * factor
    inner = (part_own[...] + part_oth[...].astype(f32)) * aux[32:33, :]
    inner = factor * (inner - normed * jnp.mean(inner * normed, axis=1, keepdims=True))
    out[...] = (mg[...] + inner).astype(bf16)


def rotary_tables():
    half_dim = HDIM // 2
    frequency = ROPE_BASE ** (-(jnp.arange(half_dim, dtype=f32) * 2.0 / HDIM))
    angles = jnp.arange(SEQ, dtype=f32)[:, None] * frequency[None, :]
    cos, sin = jnp.cos(angles), jnp.sin(angles)
    cos = jnp.concatenate([cos, cos], axis=1)
    sin = jnp.concatenate([-sin, sin], axis=1)
    return jnp.tile(cos, (1, 4)), jnp.tile(sin, (1, 4))


def swap(value, axis):
    return lax.ppermute(value, axis, [(0, 1), (1, 0)])


def body(
    tokens,
    routes,
    cotangent,
    attn_gain,
    query_weight,
    key_weight,
    value_weight,
    out_weight,
    moe_gain,
    router_weight,
    expert_gate,
    expert_up,
    expert_down,
):
    half, core, late = lax.axis_index("yh"), lax.axis_index("c"), lax.axis_index("yl")
    place = lax.axis_index("x") * 4 + lax.axis_index("z")
    pos = jnp.stack([half, core, late, half * 16 + place]).astype(jnp.int32)
    cos, sin = rotary_tables()

    packed = jnp.concatenate(
        [
            query_weight, key_weight, value_weight, out_weight, router_weight,
            attn_gain[:, None], moe_gain[:, None], jnp.zeros((16, 94), bf16),
        ],
        axis=1,
    )
    packed = jnp.broadcast_to(packed[None], (32, 16, PACK))
    w_mine = lax.all_to_all(packed, CHIPS, 0, 0, tiled=True)
    w_oth = swap(w_mine, "c")
    tok_oth = swap(tokens, "yh")
    cot_oth = swap(cotangent, "yh")

    tab, mask, grad, cot_sent = call(
        route_kernel,
        [((SLOTS, SEQ), bf16), ((SEQ, 128), f32), ((SEQ, D), bf16), ((SLOTS, D), bf16)],
        [pos, routes, cotangent, cot_oth],
        scratch=[pltpu.VMEM((128, SEQ), f32)],
        flops=700_000_000,
    )
    cot_slots = lax.all_to_all(cot_sent, PLANE, 0, 0, tiled=True)

    experts = jnp.stack([expert_gate, expert_up, expert_down])
    experts = experts.reshape(3, 16, 2, 16, 256).transpose(3, 2, 1, 0, 4).reshape(16, 2, 16, 768)
    experts = lax.all_to_all(experts, PLANE, 0, 0, tiled=True)
    e_own = lax.dynamic_index_in_dim(experts, half, 1, keepdims=False)
    e_oth = swap(lax.dynamic_index_in_dim(experts, 1 - half, 1, keepdims=False), "yh")
    e_a = jnp.stack([e_own, e_oth])
    e_b = swap(e_a, "yl")
    e_c = swap(e_a, "c")
    e_d = swap(e_b, "c")

    rows, w, aux, attn_in, q, k, v, ctx, lse, part = call(
        attn_kernel,
        [
            ((SEQ, D), bf16), ((D, PACK), bf16), ((128, D), f32), ((SEQ, D), bf16), ((SEQ, 512), bf16),
            ((SEQ, 512), bf16), ((SEQ, 512), bf16), ((SEQ, 512), bf16), ((4, 512, 128), f32), ((SEQ, D), bf16),
        ],
        [pos, tokens, tok_oth, w_mine, w_oth, cos, sin],
        flops=2_000_000_000,
    )
    part_oth = swap(part, "yh")
    middle, moe_in, gates, x_sent = call(
        mid_kernel,
        [((SEQ, D), f32), ((SEQ, D), bf16), ((SEQ, 128), f32), ((SLOTS, EXT), bf16)],
        [pos, rows, part, part_oth, aux, tab, mask],
        flops=800_000_000,
    )
    x_slots = lax.all_to_all(x_sent, PLANE, 0, 0, tiled=True)

    whole = pl.BlockSpec((2, 16, 16, 768), lambda i: (0, 0, 0, 0))
    by_row = lambda cols: pl.BlockSpec((256, cols), lambda i: (i, 0))
    dx, gate_g, up_g, scaled, w_down = call(
        expert_kernel,
        [
            ((SLOTS, EXT), bf16), ((SLOTS, 512), bf16), ((SLOTS, 512), bf16), ((SLOTS, 512), bf16),
            ((D, 512), bf16),
        ],
        [pos, x_slots, cot_slots, e_a, e_b, e_c, e_d],
        scratch=[pltpu.VMEM((D, 512), bf16), pltpu.VMEM((D, 512), bf16)],
        grid=(5,),
        in_specs=[by_row(EXT), by_row(D), whole, whole, whole, whole],
        out_specs=[by_row(EXT), by_row(512), by_row(512), by_row(512), pl.BlockSpec((D, 512), lambda i: (0, 0))],
        flops=8_000_000_000,
    )
    dx_back = lax.all_to_all(dx, PLANE, 0, 0, tiled=True)

    full = pl.BlockSpec((SLOTS, 512), lambda i: (0, 0))
    by_col = pl.BlockSpec((SLOTS, 256), lambda i: (0, i))
    pieces = pl.BlockSpec((8, 16, 1536), lambda i: (i, 0, 0))
    y, e_mine, e_sent = call(
        expert_grad_kernel,
        [((SLOTS, D), bf16), ((32, 16, 1536), bf16), ((32, 16, 1536), bf16)],
        [pos, x_slots, cot_slots, gate_g, up_g, scaled, w_down],
        scratch=[pltpu.VMEM((256, 512), bf16)],
        grid=(4,),
        in_specs=[by_col, by_col, full, full, full, pl.BlockSpec((256, 512), lambda i: (i, 0))],
        out_specs=[by_col, pieces, pieces],
        flops=5_400_000_000,
    )
    y_back = lax.all_to_all(y, PLANE, 0, 0, tiled=True)

    (comb,) = call(combine_kernel, [((SEQ, EXT), bf16)], [pos, tab, dx_back], flops=700_000_000)
    comb_oth = swap(comb, "yh")
    mg_own, part_own, part_sent, a_mine, a_sent = call(
        back_kernel,
        [
            ((HALF, D), f32), ((HALF, D), f32), ((HALF, D), bf16), ((32, 16, PACK), bf16), ((32, 16, PACK), bf16),
        ],
        [pos, comb, comb_oth, middle, moe_in, gates, aux, grad, rows, attn_in, w, q, k, v, ctx, lse, cos, sin],
        scratch=[
            pltpu.VMEM((SEQ, D), f32), pltpu.VMEM((SEQ, D), f32), pltpu.VMEM((SEQ, 512), bf16),
            pltpu.VMEM((SEQ, D), bf16), pltpu.VMEM((SEQ, D), f32), pltpu.VMEM((D, PACK), bf16),
        ],
        flops=4_000_000_000,
    )

    e_sum = (e_mine.astype(f32) + swap(e_sent, "c").astype(f32)).astype(bf16).reshape(2, 16, 16, 1536)
    e_keep = lax.dynamic_index_in_dim(e_sum, late, 0, keepdims=False)
    e_got = swap(lax.dynamic_index_in_dim(e_sum, 1 - late, 0, keepdims=False), "yl")
    e_sum = (e_keep.astype(f32) + e_got.astype(f32)).astype(bf16).reshape(16, 16, 3, 2, 256)
    e_sum = jnp.stack([e_sum[:, :, :, 0], swap(e_sum[:, :, :, 1], "yh")], axis=1)
    e_sum = lax.all_to_all(e_sum, PLANE, 0, 0, tiled=True)
    e_sum = e_sum.transpose(3, 2, 1, 0, 4).astype(f32)
    e_sum = jnp.where(half == 0, e_sum, e_sum[:, :, ::-1]).reshape(3, 16, EXPERTS, 256)

    out_own, out_sent = call(
        finish_kernel,
        [((HALF, D), f32), ((HALF, D), bf16)],
        [pos, tab, y_back, middle],
        scratch=[pltpu.VMEM((SEQ, D), f32)],
        flops=700_000_000,
    )
    output = (out_own + swap(out_sent, "yh").astype(f32)).astype(bf16)

    part_oth = swap(part_sent, "yh")
    a_sum = (a_mine.astype(f32) + swap(a_sent, "c").astype(f32)).astype(bf16)
    a_sum = lax.all_to_all(a_sum, CHIPS, 0, 0, tiled=True)
    a_sum = jnp.sum(a_sum.astype(f32), axis=0)
    gain_one = a_sum[:, 1568]
    gain_one = gain_one + swap(gain_one, "yh")
    (input_grad,) = call(
        input_kernel, [((HALF, D), bf16)], [pos, tokens, aux, mg_own, part_own, part_oth]
    )
    return (
        output,
        input_grad,
        gain_one,
        a_sum[:, :512],
        a_sum[:, 512:768],
        a_sum[:, 768:1024],
        a_sum[:, 1024:1536],
        a_sum[:, 1569],
        a_sum[:, 1536:1568],
        e_sum[0],
        e_sum[1],
        e_sum[2],
    )


def solution(mesh):
    fine = Mesh(mesh.devices.reshape(2, 4, 4, 2, 2), ("yl", "x", "z", "c", "yh"))
    dp, every = ("yl", "x", "z", "c"), ("yl", "x", "z", "c", "yh")
    in_specs = (
        P(every, None),
        P(dp, None),
        P(every, None),
        P(dp),
        P(dp, "yh"),
        P(dp, "yh"),
        P(dp, "yh"),
        P(dp, "yh"),
        P(dp),
        P(dp, None),
        P(dp, None, "yh"),
        P(dp, None, "yh"),
        P(dp, None, "yh"),
    )
    out_specs = (
        P(every, None),
        P(every, None),
        P(dp),
        P(dp, "yh"),
        P(dp, "yh"),
        P(dp, "yh"),
        P(dp, "yh"),
        P(dp),
        P(dp, None),
        P(dp, None, "yh"),
        P(dp, None, "yh"),
        P(dp, None, "yh"),
    )
    return jax.shard_map(body, mesh=fine, in_specs=in_specs, out_specs=out_specs, check_vma=False)
```

```python
import functools

import jax
import jax.numpy as jnp
from jax import lax
from jax.experimental import pallas as pl
from jax.experimental.pallas import tpu as pltpu
from jax.sharding import Mesh, PartitionSpec as P

bf16 = jnp.bfloat16
f32 = jnp.float32

D = 1024
HDIM = 64
SEQ = 256
HALF = 128
EXPERTS = 32
CAP = 80
SLOTS = 16 * CAP
EXT = D + 128
ROWS = 8 * CAP
PACK = 1664
W_ROWS = 208
NORM_EPS = 1e-06
ROPE_BASE = 10000.0
SCALE = 0.125
PLANE = ("x", "z")
NT = (((1,), (1,)), ((), ()))
TN = (((0,), (0,)), ((), ()))
VMEM_BYTES = 65000 * 1024


def mo(value, by):
    return pl.multiple_of(value, by)


def dot(a, b, dims=(((1,), (0,)), ((), ()))):
    return lax.dot_general(a, b, dims, preferred_element_type=f32)


def split(value):
    high = value.astype(bf16)
    return high, (value - high.astype(f32)).astype(bf16)


def iota(shape, dim):
    return lax.broadcasted_iota(jnp.int32, shape, dim)


def call(kernel, outs, args, scratch=(), grid=None, in_specs=None, out_specs=None, us=1, late_from=None, prefetch=False):
    smem = pl.BlockSpec(memory_space=pltpu.SMEM)
    params = pltpu.CompilerParams(vmem_limit_bytes=VMEM_BYTES)
    out_shape = [jax.ShapeDtypeStruct(shape, kind) for shape, kind in outs]
    nbytes = sum(a.size * a.dtype.itemsize for a in args) + sum(
        o.size * jnp.dtype(o.dtype).itemsize for o in out_shape
    )
    cost = pl.CostEstimate(flops=int(us * 1.15e9) + 1000, bytes_accessed=nbytes if us else 1000, transcendentals=0)
    if grid is None:
        vmem = pl.BlockSpec(memory_space=pltpu.VMEM)
        early = len(args) if late_from is None else late_from
        in_specs = [smem] + [vmem] * (early - 1) + [pl.BlockSpec(memory_space=pl.ANY)] * (len(args) - early)
        out_specs = [vmem] * len(outs)
        return pl.pallas_call(
            kernel,
            out_shape=out_shape,
            in_specs=in_specs,
            out_specs=out_specs,
            scratch_shapes=scratch,
            compiler_params=params,
            cost_estimate=cost,
        )(*args)
    if not prefetch:
        return pl.pallas_call(
            kernel,
            grid=grid,
            out_shape=out_shape,
            in_specs=[smem] + in_specs,
            out_specs=out_specs,
            scratch_shapes=scratch,
            compiler_params=params,
            cost_estimate=cost,
        )(*args)
    return pl.pallas_call(
        kernel,
        grid_spec=pltpu.PrefetchScalarGridSpec(
            num_scalar_prefetch=1, grid=grid, in_specs=in_specs, out_specs=out_specs, scratch_shapes=scratch
        ),
        out_shape=out_shape,
        compiler_params=params,
        cost_estimate=cost,
    )(*args)


def route_kernel(pos, routes, cot_own, cot_oth, packed, tab, tab_t, mask_out, grad, sent, turned):
    half = pos[0]
    named = routes[...]
    lane = iota((SEQ, 128), 1)
    mask = jnp.zeros((SEQ, 128), f32)
    for k in range(named.shape[1]):
        mask = mask + jnp.where(named[:, k : k + 1] == lane, 1.0, 0.0)
    mask_out[...] = mask
    below = jnp.where(iota((SEQ, SEQ), 0) > iota((SEQ, SEQ), 1), 1.0, 0.0).astype(bf16)
    place = dot(below, mask.astype(bf16))
    turned[...] = jnp.where(mask > 0.0, place, -1.0).T
    slot = iota((CAP, SEQ), 0).astype(f32)
    for i in range(16):
        row = turned[pl.ds(half * 16 + i, 1), :]
        tab[i * CAP : (i + 1) * CAP, :] = jnp.where(slot == row, 1.0, 0.0).astype(bf16)
    for n in range(SLOTS // 128):
        cols = slice(n * 128, (n + 1) * 128)
        tab_t[:, cols] = tab[cols, :].astype(f32).T.astype(bf16)
    grad[pl.ds(mo(half * HALF, HALF), HALF), :] = cot_own[...]
    grad[pl.ds(mo((1 - half) * HALF, HALF), HALF), :] = cot_oth[...]
    for n in range(4):
        spread_blocks(sent, n, dot(tab[...], grad[:, n * 256 : (n + 1) * 256]).astype(bf16), 16)
    sent[:, ROWS : ROWS + 192, :] = packed[...]


def spread_blocks(dst, n, value, peers):
    for i in range(peers):
        for j in range(2):
            at = (2 * n + j) * CAP
            dst[i, at : at + CAP, :] = value[i * CAP : (i + 1) * CAP, j * 128 : (j + 1) * 128]


def gather_blocks(dst, src, peers, blocks):
    for i in range(peers):
        for j in range(blocks):
            dst[i * CAP : (i + 1) * CAP, j * 128 : (j + 1) * 128] = src[i, j * CAP : (j + 1) * CAP, :]


def pick(rows, value, other):
    return jnp.where(rows == 0, value, jnp.where(rows == 1, other, 0.0))


def swap_halves(u, low):
    return jnp.where(low, pltpu.roll(u, 224, 1), pltpu.roll(u, 32, 1))


def doubled(tile, low, which):
    other = pltpu.roll(tile, 64, 1)
    return jnp.where(low, tile, other) if which == 0 else jnp.where(low, other, tile)


def stacked(tile, low):
    zero = jnp.zeros_like(tile)
    return jnp.concatenate([jnp.where(low, tile, zero), jnp.where(low, zero, tile)], axis=0)


def attn_kernel(
    pos, tok_own, tok_oth, w_a, w_b, w_c, w_d, cos, sin,
    rows, w, w_o, aux, attn_in, q_out, k_out, v_out, ctx, lse_out, part, small,
):
    half, core, late = pos[0], pos[1], pos[2]
    rows[pl.ds(mo(half * HALF, HALF), HALF), :] = tok_own[...]
    rows[pl.ds(mo((1 - half) * HALF, HALF), HALF), :] = tok_oth[...]
    for src, at_late, at_core in (
        (w_a, late, core),
        (w_b, 1 - late, core),
        (w_c, late, 1 - core),
        (w_d, 1 - late, 1 - core),
    ):
        for i in range(16):
            at = pl.ds(mo((at_late * 16 + i) * 32 + at_core * 16, 16), 16)
            w[at, :] = src[i, :, :1024]
            w_o[at, :] = src[i, :, 1024:1536]
            small[at, :] = src[i, :, 1536:PACK]
    aux[...] = small[...].astype(f32).T
    x = rows[...].astype(f32)
    factor = lax.rsqrt(jnp.mean(x * x, axis=1, keepdims=True) + NORM_EPS)
    attn_in[...] = (x * factor * aux[32:33, :]).astype(bf16)
    low32 = iota((SEQ, 256), 1) % 64 < 32
    low = iota((SEQ, 128), 1) < 64
    for n in range(4):
        lin = dot(attn_in[...], w[:, n * 256 : (n + 1) * 256])
        if n < 3:
            lin = lin * cos[...] + swap_halves(lin, low32) * sin[...]
        if n < 2:
            q_out[:, n * 256 : (n + 1) * 256] = lin.astype(bf16)
        else:
            dst = k_out if n == 2 else v_out
            for m in range(4):
                tile = lin[:, (m // 2) * 128 : (m // 2) * 128 + 128]
                dst[:, m * 128 : (m + 1) * 128] = doubled(tile, low, m % 2).astype(bf16)
    allowed = iota((2 * SEQ, SEQ), 0) % SEQ >= iota((2 * SEQ, SEQ), 1)
    for m in range(4):
        cols = slice(m * 128, (m + 1) * 128)
        scores = dot(stacked(q_out[:, cols], low), k_out[:, cols], NT) * SCALE
        scores = jnp.where(allowed, scores, -1e30)
        peak = jnp.max(scores, axis=1, keepdims=True)
        raised = jnp.exp(scores - peak)
        total = jnp.sum(raised, axis=1, keepdims=True)
        lse_out[m] = jnp.broadcast_to(peak + jnp.log(total), (2 * SEQ, 128))
        probs = (raised * (1.0 / total)).astype(bf16)
        both = dot(probs, v_out[:, cols])
        ctx[:, cols] = jnp.where(low, both[:SEQ], both[SEQ:]).astype(bf16)
    for n in range(4):
        outs = slice(n * 256, (n + 1) * 256)
        part[:, outs] = dot(ctx[...], w_o[outs, :], NT).astype(bf16)


def mid_kernel(pos, rows, part_own, part_oth, aux, tab, mask, middle, moe_in, gates_out, sent, turned):
    half = pos[0]
    value = rows[...].astype(f32) + (part_own[...].astype(f32) + part_oth[...].astype(f32))
    middle[...] = value
    factor = lax.rsqrt(jnp.mean(value * value, axis=1, keepdims=True) + NORM_EPS)
    moe_in[...] = (value * factor * aux[33:34, :]).astype(bf16)
    logits = dot(moe_in[...], aux[...].astype(bf16), NT)
    chosen = jnp.where(mask[...] > 0.0, logits, -1e30)
    raised = jnp.exp(chosen - jnp.max(chosen, axis=1, keepdims=True)) * mask[...]
    gates = raised / jnp.sum(raised, axis=1, keepdims=True)
    gates_out[...] = gates
    turned[...] = gates.T
    for n in range(4):
        spread_blocks(sent, n, dot(tab[...], moe_in[:, n * 256 : (n + 1) * 256]).astype(bf16), 16)
    lane = iota((CAP, 128), 1)
    slots = jnp.zeros((CAP, 128), f32)
    for i in range(16):
        row = turned[pl.ds(half * 16 + i, 1), :]
        found = jnp.sum(tab[i * CAP : (i + 1) * CAP, :].astype(f32) * row, axis=1, keepdims=True)
        slots = jnp.where(lane == i, found, slots)
    slots = jnp.concatenate([slots, jnp.zeros((128 - CAP, 128), f32)], axis=0).T
    at = iota((16, 128), 0)
    for i in range(16):
        line = slots[i : i + 1, :]
        high = line.astype(bf16).astype(f32)
        sent[i, ROWS : ROWS + 16, :] = pick(at, high, line - high).astype(bf16)


def weights_kernel(pos, a0, a1, a2, a3, b0, b1, b2, b3, w_gate, w_up, w_down):
    core, late = pos[1], pos[2]
    for srcs, at_core in (((a0, a1, a2, a3), core), ((b0, b1, b2, b3), 1 - core)):
        for src, at_late, f in zip(srcs, (late, 1 - late, late, 1 - late), (0, 0, 1, 1)):
            for i in range(16):
                rows = pl.ds(mo((at_late * 16 + i) * 32 + at_core * 16, 16), 16)
                for j, dst in enumerate((w_gate, w_up, w_down)):
                    for h in range(2):
                        cols = slice(f * 256 + h * 128, f * 256 + h * 128 + 128)
                        dst[rows, cols] = src[i, (j * 2 + h) * 16 : (j * 2 + h + 1) * 16, :]


def expert_kernel(pos, x, c, w_gate, w_up, w_down, dx, gate_g, up_g, scaled, xs, cs):
    gather_blocks(xs, x, 4, 8)
    gather_blocks(cs, c, 4, 8)
    lines = x[:, ROWS : ROWS + 16, :].astype(f32).reshape(64, 128)
    lines = jnp.concatenate([lines, jnp.zeros((64, 128), f32)], axis=0).T[:CAP]
    gate = jnp.concatenate(
        [lines[:, 16 * i : 16 * i + 1] + lines[:, 16 * i + 1 : 16 * i + 2] for i in range(4)], axis=0
    )
    g = dot(xs[...], w_gate[...])
    u = dot(xs[...], w_up[...])
    sig = jax.nn.sigmoid(g)
    silu = g * sig
    hidden = (silu * u).astype(bf16).astype(f32)
    raw = dot(cs[...], w_down[...])
    gate_grad = jnp.sum(hidden * raw, axis=1, keepdims=True)
    back = gate * raw
    gate_g[...] = (back * u * sig * (1.0 + g * (1.0 - sig))).astype(bf16)
    up_g[...] = (back * silu).astype(bf16)
    scaled[...] = (gate * hidden).astype(bf16)
    for n in range(4):
        cols = slice(n * 256, (n + 1) * 256)
        value = dot(gate_g[...], w_gate[cols, :], NT) + dot(up_g[...], w_up[cols, :], NT)
        spread_blocks(dx, n, value.astype(bf16), 4)
    high = gate_grad.astype(bf16).astype(f32)
    lane = iota((CAP, 128), 1)
    slots = jnp.zeros((CAP, 128), f32)
    for i in range(4):
        rows = slice(i * CAP, (i + 1) * CAP)
        slots = slots + pick(lane - 16 * i, high[rows], gate_grad[rows] - high[rows])
    slots = jnp.concatenate([slots, jnp.zeros((128 - CAP, 128), f32)], axis=0).T
    for i in range(4):
        dx[i, ROWS : ROWS + 16, :] = slots[16 * i : 16 * (i + 1), :].astype(bf16)


def expert_grad_kernel(pos, x, c, gate_g, up_g, scaled, mine, sent, xs, cs, held):
    core = pos[1]
    gather_blocks(xs, x, 16, 2)
    gather_blocks(cs, c, 16, 2)
    for j, (lhs, rhs) in enumerate(((xs, gate_g), (xs, up_g), (cs, scaled))):
        held[...] = dot(lhs[...], rhs[...], TN).astype(bf16)
        for i in range(8):
            for dst, at_core in ((mine, core), (sent, 1 - core)):
                rows = pl.ds(mo(i * 32 + at_core * 16, 16), 16)
                for f in range(2):
                    for h in range(2):
                        cols = slice(f * 256 + h * 128, f * 256 + h * 128 + 128)
                        dst[0, f, i, (j * 2 + h) * 16 : (j * 2 + h + 1) * 16, :] = held[rows, cols]


def expert_out_kernel(pos, scaled, w_down, y):
    value = dot(scaled[...], w_down[...], NT).astype(bf16)
    for i in range(16):
        for j in range(2):
            y[i, j * CAP : (j + 1) * CAP, :] = value[i * CAP : (i + 1) * CAP, j * 128 : (j + 1) * 128]


def expert_sum_kernel(pos, mine, got, got_yl, got_yh, got_diag, out):
    out[:, :96, :] = (mine[0, 0].astype(f32) + got[0, 0].astype(f32) + got_yl[...].astype(f32)).astype(bf16)
    out[:, 96:, :] = (got_yh[...].astype(f32) + got_diag[...].astype(f32)).astype(bf16)


def expert_final_kernel(pos, got, *outs):
    half = pos[0]
    for part, at_half in enumerate((half, 1 - half)):
        for j in range(6):
            at = part * 96 + j * 16
            value = jnp.swapaxes(got[:, at : at + 16, :].astype(f32), 0, 1)
            cols = slice((j % 2) * 128, (j % 2) * 128 + 128)
            outs[j // 2][:, pl.ds(mo(at_half * 16, 16), 16), cols] = value


def combine_kernel(pos, tab_t, got, out, held):
    half = pos[0]
    gather_blocks(held, got, 16, 8)
    lines = got[:, ROWS : ROWS + 16, :].astype(f32).reshape(256, 128).T[:CAP]
    lane = iota((CAP, 128), 1)
    for i in range(16):
        e = half * 16 + i
        high, low = lines[:, 16 * i : 16 * i + 1], lines[:, 16 * i + 1 : 16 * i + 2]
        extra = jnp.where(lane == e, high, jnp.where(lane == e + EXPERTS, low, 0.0))
        held[i * CAP : (i + 1) * CAP, D:EXT] = extra.astype(bf16)
    for start in range(0, EXT, 256):
        cols = slice(start, min(start + 256, EXT))
        out[:, cols] = dot(tab_t[...], held[:, cols]).astype(bf16)


def finish_kernel(pos, tab_t, got, middle, own, sent, gathered, held):
    half = pos[0]
    gather_blocks(gathered, got, 16, 8)
    for n in range(4):
        cols = slice(n * 256, (n + 1) * 256)
        held[:, cols] = dot(tab_t[...], gathered[:, cols])
    mine = pl.ds(mo(half * HALF, HALF), HALF)
    own[...] = middle[mine, :] + held[mine, :]
    sent[...] = held[pl.ds(mo((1 - half) * HALF, HALF), HALF), :].astype(bf16)


def cut_rows(mine, sent, held, late, core, blocks):
    for i in range(32):
        at_late = late if i < 16 else 1 - late
        for dst, at_core in ((mine, core), (sent, 1 - core)):
            rows = pl.ds(mo((at_late * 16 + i % 16) * 32 + at_core * 16, 16), 16)
            for b in range(blocks):
                dst[i, b * 16 : (b + 1) * 16, :] = held[rows, b * 128 : (b + 1) * 128]


def back_kernel(
    pos, comb_own, comb_oth, middle, moe_in, gates, aux, grad,
    w_o_at, ctx_at, q_at, k_at, v_at, lse_at, cos_at, sin_at, attn_in_at, w_at, rows_at,
    mg_own, part_own, part_sent, mine, sent, gains,
    w_o, ctx, q, k, v, lse, cos, sin, attn_in, w, rows, sems, mg, aog, pack, cgrad, dlin, apart,
):
    half, core, late = pos[0], pos[1], pos[2]
    pairs = (
        (w_o_at, w_o), (ctx_at, ctx), (q_at, q), (k_at, k), (v_at, v), (lse_at, lse), (cos_at, cos), (sin_at, sin),
        (attn_in_at, attn_in), (w_at, w), (rows_at, rows),
    )
    loads = [pltpu.make_async_copy(src, dst, sems.at[i]) for i, (src, dst) in enumerate(pairs)]
    for load in loads:
        load.start()
    gg = comb_own[:, D:EXT].astype(f32) + comb_oth[:, D:EXT].astype(f32)
    gg = gg + pltpu.roll(gg, 96, 1)
    gate = gates[...]
    logit_grad = gate * (gg - jnp.sum(gate * gg, axis=1, keepdims=True))
    lg_high, lg_low = split(logit_grad)
    router_t = aux[...].astype(bf16)
    moe_grad = comb_own[:, :D].astype(f32) + comb_oth[:, :D].astype(f32)
    moe_grad = moe_grad + dot(lg_high, router_t) + dot(lg_low, router_t)
    value = middle[...]
    factor = lax.rsqrt(jnp.mean(value * value, axis=1, keepdims=True) + NORM_EPS)
    normed = value * factor
    gain_two = jnp.sum(moe_grad * normed, axis=0, keepdims=True)
    inner = moe_grad * aux[33:34, :]
    mg[...] = grad[...].astype(f32) + factor * (
        inner - normed * jnp.mean(inner * normed, axis=1, keepdims=True)
    )
    mg_own[...] = mg[pl.ds(mo(half * HALF, HALF), HALF), :]
    aog[...] = mg[...].astype(bf16)
    for load in loads[:2]:
        load.wait()
    for n in range(2):
        cols = slice(n * 256, (n + 1) * 256)
        cgrad[:, cols] = dot(aog[...], w_o[:, cols]).astype(bf16)
        pack[:, 1024 + n * 256 : 1280 + n * 256] = dot(aog[...], ctx[:, cols], TN).astype(bf16)
    router_grad = dot(lg_high, moe_in[...], TN) + dot(lg_low, moe_in[...], TN)
    low32 = iota((SEQ, 256), 1) % 64 < 32
    low = iota((SEQ, 128), 1) < 64
    allowed = iota((2 * SEQ, SEQ), 0) % SEQ >= iota((2 * SEQ, SEQ), 1)
    for load in loads[2:]:
        load.wait()
    for m in range(4):
        cols = slice(m * 128, (m + 1) * 128)
        qs = stacked(q[:, cols], low)
        cs = stacked(cgrad[:, cols], low)
        scores = dot(qs, k[:, cols], NT) * SCALE
        probs = jnp.where(allowed, jnp.exp(scores - lse[m][:, :1]), 0.0)
        back = dot(cs, v[:, cols], NT)
        spread = jnp.sum(probs * back, axis=1, keepdims=True)
        sg = (probs * (back - spread)).astype(bf16)
        dq = dot(sg, k[:, cols])
        dlin[:, cols] = jnp.where(low, dq[:SEQ], dq[SEQ:]) * SCALE
        dk = dot(sg, qs, TN) * SCALE
        dv = dot(probs.astype(bf16), cs, TN)
        dk = dk + pltpu.roll(dk, 64, 1)
        dv = dv + pltpu.roll(dv, 64, 1)
        for base, val in ((512, dk), (768, dv)):
            at = slice(base + (m // 2) * 128, base + (m // 2) * 128 + 128)
            if m % 2 == 0:
                dlin[:, at] = val
            else:
                dlin[:, at] = jnp.where(low, dlin[:, at], val)
    lows = []
    for n in range(4):
        cols = slice(n * 256, (n + 1) * 256)
        lin = dlin[:, cols]
        if n < 3:
            lin = lin * cos[...] - swap_halves(lin, low32) * sin[...]
        lin = lin.astype(bf16)
        lows.append(lin)
        pack[:, cols] = dot(attn_in[...], lin, TN).astype(bf16)
    lows = jnp.concatenate(lows, axis=1)
    for n in range(4):
        cols = slice(n * 256, (n + 1) * 256)
        apart[:, cols] = dot(lows, w[cols, :], NT)
    part_own[...] = apart[pl.ds(mo(half * HALF, HALF), HALF), :]
    part_sent[...] = apart[pl.ds(mo((1 - half) * HALF, HALF), HALF), :].astype(bf16)
    x = rows[...].astype(f32)
    normed_one = x * lax.rsqrt(jnp.mean(x * x, axis=1, keepdims=True) + NORM_EPS)
    gain_one = jnp.sum(apart[...] * normed_one, axis=0, keepdims=True)
    lines = jnp.concatenate([gain_one[:, n * 128 : (n + 1) * 128] for n in range(8)], axis=0)
    high = lines.astype(bf16).astype(f32)
    gains[...] = jnp.concatenate([high, lines - high], axis=0).astype(bf16)
    pack[:, 1536:PACK] = jnp.where(iota((128, D), 0) == 33, gain_two, router_grad).T.astype(bf16)
    cut_rows(mine, sent, pack, late, core, 13)


def input_kernel(pos, tok, aux, mg, part_own, part_oth, out):
    x = tok[...].astype(f32)
    factor = lax.rsqrt(jnp.mean(x * x, axis=1, keepdims=True) + NORM_EPS)
    normed = x * factor
    inner = (part_own[...] + part_oth[...].astype(f32)) * aux[32:33, :]
    inner = factor * (inner - normed * jnp.mean(inner * normed, axis=1, keepdims=True))
    out[...] = (mg[...] + inner).astype(bf16)


def final_kernel(pos, got, w_query, w_key, w_value, w_out, w_router, gain_two, gain_one):
    total = got[0].astype(f32)
    for i in range(1, 16):
        total = total + got[i].astype(f32)
    for base, dst, blocks in ((0, w_query, 4), (4, w_key, 2), (6, w_value, 2), (8, w_out, 4)):
        for b in range(blocks):
            at = (base + b) * 16
            dst[:, b * 128 : (b + 1) * 128] = total[at : at + 16, :]
    w_router[...] = total[192:208, :32]
    turned = jnp.concatenate([total[192:208, :], jnp.zeros((112, 128), f32)], axis=0).T
    gain_two[...] = turned[33:34, :16]
    gains = total[208:216, :] + total[216:224, :]
    at = pos[4]
    row = jnp.sum(jnp.where(iota((8, 128), 0) == at // 8, gains, 0.0), axis=0, keepdims=True)
    lanes = pltpu.roll(jnp.broadcast_to(row, (8, 128)), (128 - (at % 8) * 16) % 128, 1)
    gain_one[...] = lanes[0:1, :16]


def rotary_tables():
    column = iota((SEQ, 256), 1)
    frequency = ROPE_BASE ** (-((column % (HDIM // 2)).astype(f32) * 2.0 / HDIM))
    angles = iota((SEQ, 256), 0).astype(f32) * frequency
    sin = jnp.sin(angles)
    return jnp.cos(angles), jnp.where(column % HDIM < HDIM // 2, -sin, sin)


def swap(value, axis):
    if axis == "diag":
        return lax.ppermute(value, ("yl", "yh"), [(0, 3), (3, 0), (1, 2), (2, 1)])
    return lax.ppermute(value, axis, [(0, 1), (1, 0)])


def plane(value):
    return lax.all_to_all(value, PLANE, 0, 0, tiled=True)


def added(*values, gate=None):
    total = (values[0] if gate is None else after(values[0], gate)).astype(f32)
    for value in values[1:]:
        total = total + value.astype(f32)
    return total.astype(bf16)


def after(value, *others):
    return lax.optimization_barrier((value, *others))[0]


def at_index(value, i):
    return lax.dynamic_index_in_dim(value, i, 0, keepdims=False)


def body(
    tokens,
    routes,
    cotangent,
    attn_gain,
    query_weight,
    key_weight,
    value_weight,
    out_weight,
    moe_gain,
    router_weight,
    expert_gate,
    expert_up,
    expert_down,
):
    half, core, late = lax.axis_index("yh"), lax.axis_index("c"), lax.axis_index("yl")
    place = lax.axis_index("x") * 4 + lax.axis_index("z")
    pos = jnp.stack([half, core, late, half * 16 + place, (late * 16 + place) * 2 + core]).astype(jnp.int32)
    cos, sin = rotary_tables()

    packed = jnp.concatenate(
        [
            query_weight, key_weight, value_weight, out_weight, router_weight,
            attn_gain[:, None], moe_gain[:, None], jnp.zeros((16, 94), bf16),
        ],
        axis=1,
    )
    w_a = plane(jnp.broadcast_to(packed[None], (16, 16, PACK)))
    tok_oth = swap(tokens, "yh")
    cot_oth = swap(cotangent, "yh")
    cot_oth, tok_oth, cos, sin = lax.optimization_barrier((cot_oth, tok_oth, cos, sin))

    experts = jnp.stack([expert_gate, expert_up, expert_down])
    experts = experts.reshape(3, 16, 2, 16, 2, 128).transpose(3, 2, 0, 4, 1, 5).reshape(16, 192, 128)
    tab, tab_t, mask, grad, cot_sent = call(
        route_kernel,
        [
            ((SLOTS, SEQ), bf16), ((SEQ, SLOTS), bf16), ((SEQ, 128), f32), ((SEQ, D), bf16),
            ((16, ROWS + 192, 128), bf16),
        ],
        [pos, routes, cotangent, cot_oth, experts],
        scratch=[pltpu.VMEM((128, SEQ), f32)],
        us=5,
    )
    w_a = after(w_a, cot_sent)
    w_b = swap(w_a, "yl")
    w_c = swap(w_a, "c")
    w_d = swap(w_b, "c")
    cot_slots = plane(after(cot_sent, w_c))

    e_own = lax.dynamic_slice_in_dim(cot_slots, ROWS + 96 * half, 96, 1)
    e_oth = lax.dynamic_slice_in_dim(cot_slots, ROWS + 96 * (1 - half), 96, 1)
    pieces = [e_own, swap(e_own, "yl"), swap(e_oth, "yh"), swap(e_oth, "diag")]
    pieces = pieces + [swap(piece, "c") for piece in pieces]
    w_gate, w_up, w_down = call(weights_kernel, [((D, 512), bf16)] * 3, [pos] + pieces, us=4)

    rows, w, w_o, aux, attn_in, q, k, v, ctx, lse, part = call(
        attn_kernel,
        [
            ((SEQ, D), bf16), ((D, D), bf16), ((D, 512), bf16), ((128, D), f32), ((SEQ, D), bf16),
            ((SEQ, 512), bf16), ((SEQ, 512), bf16), ((SEQ, 512), bf16), ((SEQ, 512), bf16), ((4, 512, 128), f32),
            ((SEQ, D), bf16),
        ],
        [pos, tokens, tok_oth, w_a, w_b, w_c, w_d, cos, sin],
        scratch=[pltpu.VMEM((D, 128), bf16)],
        us=7,
    )
    part_oth = swap(part, "yh")
    middle, moe_in, gates, x_sent = call(
        mid_kernel,
        [((SEQ, D), f32), ((SEQ, D), bf16), ((SEQ, 128), f32), ((16, ROWS + 16, 128), bf16)],
        [pos, rows, part, part_oth, aux, tab, mask],
        scratch=[pltpu.VMEM((128, SEQ), f32)],
        us=3,
    )
    x_slots = plane(x_sent)

    whole = pl.BlockSpec((D, 512), lambda i, *pos: (0, 0))
    by_row = pl.BlockSpec((4 * CAP, 512), lambda i, *pos: (i, 0))
    by_peer = lambda rows: pl.BlockSpec((4, rows, 128), lambda i, *pos: (i, 0, 0))
    dx, gate_g, up_g, scaled = call(
        expert_kernel,
        [((16, ROWS + 16, 128), bf16), ((SLOTS, 512), bf16), ((SLOTS, 512), bf16), ((SLOTS, 512), bf16)],
        [pos, x_slots, cot_slots, w_gate, w_up, w_down],
        scratch=[pltpu.VMEM((4 * CAP, D), bf16), pltpu.VMEM((4 * CAP, D), bf16)],
        grid=(4,),
        in_specs=[by_peer(ROWS + 16), by_peer(ROWS), whole, whole, whole],
        out_specs=[by_peer(ROWS + 16), by_row, by_row, by_row],
        us=12,
    )
    dx_back = plane(dx)

    full = pl.BlockSpec((SLOTS, 512), lambda i, *pos: (0, 0))
    by_col = pl.BlockSpec((16, 2 * CAP, 128), lambda i, *pos: (0, i, 0))
    by_owner = pl.BlockSpec((1, 2, 8, 96, 128), lambda i, pos: ((i // 2 + pos[2]) % 2, 0, i % 2, 0, 0))
    e_mine, e_sent = call(
        expert_grad_kernel,
        [((2, 2, 16, 96, 128), bf16), ((2, 2, 16, 96, 128), bf16)],
        [pos, x_slots, cot_slots, gate_g, up_g, scaled],
        scratch=[
            pltpu.VMEM((SLOTS, 256), bf16), pltpu.VMEM((SLOTS, 256), bf16), pltpu.VMEM((256, 512), bf16),
        ],
        grid=(4,),
        in_specs=[by_col, by_col, full, full, full],
        out_specs=[by_owner, by_owner],
        us=0,
        prefetch=True,
    )


    e_got = swap(e_sent, "c")
    e_yl, e_yh, e_diag = (
        swap(added(e_mine[i, j], e_got[i, j]), axis) for i, j, axis in ((1, 0, "yl"), (0, 1, "yh"), (1, 1, "diag"))
    )
    (y,) = call(
        expert_out_kernel,
        [((16, ROWS, 128), bf16)],
        [pos, after(scaled, e_got), w_down],
        grid=(4,),
        in_specs=[full, pl.BlockSpec((256, 512), lambda i, *pos: (i, 0))],
        out_specs=[by_col],
        us=0,
    )
    dx_back = after(dx_back, e_yl)
    (comb,) = call(
        combine_kernel, [((SEQ, EXT), bf16)], [pos, tab_t, dx_back],
        scratch=[pltpu.VMEM((SLOTS, EXT), bf16)], us=0,
    )
    comb = after(comb, e_yh, e_diag)
    comb_oth = swap(comb, "yh")
    y_back = plane(y)
    by_first = pl.BlockSpec((1, 1, 16, 96, 128), lambda i, *pos: (0, 0, 0, 0, 0))
    by_third = pl.BlockSpec((16, 96, 128), lambda i, *pos: (0, 0, 0))
    (e_cat,) = call(
        expert_sum_kernel,
        [((16, 192, 128), bf16)],
        [pos, after(e_mine, comb), e_got, e_yl, e_yh, e_diag],
        grid=(1,),
        in_specs=[by_first, by_first, by_third, by_third, by_third],
        out_specs=[pl.BlockSpec((16, 192, 128), lambda i, *pos: (0, 0, 0))],
        us=0,
    )
    comb_oth = after(comb_oth, e_cat)
    mg_own, part_own, part_sent, a_mine, a_sent, gains = call(
        back_kernel,
        [
            ((HALF, D), f32), ((HALF, D), f32), ((HALF, D), bf16), ((32, W_ROWS, 128), bf16),
            ((32, W_ROWS, 128), bf16), ((16, 128), bf16),
        ],
        [
            pos, comb, comb_oth, middle, moe_in, gates, aux, grad,
            w_o, ctx, q, k, v, lse, cos, sin, attn_in, w, rows,
        ],
        late_from=8,
        scratch=[
            pltpu.VMEM((D, 512), bf16), pltpu.VMEM((SEQ, 512), bf16), pltpu.VMEM((SEQ, 512), bf16),
            pltpu.VMEM((SEQ, 512), bf16), pltpu.VMEM((SEQ, 512), bf16), pltpu.VMEM((4, 512, 128), f32),
            pltpu.VMEM((SEQ, 256), f32), pltpu.VMEM((SEQ, 256), f32), pltpu.VMEM((SEQ, D), bf16),
            pltpu.VMEM((D, D), bf16), pltpu.VMEM((SEQ, D), bf16), pltpu.SemaphoreType.DMA((11,)),
            pltpu.VMEM((SEQ, D), f32), pltpu.VMEM((SEQ, D), bf16), pltpu.VMEM((D, PACK), bf16),
            pltpu.VMEM((SEQ, 512), bf16), pltpu.VMEM((SEQ, D), f32), pltpu.VMEM((SEQ, D), f32),
        ],
        us=0,
    )

    a_got = swap(a_sent, "c")
    gains = gains.astype(f32)
    gains = gains[:8] + gains[8:]
    for axis in ("yh", "c"):
        gains = gains + swap(gains, axis)
    high = gains.astype(bf16)
    gains = jnp.concatenate([high, (gains - high.astype(f32)).astype(bf16)], axis=0)
    gains = jnp.broadcast_to(gains[None], (16, 16, 128))
    a_move = jnp.concatenate([added(a_mine[16:], a_got[16:], gate=y_back), gains], axis=1)
    a_yl = swap(a_move, "yl")
    out_own, out_sent = call(
        finish_kernel,
        [((HALF, D), f32), ((HALF, D), bf16)],
        [pos, tab_t, after(y_back, a_move), middle],
        scratch=[pltpu.VMEM((SLOTS, D), bf16), pltpu.VMEM((SEQ, D), f32)],
        us=0,
    )
    e_back = plane(after(e_cat, out_sent))
    a_sum = [added(a_mine[:16], a_got[:16], a_yl[:, :W_ROWS]), added(gains, a_yl[:, W_ROWS:])]
    a_sum = jnp.concatenate(a_sum, axis=1)
    total = plane(after(a_sum, e_back))

    part_oth = swap(after(part_sent, a_sum), "yh")
    (input_grad,) = call(
        input_kernel, [((HALF, D), bf16)], [pos, tokens, aux, mg_own, part_own, part_oth], us=0
    )
    w_query, w_key, w_value, w_out, w_router, gain_two, gain_one = call(
        final_kernel,
        [((16, n), f32) for n in (512, 256, 256, 512, 32)] + [((1, 16), f32)] * 2,
        [pos, total],
        us=2,
    )

    grad_gate, grad_up, grad_down = call(
        expert_final_kernel, [((16, EXPERTS, 256), f32)] * 3, [pos, after(e_back, input_grad)], us=0
    )

    output = (out_own + swap(after(out_sent, a_sum), "yh").astype(f32)).astype(bf16)
    return (
        output,
        input_grad,
        gain_one.reshape(16),
        w_query,
        w_key,
        w_value,
        w_out,
        gain_two.reshape(16),
        w_router,
        grad_gate,
        grad_up,
        grad_down,
    )


def solution(mesh):
    fine = Mesh(mesh.devices.reshape(2, 4, 4, 2, 2), ("yl", "x", "z", "c", "yh"))
    dp, every = ("yl", "x", "z", "c"), ("yl", "x", "z", "c", "yh")
    in_specs = (
        P(every, None),
        P(dp, None),
        P(every, None),
        P(dp),
        P(dp, "yh"),
        P(dp, "yh"),
        P(dp, "yh"),
        P(dp, "yh"),
        P(dp),
        P(dp, None),
        P(dp, None, "yh"),
        P(dp, None, "yh"),
        P(dp, None, "yh"),
    )
    out_specs = (
        P(every, None),
        P(every, None),
        P(dp),
        P(dp, "yh"),
        P(dp, "yh"),
        P(dp, "yh"),
        P(dp, "yh"),
        P(dp),
        P(dp, None),
        P(dp, None, "yh"),
        P(dp, None, "yh"),
        P(dp, None, "yh"),
    )
    return jax.shard_map(body, mesh=fine, in_specs=in_specs, out_specs=out_specs, check_vma=False)
```

```python
import functools

import jax
import jax.numpy as jnp
from jax import lax
from jax.experimental import pallas as pl
from jax.experimental.pallas import tpu as pltpu
from jax.sharding import Mesh, PartitionSpec as P

bf16 = jnp.bfloat16
f32 = jnp.float32

D = 1024
HDIM = 64
SEQ = 256
HALF = 128
EXPERTS = 32
CAP = 80
SLOTS = 16 * CAP
EXT = D + 128
ROWS = 8 * CAP
PACK = 1664
NORM_EPS = 1e-06
ROPE_BASE = 10000.0
SCALE = 0.125
PLANE = ("x", "z")
NT = (((1,), (1,)), ((), ()))
TN = (((0,), (0,)), ((), ()))
VMEM_BYTES = 65472 * 1024


def mo(value, by):
    return pl.multiple_of(value, by)


def dot(a, b, dims=(((1,), (0,)), ((), ()))):
    return lax.dot_general(a, b, dims, preferred_element_type=f32)


def split(value):
    high = value.astype(bf16)
    return high, (value - high.astype(f32)).astype(bf16)


def iota(shape, dim):
    return lax.broadcasted_iota(jnp.int32, shape, dim)


def call(kernel, outs, args, scratch=(), grid=None, in_specs=None, out_specs=None, us=1, late_from=None, late_outs=0, prefetch=False):
    smem = pl.BlockSpec(memory_space=pltpu.SMEM)
    params = pltpu.CompilerParams(vmem_limit_bytes=VMEM_BYTES)
    out_shape = [jax.ShapeDtypeStruct(shape, kind) for shape, kind in outs]
    nbytes = sum(a.size * a.dtype.itemsize for a in args) + sum(
        o.size * jnp.dtype(o.dtype).itemsize for o in out_shape
    )
    cost = pl.CostEstimate(flops=int(us * 1.15e9) + 1000, bytes_accessed=nbytes if us else 1000, transcendentals=0)
    if grid is None:
        vmem = pl.BlockSpec(memory_space=pltpu.VMEM)
        early = len(args) if late_from is None else late_from
        in_specs = [smem] + [vmem] * (early - 1) + [pl.BlockSpec(memory_space=pl.ANY)] * (len(args) - early)
        out_specs = [vmem] * (len(outs) - late_outs) + [pl.BlockSpec(memory_space=pl.ANY)] * late_outs
        return pl.pallas_call(
            kernel,
            out_shape=out_shape,
            in_specs=in_specs,
            out_specs=out_specs,
            scratch_shapes=scratch,
            compiler_params=params,
            cost_estimate=cost,
        )(*args)
    if not prefetch:
        return pl.pallas_call(
            kernel,
            grid=grid,
            out_shape=out_shape,
            in_specs=[smem] + in_specs,
            out_specs=out_specs,
            scratch_shapes=scratch,
            compiler_params=params,
            cost_estimate=cost,
        )(*args)
    return pl.pallas_call(
        kernel,
        grid_spec=pltpu.PrefetchScalarGridSpec(
            num_scalar_prefetch=1, grid=grid, in_specs=in_specs, out_specs=out_specs, scratch_shapes=scratch
        ),
        out_shape=out_shape,
        compiler_params=params,
        cost_estimate=cost,
    )(*args)


def copies(pairs, sems, first=0):
    return [pltpu.make_async_copy(src, dst, sems.at[first + i]) for i, (src, dst) in enumerate(pairs)]


def start(loads):
    for load in loads:
        load.start()


def wait(loads):
    for load in loads:
        load.wait()


def place_rows(w, pieces, late, core):
    at = ((late, core), (1 - late, core), (late, 1 - core), (1 - late, 1 - core))
    return [(src, w.at[at_late, :, at_core]) for src, (at_late, at_core) in zip(pieces, at)]


def flat(w, first, last):
    return w[:, :, :, :, first:last].reshape(D, last - first)


def pack_kernel(pos, w_query, w_key, w_value, w_out, router, gain_one, gain_two, out):
    at = iota((128, 128), 0)
    rest = jnp.zeros((1, 112), f32)
    first, second = (jnp.concatenate([gain[...].astype(f32), rest], axis=1) for gain in (gain_one, gain_two))
    gains = pick(at, first, second)
    gains = gains.T[:16]
    wide = jnp.concatenate([router[...].astype(f32), jnp.zeros((16, 96), f32)], axis=1)
    small = (wide + pltpu.roll(gains, EXPERTS, 1)).astype(bf16)
    for i in range(16):
        out[i, :, :512] = w_query[...]
        out[i, :, 512:768] = w_key[...]
        out[i, :, 768:1024] = w_value[...]
        out[i, :, 1024:1536] = w_out[...]
        out[i, :, 1536:] = small


def route_kernel(pos, routes, tab, tab_t, mask_out, turned):
    half = pos[0]
    named = routes[...]
    lane = iota((SEQ, 128), 1)
    mask = jnp.zeros((SEQ, 128), f32)
    for k in range(named.shape[1]):
        mask = mask + jnp.where(named[:, k : k + 1] == lane, 1.0, 0.0)
    mask_out[...] = mask
    below = jnp.where(iota((SEQ, SEQ), 0) > iota((SEQ, SEQ), 1), 1.0, 0.0).astype(bf16)
    place = dot(below, mask.astype(bf16))
    turned[...] = jnp.where(mask > 0.0, place, -1.0).T
    slot = iota((CAP, SEQ), 0).astype(f32)
    for i in range(16):
        row = turned[pl.ds(half * 16 + i, 1), :]
        tab[i * CAP : (i + 1) * CAP, :] = jnp.where(slot == row, 1.0, 0.0).astype(bf16)
    for n in range(SLOTS // 128):
        cols = slice(n * 128, (n + 1) * 128)
        tab_t[:, cols] = tab[cols, :].astype(f32).T.astype(bf16)


def dispatch_kernel(pos, tab, cot_own, cot_oth, packed, grad, sent):
    half = pos[0]
    sent[:, ROWS : ROWS + 192, :] = packed[...]
    grad[pl.ds(mo(half * HALF, HALF), HALF), :] = cot_own[...]
    grad[pl.ds(mo((1 - half) * HALF, HALF), HALF), :] = cot_oth[...]
    for n in range(4):
        spread_blocks(sent, n, dot(tab[...], grad[:, n * 256 : (n + 1) * 256]).astype(bf16), 16)


def spread_blocks(dst, n, value, peers):
    for i in range(peers):
        for j in range(2):
            at = (2 * n + j) * CAP
            dst[i, at : at + CAP, :] = value[i * CAP : (i + 1) * CAP, j * 128 : (j + 1) * 128]


def gather_blocks(dst, src, peers, blocks):
    for i in range(peers):
        for j in range(blocks):
            dst[i * CAP : (i + 1) * CAP, j * 128 : (j + 1) * 128] = src[i, j * CAP : (j + 1) * CAP, :]


def pick(rows, value, other):
    return jnp.where(rows == 0, value, jnp.where(rows == 1, other, 0.0))


def swap_halves(u, low):
    return jnp.where(low, pltpu.roll(u, 224, 1), pltpu.roll(u, 32, 1))


def doubled(tile, low, which):
    other = pltpu.roll(tile, 64, 1)
    return jnp.where(low, tile, other) if which == 0 else jnp.where(low, other, tile)


def stacked(tile, low):
    zero = jnp.zeros_like(tile)
    return jnp.concatenate([jnp.where(low, tile, zero), jnp.where(low, zero, tile)], axis=0)


def attn_kernel(
    pos, tok_own, tok_oth, cos, sin, w_a, w_b, w_c, w_d,
    part, rows_at, aux_at, attn_in_at, q_at, k_at, v_at, ctx_at, lse_at,
    rows, aux, attn_in, q_out, k_out, v_out, ctx, lse_out, w, sems,
):
    half, core, late = pos[0], pos[1], pos[2]
    loads = copies(place_rows(w, (w_a, w_b, w_c, w_d), late, core), sems)
    start(loads)
    rows[pl.ds(mo(half * HALF, HALF), HALF), :] = tok_own[...]
    rows[pl.ds(mo((1 - half) * HALF, HALF), HALF), :] = tok_oth[...]
    x = rows[...].astype(f32)
    normed = x * lax.rsqrt(jnp.mean(x * x, axis=1, keepdims=True) + NORM_EPS)
    wait(loads)
    aux[...] = flat(w, 1536, PACK).astype(f32).T
    attn_in[...] = (normed * aux[32:33, :]).astype(bf16)
    low32 = iota((SEQ, 256), 1) % 64 < 32
    low = iota((SEQ, 128), 1) < 64
    for n in range(4):
        lin = dot(attn_in[...], flat(w, n * 256, (n + 1) * 256))
        if n < 3:
            lin = lin * cos[...] + swap_halves(lin, low32) * sin[...]
        if n < 2:
            q_out[:, n * 256 : (n + 1) * 256] = lin.astype(bf16)
        else:
            dst = k_out if n == 2 else v_out
            for m in range(4):
                tile = lin[:, (m // 2) * 128 : (m // 2) * 128 + 128]
                dst[:, m * 128 : (m + 1) * 128] = doubled(tile, low, m % 2).astype(bf16)
    pairs = [(rows, rows_at), (aux, aux_at), (attn_in, attn_in_at), (q_out, q_at), (k_out, k_at), (v_out, v_at)]
    stores = copies(pairs, sems, 4)
    start(stores)
    allowed = iota((2 * SEQ, SEQ), 0) % SEQ >= iota((2 * SEQ, SEQ), 1)
    for m in range(4):
        cols = slice(m * 128, (m + 1) * 128)
        scores = dot(stacked(q_out[:, cols], low), k_out[:, cols], NT) * SCALE
        scores = jnp.where(allowed, scores, -1e30)
        peak = jnp.max(scores, axis=1, keepdims=True)
        raised = jnp.exp(scores - peak)
        total = jnp.sum(raised, axis=1, keepdims=True)
        lse_out[m] = jnp.broadcast_to(peak + jnp.log(total), (2 * SEQ, 128))
        probs = (raised * (1.0 / total)).astype(bf16)
        both = dot(probs, v_out[:, cols])
        ctx[:, cols] = jnp.where(low, both[:SEQ], both[SEQ:]).astype(bf16)
    more = copies([(ctx, ctx_at), (lse_out, lse_at)], sems, 10)
    start(more)
    for n in range(4):
        outs = slice(n * 256, (n + 1) * 256)
        part[:, outs] = dot(ctx[...], w[n // 2, (n % 2) * 8 : (n % 2) * 8 + 8, :, :, 1024:1536].reshape(256, 512), NT).astype(bf16)
    wait(stores + more)


def mid_kernel(
    pos, rows, part_own, part_oth, aux, tab, mask,
    gates_out, middle_at, moe_in_at, sent_at, turned, middle, moe_in, sent, sems,
):
    half = pos[0]
    value = rows[...].astype(f32) + (part_own[...].astype(f32) + part_oth[...].astype(f32))
    middle[...] = value
    factor = lax.rsqrt(jnp.mean(value * value, axis=1, keepdims=True) + NORM_EPS)
    moe_in[...] = (value * factor * aux[33:34, :]).astype(bf16)
    moves = copies([(middle, middle_at), (moe_in, moe_in_at)], sems)
    start(moves)
    logits = dot(moe_in[...], aux[...].astype(bf16), NT)
    chosen = jnp.where(mask[...] > 0.0, logits, -1e30)
    raised = jnp.exp(chosen - jnp.max(chosen, axis=1, keepdims=True)) * mask[...]
    gates = raised / jnp.sum(raised, axis=1, keepdims=True)
    gates_out[...] = gates
    turned[...] = gates.T
    for n in range(4):
        spread_blocks(sent, n, dot(tab[...], moe_in[:, n * 256 : (n + 1) * 256]).astype(bf16), 16)
        at = slice(n * 160, (n + 1) * 160)
        (move,) = copies([(sent.at[:, at], sent_at.at[:, at])], sems, 2 + n)
        move.start()
        moves.append(move)
    lane = iota((CAP, 128), 1)
    slots = jnp.zeros((CAP, 128), f32)
    for i in range(16):
        row = turned[pl.ds(half * 16 + i, 1), :]
        found = jnp.sum(tab[i * CAP : (i + 1) * CAP, :].astype(f32) * row, axis=1, keepdims=True)
        slots = jnp.where(lane == i, found, slots)
    slots = jnp.concatenate([slots, jnp.zeros((128 - CAP, 128), f32)], axis=0).T
    at = iota((16, 128), 0)
    for i in range(16):
        line = slots[i : i + 1, :]
        high = line.astype(bf16).astype(f32)
        sent[i, ROWS : ROWS + 16, :] = pick(at, high, line - high).astype(bf16)
    at = slice(ROWS, ROWS + 16)
    (move,) = copies([(sent.at[:, at], sent_at.at[:, at])], sems, 6)
    move.start()
    wait(moves + [move])


def weights_kernel(pos, a0, a1, a2, a3, b0, b1, b2, b3, w_gate, w_up, w_down):
    core, late = pos[1], pos[2]
    for srcs, at_core in (((a0, a1, a2, a3), core), ((b0, b1, b2, b3), 1 - core)):
        for src, at_late, f in zip(srcs, (late, 1 - late, late, 1 - late), (0, 0, 1, 1)):
            for i in range(16):
                rows = pl.ds(mo((at_late * 16 + i) * 32 + at_core * 16, 16), 16)
                for j, dst in enumerate((w_gate, w_up, w_down)):
                    for h in range(2):
                        cols = slice(f * 256 + h * 128, f * 256 + h * 128 + 128)
                        dst[rows, cols] = src[i, (j * 2 + h) * 16 : (j * 2 + h + 1) * 16, :]


def expert_kernel(pos, x, c, w_gate, w_up, w_down, dx, gate_g, up_g, scaled, xs, cs):
    gather_blocks(xs, x, 4, 8)
    gather_blocks(cs, c, 4, 8)
    lines = x[:, ROWS : ROWS + 16, :].astype(f32).reshape(64, 128)
    lines = jnp.concatenate([lines, jnp.zeros((64, 128), f32)], axis=0).T[:CAP]
    gate = jnp.concatenate(
        [lines[:, 16 * i : 16 * i + 1] + lines[:, 16 * i + 1 : 16 * i + 2] for i in range(4)], axis=0
    )
    g = dot(xs[...], w_gate[...])
    u = dot(xs[...], w_up[...])
    sig = jax.nn.sigmoid(g)
    silu = g * sig
    hidden = (silu * u).astype(bf16).astype(f32)
    raw = dot(cs[...], w_down[...])
    gate_grad = jnp.sum(hidden * raw, axis=1, keepdims=True)
    back = gate * raw
    gate_g[...] = (back * u * sig * (1.0 + g * (1.0 - sig))).astype(bf16)
    up_g[...] = (back * silu).astype(bf16)
    scaled[...] = (gate * hidden).astype(bf16)
    for n in range(4):
        cols = slice(n * 256, (n + 1) * 256)
        value = dot(gate_g[...], w_gate[cols, :], NT) + dot(up_g[...], w_up[cols, :], NT)
        spread_blocks(dx, n, value.astype(bf16), 4)
    high = gate_grad.astype(bf16).astype(f32)
    lane = iota((CAP, 128), 1)
    slots = jnp.zeros((CAP, 128), f32)
    for i in range(4):
        rows = slice(i * CAP, (i + 1) * CAP)
        slots = slots + pick(lane - 16 * i, high[rows], gate_grad[rows] - high[rows])
    slots = jnp.concatenate([slots, jnp.zeros((128 - CAP, 128), f32)], axis=0).T
    for i in range(4):
        dx[i, ROWS : ROWS + 16, :] = slots[16 * i : 16 * (i + 1), :].astype(bf16)


def expert_grad_kernel(pos, x, c, gate_g, up_g, scaled, mine, sent, xs, cs, held):
    core = pos[1]
    gather_blocks(xs, x, 16, 2)
    gather_blocks(cs, c, 16, 2)
    for j, (lhs, rhs) in enumerate(((xs, gate_g), (xs, up_g), (cs, scaled))):
        held[...] = dot(lhs[...], rhs[...], TN).astype(bf16)
        for i in range(8):
            for dst, at_core in ((mine, core), (sent, 1 - core)):
                rows = pl.ds(mo(i * 32 + at_core * 16, 16), 16)
                for f in range(2):
                    for h in range(2):
                        cols = slice(f * 256 + h * 128, f * 256 + h * 128 + 128)
                        dst[0, f, i, (j * 2 + h) * 16 : (j * 2 + h + 1) * 16, :] = held[rows, cols]


def expert_out_kernel(pos, scaled, w_down, y):
    value = dot(scaled[...], w_down[...], NT).astype(bf16)
    for i in range(16):
        for j in range(2):
            y[i, j * CAP : (j + 1) * CAP, :] = value[i * CAP : (i + 1) * CAP, j * 128 : (j + 1) * 128]


def expert_sum_kernel(pos, mine, got, got_yl, got_yh, got_diag, out):
    out[:, :96, :] = (mine[0, 0].astype(f32) + got[0, 0].astype(f32) + got_yl[...].astype(f32)).astype(bf16)
    out[:, 96:, :] = (got_yh[...].astype(f32) + got_diag[...].astype(f32)).astype(bf16)


def expert_final_kernel(pos, got, *outs):
    half = pos[0]
    for part, at_half in enumerate((half, 1 - half)):
        for j in range(6):
            at = part * 96 + j * 16
            value = jnp.swapaxes(got[:, at : at + 16, :].astype(f32), 0, 1)
            cols = slice((j % 2) * 128, (j % 2) * 128 + 128)
            outs[j // 2][:, pl.ds(mo(at_half * 16, 16), 16), cols] = value


def combine_kernel(pos, tab_t, got, out, held):
    half = pos[0]
    gather_blocks(held, got, 16, 8)
    lines = got[:, ROWS : ROWS + 16, :].astype(f32).reshape(256, 128).T[:CAP]
    lane = iota((CAP, 128), 1)
    for i in range(16):
        e = half * 16 + i
        high, low = lines[:, 16 * i : 16 * i + 1], lines[:, 16 * i + 1 : 16 * i + 2]
        extra = jnp.where(lane == e, high, jnp.where(lane == e + EXPERTS, low, 0.0))
        held[i * CAP : (i + 1) * CAP, D:EXT] = extra.astype(bf16)
    for start in range(0, EXT, 256):
        cols = slice(start, min(start + 256, EXT))
        out[:, cols] = dot(tab_t[...], held[:, cols]).astype(bf16)


def finish_kernel(pos, tab_t, middle, got, own, sent, gathered, held):
    half = pos[0]
    gather_blocks(gathered, got, 16, 8)
    for n in range(4):
        cols = slice(n * 256, (n + 1) * 256)
        held[:, cols] = dot(tab_t[...], gathered[:, cols])
    mine = pl.ds(mo(half * HALF, HALF), HALF)
    own[...] = middle[mine, :] + held[mine, :]
    sent[...] = held[pl.ds(mo((1 - half) * HALF, HALF), HALF), :].astype(bf16)


def put(pack, first, value):
    width = value.shape[1]
    pack[:, :, :, :, first : first + width] = value.astype(bf16).reshape(2, 16, 2, 16, width)


def back_kernel(
    pos, comb_own, comb_oth, middle, moe_in, gates, aux, grad,
    w_a, w_b, w_c, w_d, ctx_at, q_at, k_at, v_at, lse_at, cos_at, sin_at, attn_in_at, rows_at,
    part_sent, gains, mg_own, part_own, mine, sent,
    w, ctx, q, k, v, lse, cos, sin, attn_in, rows, sems, mg, aog, pack, cgrad, dlin, apart,
):
    half, core, late = pos[0], pos[1], pos[2]
    pairs = place_rows(w, (w_a, w_b, w_c, w_d), late, core) + [
        (ctx_at, ctx), (q_at, q), (k_at, k), (v_at, v), (lse_at, lse), (cos_at, cos), (sin_at, sin),
        (attn_in_at, attn_in), (rows_at, rows),
    ]
    loads = copies(pairs, sems)
    start(loads)
    gg = comb_own[:, D:EXT].astype(f32) + comb_oth[:, D:EXT].astype(f32)
    gg = gg + pltpu.roll(gg, 96, 1)
    gate = gates[...]
    logit_grad = gate * (gg - jnp.sum(gate * gg, axis=1, keepdims=True))
    lg_high, lg_low = split(logit_grad)
    router_t = aux[...].astype(bf16)
    moe_grad = comb_own[:, :D].astype(f32) + comb_oth[:, :D].astype(f32)
    moe_grad = moe_grad + dot(lg_high, router_t) + dot(lg_low, router_t)
    value = middle[...]
    factor = lax.rsqrt(jnp.mean(value * value, axis=1, keepdims=True) + NORM_EPS)
    normed = value * factor
    gain_two = jnp.sum(moe_grad * normed, axis=0, keepdims=True)
    inner = moe_grad * aux[33:34, :]
    mg[...] = grad[...].astype(f32) + factor * (
        inner - normed * jnp.mean(inner * normed, axis=1, keepdims=True)
    )
    own = pl.ds(mo(half * HALF, HALF), HALF)
    stores = copies([(mg.at[own], mg_own)], sems, 13)
    start(stores)
    aog[...] = mg[...].astype(bf16)
    wait(loads[:5])
    for n in range(2):
        cols = slice(n * 256, (n + 1) * 256)
        cgrad[:, cols] = dot(aog[...], flat(w, 1024 + n * 256, 1280 + n * 256)).astype(bf16)
        put(pack, 1024 + n * 256, dot(aog[...], ctx[:, cols], TN))
    router_grad = dot(lg_high, moe_in[...], TN) + dot(lg_low, moe_in[...], TN)
    put(pack, 1536, jnp.where(iota((128, D), 0) == 33, gain_two, router_grad).T)
    low32 = iota((SEQ, 256), 1) % 64 < 32
    low = iota((SEQ, 128), 1) < 64
    allowed = iota((2 * SEQ, SEQ), 0) % SEQ >= iota((2 * SEQ, SEQ), 1)
    wait(loads[5:])
    for m in range(4):
        cols = slice(m * 128, (m + 1) * 128)
        qs = stacked(q[:, cols], low)
        cs = stacked(cgrad[:, cols], low)
        scores = dot(qs, k[:, cols], NT) * SCALE
        probs = jnp.where(allowed, jnp.exp(scores - lse[m][:, :1]), 0.0)
        back = dot(cs, v[:, cols], NT)
        spread = jnp.sum(probs * back, axis=1, keepdims=True)
        sg = (probs * (back - spread)).astype(bf16)
        dq = dot(sg, k[:, cols])
        dlin[:, cols] = jnp.where(low, dq[:SEQ], dq[SEQ:]) * SCALE
        dk = dot(sg, qs, TN) * SCALE
        dv = dot(probs.astype(bf16), cs, TN)
        dk = dk + pltpu.roll(dk, 64, 1)
        dv = dv + pltpu.roll(dv, 64, 1)
        for base, val in ((512, dk), (768, dv)):
            at = slice(base + (m // 2) * 128, base + (m // 2) * 128 + 128)
            if m % 2 == 0:
                dlin[:, at] = val
            else:
                dlin[:, at] = jnp.where(low, dlin[:, at], val)
    lows = []
    for n in range(4):
        cols = slice(n * 256, (n + 1) * 256)
        lin = dlin[:, cols]
        if n < 3:
            lin = lin * cos[...] - swap_halves(lin, low32) * sin[...]
        lin = lin.astype(bf16)
        lows.append(lin)
        put(pack, n * 256, dot(attn_in[...], lin, TN))
    pairs = [
        (pack.at[at_late, :, at_core], dst.at[i])
        for dst, at_core in ((sent, 1 - core), (mine, core))
        for i, at_late in enumerate((late, 1 - late))
    ]
    moves = copies(pairs, sems, 14)
    start(moves)
    stores = stores + moves
    lows = jnp.concatenate(lows, axis=1)
    for n in range(4):
        cols = slice(n * 256, (n + 1) * 256)
        block = w[n // 2, (n % 2) * 8 : (n % 2) * 8 + 8, :, :, :1024].reshape(256, 1024)
        apart[:, cols] = dot(lows, block, NT)
    moves = copies([(apart.at[own], part_own)], sems, 18)
    start(moves)
    part_sent[...] = apart[pl.ds(mo((1 - half) * HALF, HALF), HALF), :].astype(bf16)
    x = rows[...].astype(f32)
    normed_one = x * lax.rsqrt(jnp.mean(x * x, axis=1, keepdims=True) + NORM_EPS)
    gain_one = jnp.sum(apart[...] * normed_one, axis=0, keepdims=True)
    lines = jnp.concatenate([gain_one[:, n * 128 : (n + 1) * 128] for n in range(8)], axis=0)
    gains[...] = lines
    wait(stores + moves)


def gain_lines(gain):
    high = gain.astype(bf16).astype(f32)
    return jnp.concatenate([high, (gain - high).astype(bf16).astype(f32)], axis=0)


def halves(pairs, sems):
    loads = []
    for part in range(2):
        at = slice(part * 8, part * 8 + 8)
        loads.append(copies([(src.at[at], dst.at[at]) for src, dst in pairs], sems, part * len(pairs)))
        start(loads[-1])
    return loads


def move_kernel(pos, g_own, g_yh, g_core, g_twist, mine_at, got_at, out, gain_out, mine, got, sems):
    loads = halves([(mine_at.at[1], mine), (got_at.at[1], got)], sems)
    lines = gain_lines((g_own[...] + g_yh[...]) + (g_core[...] + g_twist[...]))
    gain_out[...] = lines
    for part in range(2):
        wait(loads[part])
        at = slice(part * 8, part * 8 + 8)
        out[at, :, :PACK] = (mine[at].astype(f32) + got[at].astype(f32)).astype(bf16)
    for i in range(16):
        out[i, :, PACK:] = lines.astype(bf16)


def sum_kernel(pos, gain, mine_at, got_at, got_yl_at, out, mine, got, got_yl, sems):
    loads = halves([(mine_at.at[0], mine), (got_at.at[0], got), (got_yl_at, got_yl)], sems)
    for part in range(2):
        wait(loads[part])
        at = slice(part * 8, part * 8 + 8)
        total = mine[at].astype(f32) + got[at].astype(f32) + got_yl[at, :, :PACK].astype(f32)
        out[at, :, :PACK] = total.astype(bf16)
    total = gain[...] + got_yl[0, :, PACK:].astype(f32)
    lines = gain_lines(total[:8] + total[8:]).astype(bf16)
    for i in range(16):
        out[i, :, PACK:] = lines


def rows_kernel(pos, tok, aux, mg, part_own, part_oth, out_own, out_oth, out, rows_out):
    x = tok[...].astype(f32)
    factor = lax.rsqrt(jnp.mean(x * x, axis=1, keepdims=True) + NORM_EPS)
    normed = x * factor
    inner = (part_own[...] + part_oth[...].astype(f32)) * aux[32:33, :]
    inner = factor * (inner - normed * jnp.mean(inner * normed, axis=1, keepdims=True))
    out[...] = (mg[...] + inner).astype(bf16)
    rows_out[...] = (out_own[...] + out_oth[...].astype(f32)).astype(bf16)


def final_kernel(pos, got, w_query, w_key, w_value, w_out, w_router, gain_two, gain_one):
    total = got[0].astype(f32)
    for i in range(1, 16):
        total = total + got[i].astype(f32)
    w_query[...] = total[:, :512]
    w_key[...] = total[:, 512:768]
    w_value[...] = total[:, 768:1024]
    w_out[...] = total[:, 1024:1536]
    w_router[...] = total[:, 1536 : 1536 + EXPERTS]
    turned = jnp.concatenate([total[:, 1536:PACK], jnp.zeros((112, 128), f32)], axis=0).T
    gain_two[...] = turned[33:34, :16]
    gains = total[:8, PACK:] + total[8:, PACK:]
    at = pos[4]
    row = jnp.sum(jnp.where(iota((8, 128), 0) == at // 8, gains, 0.0), axis=0, keepdims=True)
    lanes = pltpu.roll(jnp.broadcast_to(row, (8, 128)), (128 - (at % 8) * 16) % 128, 1)
    gain_one[...] = lanes[0:1, :16]


def rotary_tables():
    column = iota((SEQ, 256), 1)
    frequency = ROPE_BASE ** (-((column % (HDIM // 2)).astype(f32) * 2.0 / HDIM))
    angles = iota((SEQ, 256), 0).astype(f32) * frequency
    sin = jnp.sin(angles)
    return jnp.cos(angles), jnp.where(column % HDIM < HDIM // 2, -sin, sin)


def swap(value, axis):
    if axis == "twist":
        return lax.ppermute(value, ("c", "yh"), [(0, 3), (3, 0), (1, 2), (2, 1)])
    if axis == "diag":
        return lax.ppermute(value, ("yl", "yh"), [(0, 3), (3, 0), (1, 2), (2, 1)])
    return lax.ppermute(value, axis, [(0, 1), (1, 0)])


def ring(value, axis, step):
    return lax.ppermute(value, axis, [(i, (i + step) % 4) for i in range(4)])


def plane(value):
    return lax.all_to_all(value, PLANE, 0, 0, tiled=True)


def added(*values, gate=None):
    total = (values[0] if gate is None else after(values[0], gate)).astype(f32)
    for value in values[1:]:
        total = total + value.astype(f32)
    return total.astype(bf16)


def after(value, *others):
    return lax.optimization_barrier((value, *others))[0]


def at_index(value, i):
    return lax.dynamic_index_in_dim(value, i, 0, keepdims=False)


def body(
    tokens,
    routes,
    cotangent,
    attn_gain,
    query_weight,
    key_weight,
    value_weight,
    out_weight,
    moe_gain,
    router_weight,
    expert_gate,
    expert_up,
    expert_down,
):
    half, core, late = lax.axis_index("yh"), lax.axis_index("c"), lax.axis_index("yl")
    place = lax.axis_index("x") * 4 + lax.axis_index("z")
    pos = jnp.stack([half, core, late, half * 16 + place, (late * 16 + place) * 2 + core, lax.axis_index("x"), lax.axis_index("z")]).astype(jnp.int32)
    cos, sin = rotary_tables()

    (packed,) = call(
        pack_kernel,
        [((16, 16, PACK), bf16)],
        [
            pos, query_weight, key_weight, value_weight, out_weight, router_weight,
            attn_gain.reshape(1, 16), moe_gain.reshape(1, 16),
        ],
        us=0,
    )
    w_a = plane(packed)
    tok_oth = swap(tokens, "yh")
    cot_oth = swap(cotangent, "yh")

    experts = jnp.stack([expert_gate, expert_up, expert_down])
    experts = experts.reshape(3, 16, 2, 16, 2, 128).transpose(3, 2, 0, 4, 1, 5).reshape(16, 192, 128)
    tab, tab_t, mask = call(
        route_kernel,
        [((SLOTS, SEQ), bf16), ((SEQ, SLOTS), bf16), ((SEQ, 128), f32)],
        [pos, routes],
        scratch=[pltpu.VMEM((128, SEQ), f32)],
        us=0,
    )
    grad, cot_sent = call(
        dispatch_kernel,
        [((SEQ, D), bf16), ((16, ROWS + 192, 128), bf16)],
        [pos, tab, cotangent, cot_oth, experts],
        us=3,
    )
    w_a = after(w_a, experts, cot_sent, tok_oth)
    w_b = swap(w_a, "yl")
    w_c = swap(w_a, "c")
    w_d = swap(w_b, "c")
    cot_slots = plane(after(cot_sent, w_c))

    e_own = lax.dynamic_slice_in_dim(cot_slots, ROWS + 96 * half, 96, 1)
    e_oth = lax.dynamic_slice_in_dim(cot_slots, ROWS + 96 * (1 - half), 96, 1)
    pieces = [e_own, swap(e_own, "yl"), swap(e_oth, "yh"), swap(e_oth, "diag")]
    pieces = pieces + [swap(piece, "c") for piece in pieces]
    w_gate, w_up, w_down = call(weights_kernel, [((D, 512), bf16)] * 3, [pos] + pieces, us=4)

    kept = [
        ((SEQ, D), bf16), ((128, D), f32), ((SEQ, D), bf16), ((SEQ, 512), bf16), ((SEQ, 512), bf16),
        ((SEQ, 512), bf16), ((SEQ, 512), bf16), ((4, 512, 128), f32),
    ]
    part, rows, aux, attn_in, q, k, v, ctx, lse = call(
        attn_kernel,
        [((SEQ, D), bf16)] + kept,
        [pos, tokens, tok_oth, cos, sin, w_a, w_b, w_c, w_d],
        late_from=5,
        late_outs=8,
        scratch=[pltpu.VMEM(shape, kind) for shape, kind in kept]
        + [pltpu.VMEM((2, 16, 2, 16, PACK), bf16), pltpu.SemaphoreType.DMA((12,))],
        us=7,
    )
    part_oth = swap(part, "yh")
    kept = [((SEQ, D), f32), ((SEQ, D), bf16), ((16, ROWS + 16, 128), bf16)]
    gates, middle, moe_in, x_sent = call(
        mid_kernel,
        [((SEQ, 128), f32)] + kept,
        [pos, rows, part, part_oth, aux, tab, mask],
        late_outs=3,
        scratch=[pltpu.VMEM((128, SEQ), f32)]
        + [pltpu.VMEM(shape, kind) for shape, kind in kept]
        + [pltpu.SemaphoreType.DMA((7,))],
        us=3,
    )
    x_slots = plane(x_sent)

    whole = pl.BlockSpec((D, 512), lambda i, *pos: (0, 0))
    by_row = pl.BlockSpec((4 * CAP, 512), lambda i, *pos: (i, 0))
    by_peer = lambda rows: pl.BlockSpec((4, rows, 128), lambda i, *pos: (i, 0, 0))
    dx, gate_g, up_g, scaled = call(
        expert_kernel,
        [((16, ROWS + 16, 128), bf16), ((SLOTS, 512), bf16), ((SLOTS, 512), bf16), ((SLOTS, 512), bf16)],
        [pos, x_slots, cot_slots, w_gate, w_up, w_down],
        scratch=[pltpu.VMEM((4 * CAP, D), bf16), pltpu.VMEM((4 * CAP, D), bf16)],
        grid=(4,),
        in_specs=[by_peer(ROWS + 16), by_peer(ROWS), whole, whole, whole],
        out_specs=[by_peer(ROWS + 16), by_row, by_row, by_row],
        us=12,
    )
    dx_back = plane(dx)

    full = pl.BlockSpec((SLOTS, 512), lambda i, *pos: (0, 0))
    by_col = pl.BlockSpec((16, 2 * CAP, 128), lambda i, *pos: (0, i, 0))
    by_owner = pl.BlockSpec((1, 2, 8, 96, 128), lambda i, pos: ((i // 2 + pos[2]) % 2, 0, i % 2, 0, 0))
    e_mine, e_sent = call(
        expert_grad_kernel,
        [((2, 2, 16, 96, 128), bf16), ((2, 2, 16, 96, 128), bf16)],
        [pos, x_slots, cot_slots, gate_g, up_g, scaled],
        scratch=[
            pltpu.VMEM((SLOTS, 256), bf16), pltpu.VMEM((SLOTS, 256), bf16), pltpu.VMEM((256, 512), bf16),
        ],
        grid=(4,),
        in_specs=[by_col, by_col, full, full, full],
        out_specs=[by_owner, by_owner],
        us=0,
        prefetch=True,
    )


    e_got = swap(e_sent, "c")
    e_yl, e_yh, e_diag = (
        swap(added(e_mine[i, j], e_got[i, j]), axis) for i, j, axis in ((1, 0, "yl"), (0, 1, "yh"), (1, 1, "diag"))
    )
    (y,) = call(
        expert_out_kernel,
        [((16, ROWS, 128), bf16)],
        [pos, after(scaled, e_got), w_down],
        grid=(4,),
        in_specs=[full, pl.BlockSpec((256, 512), lambda i, *pos: (i, 0))],
        out_specs=[by_col],
        us=0,
    )
    dx_back = after(dx_back, e_yl, y)
    (comb,) = call(
        combine_kernel, [((SEQ, EXT), bf16)], [pos, tab_t, dx_back],
        scratch=[pltpu.VMEM((SLOTS, EXT), bf16)], us=0,
    )
    comb = after(comb, e_yh, e_diag)
    comb_oth = swap(comb, "yh")
    y_back = plane(y)
    by_first = pl.BlockSpec((1, 1, 16, 96, 128), lambda i, *pos: (0, 0, 0, 0, 0))
    by_third = pl.BlockSpec((16, 96, 128), lambda i, *pos: (0, 0, 0))
    (e_cat,) = call(
        expert_sum_kernel,
        [((16, 192, 128), bf16)],
        [pos, after(e_mine, comb), e_got, e_yl, e_yh, e_diag],
        grid=(1,),
        in_specs=[by_first, by_first, by_third, by_third, by_third],
        out_specs=[pl.BlockSpec((16, 192, 128), lambda i, *pos: (0, 0, 0))],
        us=0,
    )
    comb_oth = after(comb_oth, e_cat)
    part_sent, gains, mg_own, part_own, a_mine, a_sent = call(
        back_kernel,
        [
            ((HALF, D), bf16), ((8, 128), f32), ((HALF, D), f32), ((HALF, D), f32),
            ((2, 16, 16, PACK), bf16), ((2, 16, 16, PACK), bf16),
        ],
        [
            pos, comb, comb_oth, middle, moe_in, gates, aux, grad,
            w_a, w_b, w_c, w_d, ctx, q, k, v, lse, cos, sin, attn_in, rows,
        ],
        late_from=8,
        late_outs=4,
        scratch=[
            pltpu.VMEM((2, 16, 2, 16, PACK), bf16), pltpu.VMEM((SEQ, 512), bf16), pltpu.VMEM((SEQ, 512), bf16),
            pltpu.VMEM((SEQ, 512), bf16), pltpu.VMEM((SEQ, 512), bf16), pltpu.VMEM((4, 512, 128), f32),
            pltpu.VMEM((SEQ, 256), f32), pltpu.VMEM((SEQ, 256), f32), pltpu.VMEM((SEQ, D), bf16),
            pltpu.VMEM((SEQ, D), bf16), pltpu.SemaphoreType.DMA((19,)),
            pltpu.VMEM((SEQ, D), f32), pltpu.VMEM((SEQ, D), bf16), pltpu.VMEM((2, 16, 2, 16, PACK), bf16),
            pltpu.VMEM((SEQ, 512), bf16), pltpu.VMEM((SEQ, D), f32), pltpu.VMEM((SEQ, D), f32),
        ],
        us=0,
    )

    a_got = swap(a_sent, "c")
    block = pltpu.VMEM((16, 16, PACK), bf16)
    wide = pltpu.VMEM((16, 16, PACK + 128), bf16)
    a_move, gains = call(
        move_kernel,
        [((16, 16, PACK + 128), bf16), ((16, 128), f32)],
        [pos, gains] + [swap(gains, axis) for axis in ("yh", "c", "twist")] + [a_mine, a_got],
        late_from=5,
        scratch=[block, block, pltpu.SemaphoreType.DMA((4,))],
        us=0,
    )
    a_yl = swap(a_move, "yl")
    e_back = plane(after(e_cat, y_back))
    out_own, out_sent = call(
        finish_kernel,
        [((HALF, D), f32), ((HALF, D), bf16)],
        [pos, tab_t, middle, after(y_back, a_move)],
        scratch=[pltpu.VMEM((SLOTS, D), bf16), pltpu.VMEM((SEQ, D), f32)],
        us=0,
    )
    a_yl = after(a_yl, out_sent)
    (a_sum,) = call(
        sum_kernel,
        [((16, 16, PACK + 128), bf16)],
        [pos, gains, a_mine, a_got, a_yl],
        late_from=2,
        scratch=[block, block, wide, pltpu.SemaphoreType.DMA((6,))],
        us=0,
    )
    total = plane(after(a_sum, e_back))
    part_oth = swap(after(part_sent, a_move, y_back), "yh")
    grad_gate, grad_up, grad_down = call(
        expert_final_kernel, [((16, EXPERTS, 256), f32)] * 3, [pos, after(e_back, a_sum)], us=0
    )

    out_oth = swap(after(out_sent, a_sum), "yh")
    part_oth = after(part_oth, grad_gate)
    input_grad, output = call(
        rows_kernel,
        [((HALF, D), bf16), ((HALF, D), bf16)],
        [pos, tokens, aux, mg_own, part_own, part_oth, out_own, out_oth],
        us=0,
    )
    w_query, w_key, w_value, w_out, w_router, gain_two, gain_one = call(
        final_kernel,
        [((16, n), f32) for n in (512, 256, 256, 512, 32)] + [((1, 16), f32)] * 2,
        [pos, total],
        us=0,
    )

    return (
        output,
        input_grad,
        gain_one.reshape(16),
        w_query,
        w_key,
        w_value,
        w_out,
        gain_two.reshape(16),
        w_router,
        grad_gate,
        grad_up,
        grad_down,
    )


def solution(mesh):
    fine = Mesh(mesh.devices.reshape(2, 4, 4, 2, 2), ("yl", "x", "z", "c", "yh"))
    dp, every = ("yl", "x", "z", "c"), ("yl", "x", "z", "c", "yh")
    in_specs = (
        P(every, None),
        P(dp, None),
        P(every, None),
        P(dp),
        P(dp, "yh"),
        P(dp, "yh"),
        P(dp, "yh"),
        P(dp, "yh"),
        P(dp),
        P(dp, None),
        P(dp, None, "yh"),
        P(dp, None, "yh"),
        P(dp, None, "yh"),
    )
    out_specs = (
        P(every, None),
        P(every, None),
        P(dp),
        P(dp, "yh"),
        P(dp, "yh"),
        P(dp, "yh"),
        P(dp, "yh"),
        P(dp),
        P(dp, None),
        P(dp, None, "yh"),
        P(dp, None, "yh"),
        P(dp, None, "yh"),
    )
    return jax.shard_map(body, mesh=fine, in_specs=in_specs, out_specs=out_specs, check_vma=False)
```

```python
import math

import jax
import jax.numpy as jnp
from jax import lax
from jax.experimental import pallas as pl
from jax.experimental.pallas import tpu as pltpu
from jax.sharding import Mesh, PartitionSpec as P

bf16 = jnp.bfloat16
f32 = jnp.float32

D = 1024
HDIM = 64
SEQ = 256
HALF = 128
EXPERTS = 32
CAP = 80
SLOTS = 16 * CAP
EXT = D + 128
ROWS = 8 * CAP
PACK = 1664
NORM_EPS = 1e-06
ROPE_BASE = 10000.0
SCALE = 0.125
PLANE = ("x", "z")
NT = (((1,), (1,)), ((), ()))
TN = (((0,), (0,)), ((), ()))
VMEM_BYTES = 65472 * 1024
PART_BYTES = 40 * 1024 * 1024


def mo(value, by):
    return pl.multiple_of(value, by)


def dot(a, b, dims=(((1,), (0,)), ((), ()))):
    return lax.dot_general(a, b, dims, preferred_element_type=f32)


def split(value):
    high = value.astype(bf16)
    return high, (value - high.astype(f32)).astype(bf16)


def iota(shape, dim):
    return lax.broadcasted_iota(jnp.int32, shape, dim)


def call(kernel, outs, args, scratch=(), grid=None, in_specs=None, out_specs=None, us=1, late_from=None, late_outs=0, prefetch=False, vmem=VMEM_BYTES, hbm=False):
    smem = pl.BlockSpec(memory_space=pltpu.SMEM)
    params = pltpu.CompilerParams(vmem_limit_bytes=vmem)
    out_shape = [(pltpu.HBM if hbm else jax.ShapeDtypeStruct)(shape, kind) for shape, kind in outs]
    nbytes = sum(a.size * a.dtype.itemsize for a in args) + sum(
        math.prod(shape) * jnp.dtype(kind).itemsize for shape, kind in outs
    )
    cost = pl.CostEstimate(flops=int(us * 1.15e9) + 1000, bytes_accessed=nbytes if us else 1000, transcendentals=0)
    if grid is None:
        vmem = pl.BlockSpec(memory_space=pltpu.VMEM)
        early = len(args) if late_from is None else late_from
        in_specs = [smem] + [vmem] * (early - 1) + [pl.BlockSpec(memory_space=pl.ANY)] * (len(args) - early)
        out_specs = [vmem] * (len(outs) - late_outs) + [pl.BlockSpec(memory_space=pl.ANY)] * late_outs
        return pl.pallas_call(
            kernel,
            out_shape=out_shape,
            in_specs=in_specs,
            out_specs=out_specs,
            scratch_shapes=scratch,
            compiler_params=params,
            cost_estimate=cost,
        )(*args)
    if not prefetch:
        return pl.pallas_call(
            kernel,
            grid=grid,
            out_shape=out_shape,
            in_specs=[smem] + in_specs,
            out_specs=out_specs,
            scratch_shapes=scratch,
            compiler_params=params,
            cost_estimate=cost,
        )(*args)
    return pl.pallas_call(
        kernel,
        grid_spec=pltpu.PrefetchScalarGridSpec(
            num_scalar_prefetch=1, grid=grid, in_specs=in_specs, out_specs=out_specs, scratch_shapes=scratch
        ),
        out_shape=out_shape,
        compiler_params=params,
        cost_estimate=cost,
    )(*args)


def copies(pairs, sems, first=0):
    return [pltpu.make_async_copy(src, dst, sems.at[first + i]) for i, (src, dst) in enumerate(pairs)]


def start(loads):
    for load in loads:
        load.start()


def wait(loads):
    for load in loads:
        load.wait()


def place_rows(w, pieces, late, core):
    at = ((late, core), (1 - late, core), (late, 1 - core), (1 - late, 1 - core))
    return [(src, w.at[at_late, :, at_core]) for src, (at_late, at_core) in zip(pieces, at)]


def flat(w, first, last):
    return w[:, :, :, :, first:last].reshape(D, last - first)


def pack_kernel(pos, w_query, w_key, w_value, w_out, router, gain_one, gain_two, out):
    at = iota((128, 128), 0)
    rest = jnp.zeros((1, 112), f32)
    first, second = (jnp.concatenate([gain[...].astype(f32), rest], axis=1) for gain in (gain_one, gain_two))
    gains = pick(at, first, second)
    gains = gains.T[:16]
    wide = jnp.concatenate([router[...].astype(f32), jnp.zeros((16, 96), f32)], axis=1)
    small = (wide + pltpu.roll(gains, EXPERTS, 1)).astype(bf16)
    for i in range(16):
        out[i, :, :512] = w_query[...]
        out[i, :, 512:768] = w_key[...]
        out[i, :, 768:1024] = w_value[...]
        out[i, :, 1024:1536] = w_out[...]
        out[i, :, 1536:] = small


def route_kernel(pos, routes, tab, tab_t, mask_out, turned):
    half = pos[0]
    named = routes[...]
    lane = iota((SEQ, 128), 1)
    mask = jnp.zeros((SEQ, 128), f32)
    for k in range(named.shape[1]):
        mask = mask + jnp.where(named[:, k : k + 1] == lane, 1.0, 0.0)
    mask_out[...] = mask
    below = jnp.where(iota((SEQ, SEQ), 0) > iota((SEQ, SEQ), 1), 1.0, 0.0).astype(bf16)
    place = dot(below, mask.astype(bf16))
    turned[...] = jnp.where(mask > 0.0, place, -1.0).T
    slot = iota((CAP, SEQ), 0).astype(f32)
    for i in range(16):
        row = turned[pl.ds(half * 16 + i, 1), :]
        tab[i * CAP : (i + 1) * CAP, :] = jnp.where(slot == row, 1.0, 0.0).astype(bf16)
    for n in range(SLOTS // 128):
        cols = slice(n * 128, (n + 1) * 128)
        tab_t[:, cols] = tab[cols, :].astype(f32).T.astype(bf16)


def dispatch_kernel(pos, tab, cot_own, cot_oth, packed, grad, sent):
    half = pos[0]
    sent[:, ROWS : ROWS + 192, :] = packed[...]
    grad[pl.ds(mo(half * HALF, HALF), HALF), :] = cot_own[...]
    grad[pl.ds(mo((1 - half) * HALF, HALF), HALF), :] = cot_oth[...]
    for n in range(4):
        spread_blocks(sent, n, dot(tab[...], grad[:, n * 256 : (n + 1) * 256]).astype(bf16), 16)


def spread_blocks(dst, n, value, peers):
    for i in range(peers):
        for j in range(2):
            at = (2 * n + j) * CAP
            dst[i, at : at + CAP, :] = value[i * CAP : (i + 1) * CAP, j * 128 : (j + 1) * 128]


def gather_blocks(dst, src, peers, blocks):
    for i in range(peers):
        for j in range(blocks):
            dst[i * CAP : (i + 1) * CAP, j * 128 : (j + 1) * 128] = src[i, j * CAP : (j + 1) * CAP, :]


def pick(rows, value, other):
    return jnp.where(rows == 0, value, jnp.where(rows == 1, other, 0.0))


def swap_halves(u, low):
    return jnp.where(low, pltpu.roll(u, 224, 1), pltpu.roll(u, 32, 1))


def doubled(tile, low, which):
    other = pltpu.roll(tile, 64, 1)
    return jnp.where(low, tile, other) if which == 0 else jnp.where(low, other, tile)


def stacked(tile, low):
    zero = jnp.zeros_like(tile)
    return jnp.concatenate([jnp.where(low, tile, zero), jnp.where(low, zero, tile)], axis=0)


def attn_kernel(
    pos, tok_own, tok_oth, cos, sin, w_a, w_b, w_c, w_d,
    part, rows_at, aux_at, attn_in_at, q_at, k_at, v_at, ctx_at, lse_at,
    rows, aux, attn_in, q_out, k_out, v_out, ctx, lse_out, w, sems,
):
    half, core, late = pos[0], pos[1], pos[2]
    loads = copies(place_rows(w, (w_a, w_b, w_c, w_d), late, core), sems)
    start(loads)
    rows[pl.ds(mo(half * HALF, HALF), HALF), :] = tok_own[...]
    rows[pl.ds(mo((1 - half) * HALF, HALF), HALF), :] = tok_oth[...]
    x = rows[...].astype(f32)
    normed = x * lax.rsqrt(jnp.mean(x * x, axis=1, keepdims=True) + NORM_EPS)
    wait(loads)
    aux[...] = flat(w, 1536, PACK).astype(f32).T
    attn_in[...] = (normed * aux[32:33, :]).astype(bf16)
    low32 = iota((SEQ, 256), 1) % 64 < 32
    low = iota((SEQ, 128), 1) < 64
    for n in range(4):
        lin = dot(attn_in[...], flat(w, n * 256, (n + 1) * 256))
        if n < 3:
            lin = lin * cos[...] + swap_halves(lin, low32) * sin[...]
        if n < 2:
            q_out[:, n * 256 : (n + 1) * 256] = lin.astype(bf16)
        else:
            dst = k_out if n == 2 else v_out
            for m in range(4):
                tile = lin[:, (m // 2) * 128 : (m // 2) * 128 + 128]
                dst[:, m * 128 : (m + 1) * 128] = doubled(tile, low, m % 2).astype(bf16)
    pairs = [(rows, rows_at), (aux, aux_at), (attn_in, attn_in_at), (q_out, q_at), (k_out, k_at), (v_out, v_at)]
    stores = copies(pairs, sems, 4)
    start(stores)
    allowed = iota((2 * SEQ, SEQ), 0) % SEQ >= iota((2 * SEQ, SEQ), 1)
    for m in range(4):
        cols = slice(m * 128, (m + 1) * 128)
        scores = dot(stacked(q_out[:, cols], low), k_out[:, cols], NT) * SCALE
        scores = jnp.where(allowed, scores, -1e30)
        peak = jnp.max(scores, axis=1, keepdims=True)
        raised = jnp.exp(scores - peak)
        total = jnp.sum(raised, axis=1, keepdims=True)
        lse_out[m] = jnp.broadcast_to(peak + jnp.log(total), (2 * SEQ, 128))
        probs = (raised * (1.0 / total)).astype(bf16)
        both = dot(probs, v_out[:, cols])
        ctx[:, cols] = jnp.where(low, both[:SEQ], both[SEQ:]).astype(bf16)
    more = copies([(ctx, ctx_at), (lse_out, lse_at)], sems, 10)
    start(more)
    for n in range(4):
        outs = slice(n * 256, (n + 1) * 256)
        part[:, outs] = dot(ctx[...], w[n // 2, (n % 2) * 8 : (n % 2) * 8 + 8, :, :, 1024:1536].reshape(256, 512), NT).astype(bf16)
    wait(stores + more)


def mid_kernel(
    pos, rows, part_own, part_oth, aux, tab, mask,
    gates_out, middle_at, moe_in_at, sent_at, turned, middle, moe_in, sent, sems,
):
    half = pos[0]
    value = rows[...].astype(f32) + (part_own[...].astype(f32) + part_oth[...].astype(f32))
    middle[...] = value
    factor = lax.rsqrt(jnp.mean(value * value, axis=1, keepdims=True) + NORM_EPS)
    moe_in[...] = (value * factor * aux[33:34, :]).astype(bf16)
    moves = copies([(middle, middle_at), (moe_in, moe_in_at)], sems)
    start(moves)
    logits = dot(moe_in[...], aux[...].astype(bf16), NT)
    chosen = jnp.where(mask[...] > 0.0, logits, -1e30)
    raised = jnp.exp(chosen - jnp.max(chosen, axis=1, keepdims=True)) * mask[...]
    gates = raised / jnp.sum(raised, axis=1, keepdims=True)
    gates_out[...] = gates
    turned[...] = gates.T
    for n in range(4):
        spread_blocks(sent, n, dot(tab[...], moe_in[:, n * 256 : (n + 1) * 256]).astype(bf16), 16)
        at = slice(n * 160, (n + 1) * 160)
        (move,) = copies([(sent.at[:, at], sent_at.at[:, at])], sems, 2 + n)
        move.start()
        moves.append(move)
    lane = iota((CAP, 128), 1)
    slots = jnp.zeros((CAP, 128), f32)
    for i in range(16):
        row = turned[pl.ds(half * 16 + i, 1), :]
        found = jnp.sum(tab[i * CAP : (i + 1) * CAP, :].astype(f32) * row, axis=1, keepdims=True)
        slots = jnp.where(lane == i, found, slots)
    slots = jnp.concatenate([slots, jnp.zeros((128 - CAP, 128), f32)], axis=0).T
    at = iota((16, 128), 0)
    for i in range(16):
        line = slots[i : i + 1, :]
        high = line.astype(bf16).astype(f32)
        sent[i, ROWS : ROWS + 16, :] = pick(at, high, line - high).astype(bf16)
    at = slice(ROWS, ROWS + 16)
    (move,) = copies([(sent.at[:, at], sent_at.at[:, at])], sems, 6)
    move.start()
    wait(moves + [move])


def weights_kernel(pos, a0, a1, a2, a3, b0, b1, b2, b3, w_gate, w_up, w_down):
    core, late = pos[1], pos[2]
    for srcs, at_core in (((a0, a1, a2, a3), core), ((b0, b1, b2, b3), 1 - core)):
        for src, at_late, f in zip(srcs, (late, 1 - late, late, 1 - late), (0, 0, 1, 1)):
            for i in range(16):
                rows = pl.ds(mo((at_late * 16 + i) * 32 + at_core * 16, 16), 16)
                for j, dst in enumerate((w_gate, w_up, w_down)):
                    for h in range(2):
                        cols = slice(f * 256 + h * 128, f * 256 + h * 128 + 128)
                        dst[rows, cols] = src[i, (j * 2 + h) * 16 : (j * 2 + h + 1) * 16, :]


def expert_kernel(pos, x, c, w_gate, w_up, w_down, dx, gate_g, up_g, scaled, xs, cs):
    gather_blocks(xs, x, 4, 8)
    gather_blocks(cs, c, 4, 8)
    lines = x[:, ROWS : ROWS + 16, :].astype(f32).reshape(64, 128)
    lines = jnp.concatenate([lines, jnp.zeros((64, 128), f32)], axis=0).T[:CAP]
    gate = jnp.concatenate(
        [lines[:, 16 * i : 16 * i + 1] + lines[:, 16 * i + 1 : 16 * i + 2] for i in range(4)], axis=0
    )
    g = dot(xs[...], w_gate[...])
    u = dot(xs[...], w_up[...])
    sig = jax.nn.sigmoid(g)
    silu = g * sig
    hidden = (silu * u).astype(bf16).astype(f32)
    raw = dot(cs[...], w_down[...])
    gate_grad = jnp.sum(hidden * raw, axis=1, keepdims=True)
    back = gate * raw
    gate_g[...] = (back * u * sig * (1.0 + g * (1.0 - sig))).astype(bf16)
    up_g[...] = (back * silu).astype(bf16)
    scaled[...] = (gate * hidden).astype(bf16)
    for n in range(4):
        cols = slice(n * 256, (n + 1) * 256)
        value = dot(gate_g[...], w_gate[cols, :], NT) + dot(up_g[...], w_up[cols, :], NT)
        spread_blocks(dx, n, value.astype(bf16), 4)
    high = gate_grad.astype(bf16).astype(f32)
    lane = iota((CAP, 128), 1)
    slots = jnp.zeros((CAP, 128), f32)
    for i in range(4):
        rows = slice(i * CAP, (i + 1) * CAP)
        slots = slots + pick(lane - 16 * i, high[rows], gate_grad[rows] - high[rows])
    slots = jnp.concatenate([slots, jnp.zeros((128 - CAP, 128), f32)], axis=0).T
    for i in range(4):
        dx[i, ROWS : ROWS + 16, :] = slots[16 * i : 16 * (i + 1), :].astype(bf16)


def expert_grad_kernel(pos, x, c, gate_g, up_g, scaled, mine, sent, xs, cs, held):
    core = pos[1]
    gather_blocks(xs, x, 16, 2)
    gather_blocks(cs, c, 16, 2)
    for j, (lhs, rhs) in enumerate(((xs, gate_g), (xs, up_g), (cs, scaled))):
        held[...] = dot(lhs[...], rhs[...], TN).astype(bf16)
        for i in range(8):
            for dst, at_core in ((mine, core), (sent, 1 - core)):
                rows = pl.ds(mo(i * 32 + at_core * 16, 16), 16)
                for f in range(2):
                    for h in range(2):
                        cols = slice(f * 256 + h * 128, f * 256 + h * 128 + 128)
                        dst[0, f, i, (j * 2 + h) * 16 : (j * 2 + h + 1) * 16, :] = held[rows, cols]


def expert_out_kernel(pos, scaled, w_down, y):
    value = dot(scaled[...], w_down[...], NT).astype(bf16)
    for i in range(16):
        for j in range(2):
            y[i, j * CAP : (j + 1) * CAP, :] = value[i * CAP : (i + 1) * CAP, j * 128 : (j + 1) * 128]


def expert_sum_kernel(pos, mine, got, got_yl, got_yh, got_diag, out):
    out[:, :96, :] = (mine[0, 0].astype(f32) + got[0, 0].astype(f32) + got_yl[...].astype(f32)).astype(bf16)
    out[:, 96:, :] = (got_yh[...].astype(f32) + got_diag[...].astype(f32)).astype(bf16)


def expert_final_kernel(pos, got, *outs):
    half = pos[0]
    for part, at_half in enumerate((half, 1 - half)):
        for j in range(6):
            at = part * 96 + j * 16
            value = jnp.swapaxes(got[:, at : at + 16, :].astype(f32), 0, 1)
            cols = slice((j % 2) * 128, (j % 2) * 128 + 128)
            outs[j // 2][:, pl.ds(mo(at_half * 16, 16), 16), cols] = value


def combine_kernel(pos, tab_t, got, out, held):
    half = pos[0]
    gather_blocks(held, got, 16, 8)
    lines = got[:, ROWS : ROWS + 16, :].astype(f32).reshape(256, 128).T[:CAP]
    lane = iota((CAP, 128), 1)
    for i in range(16):
        e = half * 16 + i
        high, low = lines[:, 16 * i : 16 * i + 1], lines[:, 16 * i + 1 : 16 * i + 2]
        extra = jnp.where(lane == e, high, jnp.where(lane == e + EXPERTS, low, 0.0))
        held[i * CAP : (i + 1) * CAP, D:EXT] = extra.astype(bf16)
    for start in range(0, EXT, 256):
        cols = slice(start, min(start + 256, EXT))
        out[:, cols] = dot(tab_t[...], held[:, cols]).astype(bf16)


def finish_kernel(pos, tab_t, middle, got, part_sent, own, sent, gathered, held):
    half = pos[0]
    gather_blocks(gathered, got, 16, 8)
    for n in range(4):
        cols = slice(n * 256, (n + 1) * 256)
        held[:, cols] = dot(tab_t[...], gathered[:, cols])
    mine = pl.ds(mo(half * HALF, HALF), HALF)
    own[...] = middle[mine, :] + held[mine, :]
    sent[0] = held[pl.ds(mo((1 - half) * HALF, HALF), HALF), :].astype(bf16)
    sent[1] = part_sent[...]


def put(pack, first, value):
    width = value.shape[1]
    pack[:, :, :, :, first : first + width] = value.astype(bf16).reshape(2, 16, 2, 16, width)


def back_kernel(
    pos, comb_own, comb_oth, middle, moe_in, gates, aux, grad,
    w_a, w_b, w_c, w_d, ctx_at, q_at, k_at, v_at, lse_at, cos_at, sin_at, attn_in_at, rows_at,
    part_sent, gains, mg_own, part_own, mine, sent,
    w, ctx, q, k, v, lse, cos, sin, attn_in, rows, sems, mg, aog, pack, cgrad, dlin, apart,
):
    half, core, late = pos[0], pos[1], pos[2]
    pairs = place_rows(w, (w_a, w_b, w_c, w_d), late, core) + [
        (ctx_at, ctx), (q_at, q), (k_at, k), (v_at, v), (lse_at, lse), (cos_at, cos), (sin_at, sin),
        (attn_in_at, attn_in), (rows_at, rows),
    ]
    loads = copies(pairs, sems)
    start(loads)
    gg = comb_own[:, D:EXT].astype(f32) + comb_oth[:, D:EXT].astype(f32)
    gg = gg + pltpu.roll(gg, 96, 1)
    gate = gates[...]
    logit_grad = gate * (gg - jnp.sum(gate * gg, axis=1, keepdims=True))
    lg_high, lg_low = split(logit_grad)
    router_t = aux[...].astype(bf16)
    moe_grad = comb_own[:, :D].astype(f32) + comb_oth[:, :D].astype(f32)
    moe_grad = moe_grad + dot(lg_high, router_t) + dot(lg_low, router_t)
    value = middle[...]
    factor = lax.rsqrt(jnp.mean(value * value, axis=1, keepdims=True) + NORM_EPS)
    normed = value * factor
    gain_two = jnp.sum(moe_grad * normed, axis=0, keepdims=True)
    inner = moe_grad * aux[33:34, :]
    mg[...] = grad[...].astype(f32) + factor * (
        inner - normed * jnp.mean(inner * normed, axis=1, keepdims=True)
    )
    own = pl.ds(mo(half * HALF, HALF), HALF)
    stores = copies([(mg.at[own], mg_own)], sems, 13)
    start(stores)
    aog[...] = mg[...].astype(bf16)
    wait(loads[:5])
    for n in range(2):
        cols = slice(n * 256, (n + 1) * 256)
        cgrad[:, cols] = dot(aog[...], flat(w, 1024 + n * 256, 1280 + n * 256)).astype(bf16)
        put(pack, 1024 + n * 256, dot(aog[...], ctx[:, cols], TN))
    router_grad = dot(lg_high, moe_in[...], TN) + dot(lg_low, moe_in[...], TN)
    put(pack, 1536, jnp.where(iota((128, D), 0) == 33, gain_two, router_grad).T)
    low32 = iota((SEQ, 256), 1) % 64 < 32
    low = iota((SEQ, 128), 1) < 64
    allowed = iota((2 * SEQ, SEQ), 0) % SEQ >= iota((2 * SEQ, SEQ), 1)
    wait(loads[5:])
    for m in range(4):
        cols = slice(m * 128, (m + 1) * 128)
        qs = stacked(q[:, cols], low)
        cs = stacked(cgrad[:, cols], low)
        scores = dot(qs, k[:, cols], NT) * SCALE
        probs = jnp.where(allowed, jnp.exp(scores - lse[m][:, :1]), 0.0)
        back = dot(cs, v[:, cols], NT)
        spread = jnp.sum(probs * back, axis=1, keepdims=True)
        sg = (probs * (back - spread)).astype(bf16)
        dq = dot(sg, k[:, cols])
        dlin[:, cols] = jnp.where(low, dq[:SEQ], dq[SEQ:]) * SCALE
        dk = dot(sg, qs, TN) * SCALE
        dv = dot(probs.astype(bf16), cs, TN)
        dk = dk + pltpu.roll(dk, 64, 1)
        dv = dv + pltpu.roll(dv, 64, 1)
        for base, val in ((512, dk), (768, dv)):
            at = slice(base + (m // 2) * 128, base + (m // 2) * 128 + 128)
            if m % 2 == 0:
                dlin[:, at] = val
            else:
                dlin[:, at] = jnp.where(low, dlin[:, at], val)
    lows = []
    for n in range(4):
        cols = slice(n * 256, (n + 1) * 256)
        lin = dlin[:, cols]
        if n < 3:
            lin = lin * cos[...] - swap_halves(lin, low32) * sin[...]
        lin = lin.astype(bf16)
        lows.append(lin)
        put(pack, n * 256, dot(attn_in[...], lin, TN))
    pairs = [
        (pack.at[at_late, :, at_core], dst.at[i])
        for dst, at_core in ((sent, 1 - core), (mine, core))
        for i, at_late in enumerate((late, 1 - late))
    ]
    moves = copies(pairs, sems, 14)
    start(moves)
    stores = stores + moves
    lows = jnp.concatenate(lows, axis=1)
    for n in range(4):
        cols = slice(n * 256, (n + 1) * 256)
        block = w[n // 2, (n % 2) * 8 : (n % 2) * 8 + 8, :, :, :1024].reshape(256, 1024)
        apart[:, cols] = dot(lows, block, NT)
    moves = copies([(apart.at[own], part_own)], sems, 18)
    start(moves)
    part_sent[...] = apart[pl.ds(mo((1 - half) * HALF, HALF), HALF), :].astype(bf16)
    x = rows[...].astype(f32)
    normed_one = x * lax.rsqrt(jnp.mean(x * x, axis=1, keepdims=True) + NORM_EPS)
    gain_one = jnp.sum(apart[...] * normed_one, axis=0, keepdims=True)
    lines = jnp.concatenate([gain_one[:, n * 128 : (n + 1) * 128] for n in range(8)], axis=0)
    gains[...] = lines
    wait(stores + moves)


def gain_lines(gain):
    high = gain.astype(bf16).astype(f32)
    return jnp.concatenate([high, (gain - high).astype(bf16).astype(f32)], axis=0)


def halves(pairs, sems):
    loads = []
    for part in range(2):
        at = slice(part * 8, part * 8 + 8)
        loads.append(copies([(src.at[at], dst.at[at]) for src, dst in pairs], sems, part * len(pairs)))
        start(loads[-1])
    return loads


def move_kernel(pos, g_own, g_yh, g_core, g_twist, mine_at, got_at, out, gain_out, mine, got, sems):
    loads = halves([(mine_at.at[1], mine), (got_at.at[1], got)], sems)
    lines = gain_lines((g_own[...] + g_yh[...]) + (g_core[...] + g_twist[...]))
    gain_out[...] = lines
    for part in range(2):
        wait(loads[part])
        at = slice(part * 8, part * 8 + 8)
        out[at, :, :PACK] = (mine[at].astype(f32) + got[at].astype(f32)).astype(bf16)
    for i in range(16):
        out[i, :, PACK:] = lines.astype(bf16)


def sum_kernel(pos, gain, mine_at, got_at, got_yl_at, out, mine, got, got_yl, sems):
    loads = halves([(mine_at.at[0], mine), (got_at.at[0], got), (got_yl_at, got_yl)], sems)
    for part in range(2):
        wait(loads[part])
        at = slice(part * 8, part * 8 + 8)
        total = mine[at].astype(f32) + got[at].astype(f32) + got_yl[at, :, :PACK].astype(f32)
        out[at, :, :PACK] = total.astype(bf16)
    total = gain[...] + got_yl[0, :, PACK:].astype(f32)
    lines = gain_lines(total[:8] + total[8:]).astype(bf16)
    for i in range(16):
        out[i, :, PACK:] = lines


def rows_kernel(pos, tok, aux, mg, part_own, out_own, got, out, rows_out):
    x = tok[...].astype(f32)
    factor = lax.rsqrt(jnp.mean(x * x, axis=1, keepdims=True) + NORM_EPS)
    normed = x * factor
    inner = (part_own[...] + got[1].astype(f32)) * aux[32:33, :]
    inner = factor * (inner - normed * jnp.mean(inner * normed, axis=1, keepdims=True))
    out[...] = (mg[...] + inner).astype(bf16)
    rows_out[...] = (out_own[...] + got[0].astype(f32)).astype(bf16)


def final_kernel(pos, got, w_query, w_key, w_value, w_out, w_router, gain_two, gain_one):
    total = got[0].astype(f32)
    for i in range(1, 16):
        total = total + got[i].astype(f32)
    w_query[...] = total[:, :512]
    w_key[...] = total[:, 512:768]
    w_value[...] = total[:, 768:1024]
    w_out[...] = total[:, 1024:1536]
    w_router[...] = total[:, 1536 : 1536 + EXPERTS]
    turned = jnp.concatenate([total[:, 1536:PACK], jnp.zeros((112, 128), f32)], axis=0).T
    gain_two[...] = turned[33:34, :16]
    gains = total[:8, PACK:] + total[8:, PACK:]
    at = pos[4]
    row = jnp.sum(jnp.where(iota((8, 128), 0) == at // 8, gains, 0.0), axis=0, keepdims=True)
    lanes = pltpu.roll(jnp.broadcast_to(row, (8, 128)), (128 - (at % 8) * 16) % 128, 1)
    gain_one[...] = lanes[0:1, :16]


def rotary_tables():
    column = iota((SEQ, 256), 1)
    frequency = ROPE_BASE ** (-((column % (HDIM // 2)).astype(f32) * 2.0 / HDIM))
    angles = iota((SEQ, 256), 0).astype(f32) * frequency
    sin = jnp.sin(angles)
    return jnp.cos(angles), jnp.where(column % HDIM < HDIM // 2, -sin, sin)


def swap(value, axis):
    if axis == "twist":
        return lax.ppermute(value, ("c", "yh"), [(0, 3), (3, 0), (1, 2), (2, 1)])
    if axis == "diag":
        return lax.ppermute(value, ("yl", "yh"), [(0, 3), (3, 0), (1, 2), (2, 1)])
    return lax.ppermute(value, axis, [(0, 1), (1, 0)])


def ring(value, axis, step):
    return lax.ppermute(value, axis, [(i, (i + step) % 4) for i in range(4)])


def plane(value):
    return lax.all_to_all(value, PLANE, 0, 0, tiled=True)


def added(*values, gate=None):
    total = (values[0] if gate is None else after(values[0], gate)).astype(f32)
    for value in values[1:]:
        total = total + value.astype(f32)
    return total.astype(bf16)


def in_hbm(value):
    return pltpu.with_memory_space_constraint(value, pltpu.HBM)


def after(value, *others):
    return lax.optimization_barrier((value, *others))[0]


def at_index(value, i):
    return lax.dynamic_index_in_dim(value, i, 0, keepdims=False)


def body(
    tokens,
    routes,
    cotangent,
    attn_gain,
    query_weight,
    key_weight,
    value_weight,
    out_weight,
    moe_gain,
    router_weight,
    expert_gate,
    expert_up,
    expert_down,
):
    half, core, late = lax.axis_index("yh"), lax.axis_index("c"), lax.axis_index("yl")
    place = lax.axis_index("x") * 4 + lax.axis_index("z")
    pos = jnp.stack([half, core, late, half * 16 + place, (late * 16 + place) * 2 + core, lax.axis_index("x"), lax.axis_index("z")]).astype(jnp.int32)
    cos, sin = rotary_tables()

    (packed,) = call(
        pack_kernel,
        [((16, 16, PACK), bf16)],
        [
            pos, query_weight, key_weight, value_weight, out_weight, router_weight,
            attn_gain.reshape(1, 16), moe_gain.reshape(1, 16),
        ],
        us=0,
    )
    w_a = plane(packed)
    tok_oth = swap(tokens, "yh")
    cot_oth = swap(cotangent, "yh")

    experts = jnp.stack([expert_gate, expert_up, expert_down])
    experts = experts.reshape(3, 16, 2, 16, 2, 128).transpose(3, 2, 0, 4, 1, 5).reshape(16, 192, 128)
    tab, tab_t, mask = call(
        route_kernel,
        [((SLOTS, SEQ), bf16), ((SEQ, SLOTS), bf16), ((SEQ, 128), f32)],
        [pos, routes],
        scratch=[pltpu.VMEM((128, SEQ), f32)],
        us=0,
    )
    grad, cot_sent = call(
        dispatch_kernel,
        [((SEQ, D), bf16), ((16, ROWS + 192, 128), bf16)],
        [pos, tab, cotangent, cot_oth, experts],
        us=3,
    )
    w_a = after(w_a, experts, cot_sent, tok_oth)
    w_b = swap(w_a, "yl")
    w_c = swap(w_a, "c")
    w_d = swap(w_b, "c")
    cot_slots = plane(after(cot_sent, w_c))

    e_own = lax.dynamic_slice_in_dim(cot_slots, ROWS + 96 * half, 96, 1)
    e_oth = lax.dynamic_slice_in_dim(cot_slots, ROWS + 96 * (1 - half), 96, 1)
    pieces = [e_own, swap(e_own, "yl"), swap(e_oth, "yh"), swap(e_oth, "diag")]
    pieces = pieces + [swap(piece, "c") for piece in pieces]
    w_gate, w_up, w_down = call(weights_kernel, [((D, 512), bf16)] * 3, [pos] + pieces, us=4, vmem=PART_BYTES)

    kept = [
        ((SEQ, D), bf16), ((128, D), f32), ((SEQ, D), bf16), ((SEQ, 512), bf16), ((SEQ, 512), bf16),
        ((SEQ, 512), bf16), ((SEQ, 512), bf16), ((4, 512, 128), f32),
    ]
    part, rows, aux, attn_in, q, k, v, ctx, lse = call(
        attn_kernel,
        [((SEQ, D), bf16)] + kept,
        [pos, tokens, tok_oth, cos, sin, w_a, w_b, w_c, w_d],
        late_from=5,
        late_outs=8,
        scratch=[pltpu.VMEM(shape, kind) for shape, kind in kept]
        + [pltpu.VMEM((2, 16, 2, 16, PACK), bf16), pltpu.SemaphoreType.DMA((12,))],
        us=7,
    )
    part_oth = swap(part, "yh")
    kept = [((SEQ, D), f32), ((SEQ, D), bf16), ((16, ROWS + 16, 128), bf16)]
    gates, middle, moe_in, x_sent = call(
        mid_kernel,
        [((SEQ, 128), f32)] + kept,
        [pos, rows, part, part_oth, aux, tab, mask],
        late_outs=3,
        scratch=[pltpu.VMEM((128, SEQ), f32)]
        + [pltpu.VMEM(shape, kind) for shape, kind in kept]
        + [pltpu.SemaphoreType.DMA((7,))],
        us=3,
    )
    x_slots = plane(x_sent)

    whole = pl.BlockSpec((D, 512), lambda i, *pos: (0, 0))
    by_row = pl.BlockSpec((4 * CAP, 512), lambda i, *pos: (i, 0))
    by_peer = lambda rows: pl.BlockSpec((4, rows, 128), lambda i, *pos: (i, 0, 0))
    dx, gate_g, up_g, scaled = call(
        expert_kernel,
        [((16, ROWS + 16, 128), bf16), ((SLOTS, 512), bf16), ((SLOTS, 512), bf16), ((SLOTS, 512), bf16)],
        [pos, in_hbm(x_slots), in_hbm(cot_slots), w_gate, w_up, w_down],
        scratch=[pltpu.VMEM((4 * CAP, D), bf16), pltpu.VMEM((4 * CAP, D), bf16)],
        grid=(4,),
        in_specs=[by_peer(ROWS + 16), by_peer(ROWS), whole, whole, whole],
        out_specs=[by_peer(ROWS + 16), by_row, by_row, by_row],
        us=12,
        hbm=True,
        vmem=PART_BYTES,
    )
    dx_back = plane(dx)

    full = pl.BlockSpec((SLOTS, 512), lambda i, *pos: (0, 0))
    by_col = pl.BlockSpec((16, 2 * CAP, 128), lambda i, *pos: (0, i, 0))
    by_owner = pl.BlockSpec((1, 2, 8, 96, 128), lambda i, pos: ((i // 2 + pos[2]) % 2, 0, i % 2, 0, 0))
    e_mine, e_sent = call(
        expert_grad_kernel,
        [((2, 2, 16, 96, 128), bf16), ((2, 2, 16, 96, 128), bf16)],
        [pos, x_slots, cot_slots, gate_g, up_g, scaled],
        scratch=[
            pltpu.VMEM((SLOTS, 256), bf16), pltpu.VMEM((SLOTS, 256), bf16), pltpu.VMEM((256, 512), bf16),
        ],
        grid=(4,),
        in_specs=[by_col, by_col, full, full, full],
        out_specs=[by_owner, by_owner],
        us=0,
        prefetch=True,
    )


    e_got = swap(e_sent, "c")
    e_yl, e_yh, e_diag = (
        swap(added(e_mine[i, j], e_got[i, j]), axis) for i, j, axis in ((1, 0, "yl"), (0, 1, "yh"), (1, 1, "diag"))
    )
    (y,) = call(
        expert_out_kernel,
        [((16, ROWS, 128), bf16)],
        [pos, after(scaled, e_got), w_down],
        grid=(4,),
        in_specs=[full, pl.BlockSpec((256, 512), lambda i, *pos: (i, 0))],
        out_specs=[by_col],
        us=0,
    )
    dx_back = after(dx_back, e_yl, y)
    (comb,) = call(
        combine_kernel, [((SEQ, EXT), bf16)], [pos, tab_t, dx_back],
        scratch=[pltpu.VMEM((SLOTS, EXT), bf16)], us=0,
    )
    comb = after(comb, e_yh, e_diag)
    comb_oth = swap(comb, "yh")
    y_back = plane(y)
    by_first = pl.BlockSpec((1, 1, 16, 96, 128), lambda i, *pos: (0, 0, 0, 0, 0))
    by_third = pl.BlockSpec((16, 96, 128), lambda i, *pos: (0, 0, 0))
    (e_cat,) = call(
        expert_sum_kernel,
        [((16, 192, 128), bf16)],
        [pos, after(e_mine, comb), e_got, e_yl, e_yh, e_diag],
        grid=(1,),
        in_specs=[by_first, by_first, by_third, by_third, by_third],
        out_specs=[pl.BlockSpec((16, 192, 128), lambda i, *pos: (0, 0, 0))],
        us=0,
    )
    comb_oth = after(comb_oth, e_cat)
    part_sent, gains, mg_own, part_own, a_mine, a_sent = call(
        back_kernel,
        [
            ((HALF, D), bf16), ((8, 128), f32), ((HALF, D), f32), ((HALF, D), f32),
            ((2, 16, 16, PACK), bf16), ((2, 16, 16, PACK), bf16),
        ],
        [
            pos, comb, comb_oth, middle, moe_in, gates, aux, grad,
            w_a, w_b, w_c, w_d, ctx, q, k, v, lse, cos, sin, attn_in, rows,
        ],
        late_from=8,
        late_outs=4,
        scratch=[
            pltpu.VMEM((2, 16, 2, 16, PACK), bf16), pltpu.VMEM((SEQ, 512), bf16), pltpu.VMEM((SEQ, 512), bf16),
            pltpu.VMEM((SEQ, 512), bf16), pltpu.VMEM((SEQ, 512), bf16), pltpu.VMEM((4, 512, 128), f32),
            pltpu.VMEM((SEQ, 256), f32), pltpu.VMEM((SEQ, 256), f32), pltpu.VMEM((SEQ, D), bf16),
            pltpu.VMEM((SEQ, D), bf16), pltpu.SemaphoreType.DMA((19,)),
            pltpu.VMEM((SEQ, D), f32), pltpu.VMEM((SEQ, D), bf16), pltpu.VMEM((2, 16, 2, 16, PACK), bf16),
            pltpu.VMEM((SEQ, 512), bf16), pltpu.VMEM((SEQ, D), f32), pltpu.VMEM((SEQ, D), f32),
        ],
        us=0,
    )

    a_got = swap(a_sent, "c")
    block = pltpu.VMEM((16, 16, PACK), bf16)
    wide = pltpu.VMEM((16, 16, PACK + 128), bf16)
    a_move, gains = call(
        move_kernel,
        [((16, 16, PACK + 128), bf16), ((16, 128), f32)],
        [pos, gains] + [swap(gains, axis) for axis in ("yh", "c", "twist")] + [a_mine, a_got],
        late_from=5,
        scratch=[block, block, pltpu.SemaphoreType.DMA((4,))],
        us=0,
    )
    a_yl = swap(a_move, "yl")
    e_back = plane(after(e_cat, y_back))
    out_own, out_sent = call(
        finish_kernel,
        [((HALF, D), f32), ((2, HALF, D), bf16)],
        [pos, tab_t, middle, after(y_back, a_move), part_sent],
        scratch=[pltpu.VMEM((SLOTS, D), bf16), pltpu.VMEM((SEQ, D), f32)],
        us=0,
    )
    a_yl = after(a_yl, out_sent)
    (a_sum,) = call(
        sum_kernel,
        [((16, 16, PACK + 128), bf16)],
        [pos, gains, a_mine, a_got, a_yl],
        late_from=2,
        scratch=[block, block, wide, pltpu.SemaphoreType.DMA((6,))],
        us=0,
    )
    total = plane(after(a_sum, e_back))
    grad_gate, grad_up, grad_down = call(
        expert_final_kernel, [((16, EXPERTS, 256), f32)] * 3, [pos, after(e_back, a_sum)], us=0
    )

    rows_oth = swap(after(out_sent, a_sum), "yh")
    rows_oth = after(rows_oth, grad_gate)
    input_grad, output = call(
        rows_kernel,
        [((HALF, D), bf16), ((HALF, D), bf16)],
        [pos, tokens, aux, mg_own, part_own, out_own, rows_oth],
        us=0,
    )
    w_query, w_key, w_value, w_out, w_router, gain_two, gain_one = call(
        final_kernel,
        [((16, n), f32) for n in (512, 256, 256, 512, 32)] + [((1, 16), f32)] * 2,
        [pos, total],
        us=0,
    )

    return (
        output,
        input_grad,
        gain_one.reshape(16),
        w_query,
        w_key,
        w_value,
        w_out,
        gain_two.reshape(16),
        w_router,
        grad_gate,
        grad_up,
        grad_down,
    )


def solution(mesh):
    fine = Mesh(mesh.devices.reshape(2, 4, 4, 2, 2), ("yl", "x", "z", "c", "yh"))
    dp, every = ("yl", "x", "z", "c"), ("yl", "x", "z", "c", "yh")
    in_specs = (
        P(every, None),
        P(dp, None),
        P(every, None),
        P(dp),
        P(dp, "yh"),
        P(dp, "yh"),
        P(dp, "yh"),
        P(dp, "yh"),
        P(dp),
        P(dp, None),
        P(dp, None, "yh"),
        P(dp, None, "yh"),
        P(dp, None, "yh"),
    )
    out_specs = (
        P(every, None),
        P(every, None),
        P(dp),
        P(dp, "yh"),
        P(dp, "yh"),
        P(dp, "yh"),
        P(dp, "yh"),
        P(dp),
        P(dp, None),
        P(dp, None, "yh"),
        P(dp, None, "yh"),
        P(dp, None, "yh"),
    )
    return jax.shard_map(body, mesh=fine, in_specs=in_specs, out_specs=out_specs, check_vma=False)
```

```python
import math

import jax
import jax.numpy as jnp
from jax import lax
from jax.experimental import pallas as pl
from jax.experimental.pallas import tpu as pltpu
from jax.sharding import Mesh, PartitionSpec as P

bf16 = jnp.bfloat16
f32 = jnp.float32

D = 1024
HDIM = 64
SEQ = 256
HALF = 128
EXPERTS = 32
CAP = 80
SLOTS = 16 * CAP
EXT = D + 128
ROWS = 8 * CAP
PACK = 1664
NORM_EPS = 1e-06
ROPE_BASE = 10000.0
SCALE = 0.125
PLANE = ("x", "z")
NT = (((1,), (1,)), ((), ()))
TN = (((0,), (0,)), ((), ()))
VMEM_BYTES = 65472 * 1024
PART_BYTES = 40 * 1024 * 1024


def mo(value, by):
    return pl.multiple_of(value, by)


def dot(a, b, dims=(((1,), (0,)), ((), ()))):
    return lax.dot_general(a, b, dims, preferred_element_type=f32)


def split(value):
    high = value.astype(bf16)
    return high, (value - high.astype(f32)).astype(bf16)


def iota(shape, dim):
    return lax.broadcasted_iota(jnp.int32, shape, dim)


def call(kernel, outs, args, scratch=(), grid=None, in_specs=None, out_specs=None, us=1, late_from=None, late_outs=0, prefetch=False, vmem=VMEM_BYTES, hbm=False):
    smem = pl.BlockSpec(memory_space=pltpu.SMEM)
    params = pltpu.CompilerParams(vmem_limit_bytes=vmem)
    out_shape = [(pltpu.HBM if hbm else jax.ShapeDtypeStruct)(shape, kind) for shape, kind in outs]
    nbytes = sum(a.size * a.dtype.itemsize for a in args) + sum(
        math.prod(shape) * jnp.dtype(kind).itemsize for shape, kind in outs
    )
    cost = pl.CostEstimate(flops=int(us * 1.15e9) + 1000, bytes_accessed=nbytes if us else 1000, transcendentals=0)
    if grid is None:
        vmem = pl.BlockSpec(memory_space=pltpu.VMEM)
        early = len(args) if late_from is None else late_from
        in_specs = [smem] + [vmem] * (early - 1) + [pl.BlockSpec(memory_space=pl.ANY)] * (len(args) - early)
        out_specs = [vmem] * (len(outs) - late_outs) + [pl.BlockSpec(memory_space=pl.ANY)] * late_outs
        return pl.pallas_call(
            kernel,
            out_shape=out_shape,
            in_specs=in_specs,
            out_specs=out_specs,
            scratch_shapes=scratch,
            compiler_params=params,
            cost_estimate=cost,
        )(*args)
    if not prefetch:
        return pl.pallas_call(
            kernel,
            grid=grid,
            out_shape=out_shape,
            in_specs=[smem] + in_specs,
            out_specs=out_specs,
            scratch_shapes=scratch,
            compiler_params=params,
            cost_estimate=cost,
        )(*args)
    return pl.pallas_call(
        kernel,
        grid_spec=pltpu.PrefetchScalarGridSpec(
            num_scalar_prefetch=1, grid=grid, in_specs=in_specs, out_specs=out_specs, scratch_shapes=scratch
        ),
        out_shape=out_shape,
        compiler_params=params,
        cost_estimate=cost,
    )(*args)


def copies(pairs, sems, first=0):
    return [pltpu.make_async_copy(src, dst, sems.at[first + i]) for i, (src, dst) in enumerate(pairs)]


def start(loads):
    for load in loads:
        load.start()


def wait(loads):
    for load in loads:
        load.wait()


def place_rows(w, pieces, late, core):
    at = ((late, core), (1 - late, core), (late, 1 - core), (1 - late, 1 - core))
    return [(src, w.at[at_late, :, at_core]) for src, (at_late, at_core) in zip(pieces, at)]


def flat(w, first, last):
    return w[:, :, :, :, first:last].reshape(D, last - first)


def pack_kernel(pos, w_query, w_key, w_value, w_out, router, gain_one, gain_two, out):
    at = iota((128, 128), 0)
    rest = jnp.zeros((1, 112), f32)
    first, second = (jnp.concatenate([gain[...].astype(f32), rest], axis=1) for gain in (gain_one, gain_two))
    gains = pick(at, first, second)
    gains = gains.T[:16]
    wide = jnp.concatenate([router[...].astype(f32), jnp.zeros((16, 96), f32)], axis=1)
    small = (wide + pltpu.roll(gains, EXPERTS, 1)).astype(bf16)
    for i in range(16):
        out[i, :, :512] = w_query[...]
        out[i, :, 512:768] = w_key[...]
        out[i, :, 768:1024] = w_value[...]
        out[i, :, 1024:1536] = w_out[...]
        out[i, :, 1536:] = small


def route_kernel(pos, routes, tab, tab_t, mask_out, turned):
    half = pos[0]
    named = routes[...]
    lane = iota((SEQ, 128), 1)
    mask = jnp.zeros((SEQ, 128), f32)
    for k in range(named.shape[1]):
        mask = mask + jnp.where(named[:, k : k + 1] == lane, 1.0, 0.0)
    mask_out[...] = mask
    below = jnp.where(iota((SEQ, SEQ), 0) > iota((SEQ, SEQ), 1), 1.0, 0.0).astype(bf16)
    place = dot(below, mask.astype(bf16))
    turned[...] = jnp.where(mask > 0.0, place, -1.0).T
    slot = iota((CAP, SEQ), 0).astype(f32)
    for i in range(16):
        row = turned[pl.ds(half * 16 + i, 1), :]
        tab[i * CAP : (i + 1) * CAP, :] = jnp.where(slot == row, 1.0, 0.0).astype(bf16)
    for n in range(SLOTS // 128):
        cols = slice(n * 128, (n + 1) * 128)
        tab_t[:, cols] = tab[cols, :].astype(f32).T.astype(bf16)


def dispatch_kernel(pos, tab, cot_own, cot_oth, packed, grad, sent):
    half = pos[0]
    sent[:, ROWS : ROWS + 192, :] = packed[...]
    grad[pl.ds(mo(half * HALF, HALF), HALF), :] = cot_own[...]
    grad[pl.ds(mo((1 - half) * HALF, HALF), HALF), :] = cot_oth[...]
    for n in range(4):
        spread_blocks(sent, n, dot(tab[...], grad[:, n * 256 : (n + 1) * 256]).astype(bf16), 16)


def spread_blocks(dst, n, value, peers):
    for i in range(peers):
        for j in range(2):
            at = (2 * n + j) * CAP
            dst[i, at : at + CAP, :] = value[i * CAP : (i + 1) * CAP, j * 128 : (j + 1) * 128]


def gather_blocks(dst, src, peers, blocks):
    for i in range(peers):
        for j in range(blocks):
            dst[i * CAP : (i + 1) * CAP, j * 128 : (j + 1) * 128] = src[i, j * CAP : (j + 1) * CAP, :]


def pick(rows, value, other):
    return jnp.where(rows == 0, value, jnp.where(rows == 1, other, 0.0))


def swap_halves(u, low):
    return jnp.where(low, pltpu.roll(u, 224, 1), pltpu.roll(u, 32, 1))


def doubled(tile, low, which):
    other = pltpu.roll(tile, 64, 1)
    return jnp.where(low, tile, other) if which == 0 else jnp.where(low, other, tile)


def stacked(tile, low):
    zero = jnp.zeros_like(tile)
    return jnp.concatenate([jnp.where(low, tile, zero), jnp.where(low, zero, tile)], axis=0)


def attn_kernel(
    pos, tok_own, tok_oth, cos, sin, w_a, w_b, w_c, w_d,
    part, rows_at, aux_at, attn_in_at, q_at, k_at, v_at, ctx_at, lse_at,
    rows, aux, attn_in, q_out, k_out, v_out, ctx, lse_out, w, sems,
):
    half, core, late = pos[0], pos[1], pos[2]
    loads = copies(place_rows(w, (w_a, w_b, w_c, w_d), late, core), sems)
    start(loads)
    rows[pl.ds(mo(half * HALF, HALF), HALF), :] = tok_own[...]
    rows[pl.ds(mo((1 - half) * HALF, HALF), HALF), :] = tok_oth[...]
    x = rows[...].astype(f32)
    normed = x * lax.rsqrt(jnp.mean(x * x, axis=1, keepdims=True) + NORM_EPS)
    wait(loads)
    aux[...] = flat(w, 1536, PACK).astype(f32).T
    attn_in[...] = (normed * aux[32:33, :]).astype(bf16)
    low32 = iota((SEQ, 256), 1) % 64 < 32
    low = iota((SEQ, 128), 1) < 64
    for n in range(4):
        lin = dot(attn_in[...], flat(w, n * 256, (n + 1) * 256))
        if n < 3:
            lin = lin * cos[...] + swap_halves(lin, low32) * sin[...]
        if n < 2:
            q_out[:, n * 256 : (n + 1) * 256] = lin.astype(bf16)
        else:
            dst = k_out if n == 2 else v_out
            for m in range(4):
                tile = lin[:, (m // 2) * 128 : (m // 2) * 128 + 128]
                dst[:, m * 128 : (m + 1) * 128] = doubled(tile, low, m % 2).astype(bf16)
    pairs = [(rows, rows_at), (aux, aux_at), (attn_in, attn_in_at), (q_out, q_at), (k_out, k_at), (v_out, v_at)]
    stores = copies(pairs, sems, 4)
    start(stores)
    allowed = iota((2 * SEQ, SEQ), 0) % SEQ >= iota((2 * SEQ, SEQ), 1)
    for m in range(4):
        cols = slice(m * 128, (m + 1) * 128)
        scores = dot(stacked(q_out[:, cols], low), k_out[:, cols], NT) * SCALE
        scores = jnp.where(allowed, scores, -1e30)
        peak = jnp.max(scores, axis=1, keepdims=True)
        raised = jnp.exp(scores - peak)
        total = jnp.sum(raised, axis=1, keepdims=True)
        lse_out[m] = jnp.broadcast_to(peak + jnp.log(total), (2 * SEQ, 128))
        probs = (raised * (1.0 / total)).astype(bf16)
        both = dot(probs, v_out[:, cols])
        ctx[:, cols] = jnp.where(low, both[:SEQ], both[SEQ:]).astype(bf16)
    more = copies([(ctx, ctx_at), (lse_out, lse_at)], sems, 10)
    start(more)
    for n in range(4):
        outs = slice(n * 256, (n + 1) * 256)
        part[:, outs] = dot(ctx[...], w[n // 2, (n % 2) * 8 : (n % 2) * 8 + 8, :, :, 1024:1536].reshape(256, 512), NT).astype(bf16)
    wait(stores + more)


def mid_kernel(
    pos, rows, part_own, part_oth, aux, tab, mask,
    gates_out, middle_at, moe_in_at, sent_at, turned, middle, moe_in, sent, sems,
):
    half = pos[0]
    value = rows[...].astype(f32) + (part_own[...].astype(f32) + part_oth[...].astype(f32))
    middle[...] = value
    factor = lax.rsqrt(jnp.mean(value * value, axis=1, keepdims=True) + NORM_EPS)
    moe_in[...] = (value * factor * aux[33:34, :]).astype(bf16)
    moves = copies([(middle, middle_at), (moe_in, moe_in_at)], sems)
    start(moves)
    logits = dot(moe_in[...], aux[...].astype(bf16), NT)
    chosen = jnp.where(mask[...] > 0.0, logits, -1e30)
    raised = jnp.exp(chosen - jnp.max(chosen, axis=1, keepdims=True)) * mask[...]
    gates = raised / jnp.sum(raised, axis=1, keepdims=True)
    gates_out[...] = gates
    turned[...] = gates.T
    for n in range(4):
        spread_blocks(sent, n, dot(tab[...], moe_in[:, n * 256 : (n + 1) * 256]).astype(bf16), 16)
        at = slice(n * 160, (n + 1) * 160)
        (move,) = copies([(sent.at[:, at], sent_at.at[:, at])], sems, 2 + n)
        move.start()
        moves.append(move)
    lane = iota((CAP, 128), 1)
    slots = jnp.zeros((CAP, 128), f32)
    for i in range(16):
        row = turned[pl.ds(half * 16 + i, 1), :]
        found = jnp.sum(tab[i * CAP : (i + 1) * CAP, :].astype(f32) * row, axis=1, keepdims=True)
        slots = jnp.where(lane == i, found, slots)
    slots = jnp.concatenate([slots, jnp.zeros((128 - CAP, 128), f32)], axis=0).T
    at = iota((16, 128), 0)
    for i in range(16):
        line = slots[i : i + 1, :]
        high = line.astype(bf16).astype(f32)
        sent[i, ROWS : ROWS + 16, :] = pick(at, high, line - high).astype(bf16)
    at = slice(ROWS, ROWS + 16)
    (move,) = copies([(sent.at[:, at], sent_at.at[:, at])], sems, 6)
    move.start()
    wait(moves + [move])


def weights_kernel(pos, a0, a1, a2, a3, b0, b1, b2, b3, w_gate, w_up, w_down):
    core, late = pos[1], pos[2]
    for srcs, at_core in (((a0, a1, a2, a3), core), ((b0, b1, b2, b3), 1 - core)):
        for src, at_late, f in zip(srcs, (late, 1 - late, late, 1 - late), (0, 0, 1, 1)):
            for i in range(16):
                rows = pl.ds(mo((at_late * 16 + i) * 32 + at_core * 16, 16), 16)
                for j, dst in enumerate((w_gate, w_up, w_down)):
                    for h in range(2):
                        cols = slice(f * 256 + h * 128, f * 256 + h * 128 + 128)
                        dst[rows, cols] = src[i, (j * 2 + h) * 16 : (j * 2 + h + 1) * 16, :]


def expert_kernel(pos, x, c, w_gate, w_up, w_down, dx, gate_g, up_g, scaled, xs, cs):
    gather_blocks(xs, x, 4, 8)
    gather_blocks(cs, c, 4, 8)
    lines = x[:, ROWS : ROWS + 16, :].astype(f32).reshape(64, 128)
    lines = jnp.concatenate([lines, jnp.zeros((64, 128), f32)], axis=0).T[:CAP]
    gate = jnp.concatenate(
        [lines[:, 16 * i : 16 * i + 1] + lines[:, 16 * i + 1 : 16 * i + 2] for i in range(4)], axis=0
    )
    g = dot(xs[...], w_gate[...])
    u = dot(xs[...], w_up[...])
    sig = jax.nn.sigmoid(g)
    silu = g * sig
    hidden = (silu * u).astype(bf16).astype(f32)
    raw = dot(cs[...], w_down[...])
    gate_grad = jnp.sum(hidden * raw, axis=1, keepdims=True)
    back = gate * raw
    gate_g[...] = (back * u * sig * (1.0 + g * (1.0 - sig))).astype(bf16)
    up_g[...] = (back * silu).astype(bf16)
    scaled[...] = (gate * hidden).astype(bf16)
    for n in range(4):
        cols = slice(n * 256, (n + 1) * 256)
        value = dot(gate_g[...], w_gate[cols, :], NT) + dot(up_g[...], w_up[cols, :], NT)
        spread_blocks(dx, n, value.astype(bf16), 4)
    high = gate_grad.astype(bf16).astype(f32)
    lane = iota((CAP, 128), 1)
    slots = jnp.zeros((CAP, 128), f32)
    for i in range(4):
        rows = slice(i * CAP, (i + 1) * CAP)
        slots = slots + pick(lane - 16 * i, high[rows], gate_grad[rows] - high[rows])
    slots = jnp.concatenate([slots, jnp.zeros((128 - CAP, 128), f32)], axis=0).T
    for i in range(4):
        dx[i, ROWS : ROWS + 16, :] = slots[16 * i : 16 * (i + 1), :].astype(bf16)


def expert_grad_kernel(pos, x, c, gate_g, up_g, scaled, mine, sent, xs, cs, held):
    core = pos[1]
    gather_blocks(xs, x, 16, 2)
    gather_blocks(cs, c, 16, 2)
    for j, (lhs, rhs) in enumerate(((xs, gate_g), (xs, up_g), (cs, scaled))):
        held[...] = dot(lhs[...], rhs[...], TN).astype(bf16)
        for i in range(8):
            for dst, at_core in ((mine, core), (sent, 1 - core)):
                rows = pl.ds(mo(i * 32 + at_core * 16, 16), 16)
                for f in range(2):
                    for h in range(2):
                        cols = slice(f * 256 + h * 128, f * 256 + h * 128 + 128)
                        dst[0, f, i, (j * 2 + h) * 16 : (j * 2 + h + 1) * 16, :] = held[rows, cols]


def expert_out_kernel(pos, scaled, w_down, y):
    value = dot(scaled[...], w_down[...], NT).astype(bf16)
    for i in range(16):
        for j in range(2):
            y[i, j * CAP : (j + 1) * CAP, :] = value[i * CAP : (i + 1) * CAP, j * 128 : (j + 1) * 128]


def expert_sum_kernel(pos, mine, got, got_yl, got_yh, got_diag, out):
    out[:, :96, :] = (mine[0, 0].astype(f32) + got[0, 0].astype(f32) + got_yl[...].astype(f32)).astype(bf16)
    out[:, 96:, :] = (got_yh[...].astype(f32) + got_diag[...].astype(f32)).astype(bf16)


def expert_final_kernel(pos, got, *outs):
    half = pos[0]
    for part, at_half in enumerate((half, 1 - half)):
        for j in range(6):
            at = part * 96 + j * 16
            value = jnp.swapaxes(got[:, at : at + 16, :].astype(f32), 0, 1)
            cols = slice((j % 2) * 128, (j % 2) * 128 + 128)
            outs[j // 2][:, pl.ds(mo(at_half * 16, 16), 16), cols] = value


def combine_kernel(pos, tab_t, got, out, held):
    half = pos[0]
    gather_blocks(held, got, 16, 8)
    lines = got[:, ROWS : ROWS + 16, :].astype(f32).reshape(256, 128).T[:CAP]
    lane = iota((CAP, 128), 1)
    for i in range(16):
        e = half * 16 + i
        high, low = lines[:, 16 * i : 16 * i + 1], lines[:, 16 * i + 1 : 16 * i + 2]
        extra = jnp.where(lane == e, high, jnp.where(lane == e + EXPERTS, low, 0.0))
        held[i * CAP : (i + 1) * CAP, D:EXT] = extra.astype(bf16)
    for start in range(0, EXT, 256):
        cols = slice(start, min(start + 256, EXT))
        out[:, cols] = dot(tab_t[...], held[:, cols]).astype(bf16)


def finish_kernel(pos, tab_t, middle, got, part_sent, own, sent, gathered, held):
    half = pos[0]
    gather_blocks(gathered, got, 16, 8)
    for n in range(4):
        cols = slice(n * 256, (n + 1) * 256)
        held[:, cols] = dot(tab_t[...], gathered[:, cols])
    mine = pl.ds(mo(half * HALF, HALF), HALF)
    own[...] = middle[mine, :] + held[mine, :]
    sent[0] = held[pl.ds(mo((1 - half) * HALF, HALF), HALF), :].astype(bf16)
    sent[1] = part_sent[...]


def put(pack, first, value):
    width = value.shape[1]
    pack[:, :, :, :, first : first + width] = value.astype(bf16).reshape(2, 16, 2, 16, width)


def back_kernel(
    pos, comb_own, comb_oth, middle, moe_in, gates, aux, grad,
    w_a, w_b, w_c, w_d, ctx_at, q_at, k_at, v_at, lse_at, cos_at, sin_at, attn_in_at, rows_at,
    part_sent, gains, mg_own, part_own, mine, sent,
    w, ctx, q, k, v, lse, cos, sin, attn_in, rows, sems, mg, aog, pack, cgrad, dlin, apart,
):
    half, core, late = pos[0], pos[1], pos[2]
    pairs = place_rows(w, (w_a, w_b, w_c, w_d), late, core) + [
        (ctx_at, ctx), (q_at, q), (k_at, k), (v_at, v), (lse_at, lse), (cos_at, cos), (sin_at, sin),
        (attn_in_at, attn_in), (rows_at, rows),
    ]
    loads = copies(pairs, sems)
    start(loads)
    gg = comb_own[:, D:EXT].astype(f32) + comb_oth[:, D:EXT].astype(f32)
    gg = gg + pltpu.roll(gg, 96, 1)
    gate = gates[...]
    logit_grad = gate * (gg - jnp.sum(gate * gg, axis=1, keepdims=True))
    lg_high, lg_low = split(logit_grad)
    router_t = aux[...].astype(bf16)
    moe_grad = comb_own[:, :D].astype(f32) + comb_oth[:, :D].astype(f32)
    moe_grad = moe_grad + dot(lg_high, router_t) + dot(lg_low, router_t)
    value = middle[...]
    factor = lax.rsqrt(jnp.mean(value * value, axis=1, keepdims=True) + NORM_EPS)
    normed = value * factor
    gain_two = jnp.sum(moe_grad * normed, axis=0, keepdims=True)
    inner = moe_grad * aux[33:34, :]
    mg[...] = grad[...].astype(f32) + factor * (
        inner - normed * jnp.mean(inner * normed, axis=1, keepdims=True)
    )
    own = pl.ds(mo(half * HALF, HALF), HALF)
    stores = copies([(mg.at[own], mg_own)], sems, 13)
    start(stores)
    aog[...] = mg[...].astype(bf16)
    wait(loads[:5])
    for n in range(2):
        cols = slice(n * 256, (n + 1) * 256)
        cgrad[:, cols] = dot(aog[...], flat(w, 1024 + n * 256, 1280 + n * 256)).astype(bf16)
        put(pack, 1024 + n * 256, dot(aog[...], ctx[:, cols], TN))
    router_grad = dot(lg_high, moe_in[...], TN) + dot(lg_low, moe_in[...], TN)
    put(pack, 1536, jnp.where(iota((128, D), 0) == 33, gain_two, router_grad).T)
    low32 = iota((SEQ, 256), 1) % 64 < 32
    low = iota((SEQ, 128), 1) < 64
    allowed = iota((2 * SEQ, SEQ), 0) % SEQ >= iota((2 * SEQ, SEQ), 1)
    wait(loads[5:])
    for m in range(4):
        cols = slice(m * 128, (m + 1) * 128)
        qs = stacked(q[:, cols], low)
        cs = stacked(cgrad[:, cols], low)
        scores = dot(qs, k[:, cols], NT) * SCALE
        probs = jnp.where(allowed, jnp.exp(scores - lse[m][:, :1]), 0.0)
        back = dot(cs, v[:, cols], NT)
        spread = jnp.sum(probs * back, axis=1, keepdims=True)
        sg = (probs * (back - spread)).astype(bf16)
        dq = dot(sg, k[:, cols])
        dlin[:, cols] = jnp.where(low, dq[:SEQ], dq[SEQ:]) * SCALE
        dk = dot(sg, qs, TN) * SCALE
        dv = dot(probs.astype(bf16), cs, TN)
        dk = dk + pltpu.roll(dk, 64, 1)
        dv = dv + pltpu.roll(dv, 64, 1)
        for base, val in ((512, dk), (768, dv)):
            at = slice(base + (m // 2) * 128, base + (m // 2) * 128 + 128)
            if m % 2 == 0:
                dlin[:, at] = val
            else:
                dlin[:, at] = jnp.where(low, dlin[:, at], val)
    lows = []
    for n in range(4):
        cols = slice(n * 256, (n + 1) * 256)
        lin = dlin[:, cols]
        if n < 3:
            lin = lin * cos[...] - swap_halves(lin, low32) * sin[...]
        lin = lin.astype(bf16)
        lows.append(lin)
        put(pack, n * 256, dot(attn_in[...], lin, TN))
    pairs = [
        (pack.at[at_late, :, at_core], dst.at[i])
        for dst, at_core in ((sent, 1 - core), (mine, core))
        for i, at_late in enumerate((late, 1 - late))
    ]
    moves = copies(pairs, sems, 14)
    start(moves)
    stores = stores + moves
    lows = jnp.concatenate(lows, axis=1)
    for n in range(4):
        cols = slice(n * 256, (n + 1) * 256)
        block = w[n // 2, (n % 2) * 8 : (n % 2) * 8 + 8, :, :, :1024].reshape(256, 1024)
        apart[:, cols] = dot(lows, block, NT)
    moves = copies([(apart.at[own], part_own)], sems, 18)
    start(moves)
    part_sent[...] = apart[pl.ds(mo((1 - half) * HALF, HALF), HALF), :].astype(bf16)
    x = rows[...].astype(f32)
    normed_one = x * lax.rsqrt(jnp.mean(x * x, axis=1, keepdims=True) + NORM_EPS)
    gain_one = jnp.sum(apart[...] * normed_one, axis=0, keepdims=True)
    lines = jnp.concatenate([gain_one[:, n * 128 : (n + 1) * 128] for n in range(8)], axis=0)
    gains[...] = lines
    wait(stores + moves)


def gain_lines(gain):
    high = gain.astype(bf16).astype(f32)
    return jnp.concatenate([high, (gain - high).astype(bf16).astype(f32)], axis=0)


def halves(pairs, sems):
    loads = []
    for part in range(2):
        at = slice(part * 8, part * 8 + 8)
        loads.append(copies([(src.at[at], dst.at[at]) for src, dst in pairs], sems, part * len(pairs)))
        start(loads[-1])
    return loads


def move_kernel(pos, g_own, g_yh, g_core, g_twist, mine_at, got_at, out, gain_out, mine, got, sems):
    loads = halves([(mine_at.at[1], mine), (got_at.at[1], got)], sems)
    lines = gain_lines((g_own[...] + g_yh[...]) + (g_core[...] + g_twist[...]))
    gain_out[...] = lines
    for part in range(2):
        wait(loads[part])
        at = slice(part * 8, part * 8 + 8)
        out[at, :, :PACK] = (mine[at].astype(f32) + got[at].astype(f32)).astype(bf16)
    for i in range(16):
        out[i, :, PACK:] = lines.astype(bf16)


def sum_kernel(pos, gain, mine_at, got_at, got_yl_at, out, mine, got, got_yl, sems):
    loads = halves([(mine_at.at[0], mine), (got_at.at[0], got), (got_yl_at, got_yl)], sems)
    for part in range(2):
        wait(loads[part])
        at = slice(part * 8, part * 8 + 8)
        total = mine[at].astype(f32) + got[at].astype(f32) + got_yl[at, :, :PACK].astype(f32)
        out[at, :, :PACK] = total.astype(bf16)
    total = gain[...] + got_yl[0, :, PACK:].astype(f32)
    lines = gain_lines(total[:8] + total[8:]).astype(bf16)
    for i in range(16):
        out[i, :, PACK:] = lines


def rows_kernel(pos, tok, aux, mg, part_own, out_own, got, out, rows_out):
    x = tok[...].astype(f32)
    factor = lax.rsqrt(jnp.mean(x * x, axis=1, keepdims=True) + NORM_EPS)
    normed = x * factor
    inner = (part_own[...] + got[1].astype(f32)) * aux[32:33, :]
    inner = factor * (inner - normed * jnp.mean(inner * normed, axis=1, keepdims=True))
    out[...] = (mg[...] + inner).astype(bf16)
    rows_out[...] = (out_own[...] + got[0].astype(f32)).astype(bf16)


def final_kernel(pos, got, w_query, w_key, w_value, w_out, w_router, gain_two, gain_one):
    total = got[0].astype(f32)
    for i in range(1, 16):
        total = total + got[i].astype(f32)
    w_query[...] = total[:, :512]
    w_key[...] = total[:, 512:768]
    w_value[...] = total[:, 768:1024]
    w_out[...] = total[:, 1024:1536]
    w_router[...] = total[:, 1536 : 1536 + EXPERTS]
    turned = jnp.concatenate([total[:, 1536:PACK], jnp.zeros((112, 128), f32)], axis=0).T
    gain_two[...] = turned[33:34, :16]
    gains = total[:8, PACK:] + total[8:, PACK:]
    at = pos[4]
    row = jnp.sum(jnp.where(iota((8, 128), 0) == at // 8, gains, 0.0), axis=0, keepdims=True)
    lanes = pltpu.roll(jnp.broadcast_to(row, (8, 128)), (128 - (at % 8) * 16) % 128, 1)
    gain_one[...] = lanes[0:1, :16]


def rotary_tables():
    column = iota((SEQ, 256), 1)
    frequency = ROPE_BASE ** (-((column % (HDIM // 2)).astype(f32) * 2.0 / HDIM))
    angles = iota((SEQ, 256), 0).astype(f32) * frequency
    sin = jnp.sin(angles)
    return jnp.cos(angles), jnp.where(column % HDIM < HDIM // 2, -sin, sin)


def swap(value, axis):
    if axis == "twist":
        return lax.ppermute(value, ("c", "yh"), [(0, 3), (3, 0), (1, 2), (2, 1)])
    if axis == "diag":
        return lax.ppermute(value, ("yl", "yh"), [(0, 3), (3, 0), (1, 2), (2, 1)])
    return lax.ppermute(value, axis, [(0, 1), (1, 0)])


def ring(value, axis, step):
    return lax.ppermute(value, axis, [(i, (i + step) % 4) for i in range(4)])


def plane(value):
    return lax.all_to_all(value, PLANE, 0, 0, tiled=True)


def added(*values, gate=None):
    total = (values[0] if gate is None else after(values[0], gate)).astype(f32)
    for value in values[1:]:
        total = total + value.astype(f32)
    return total.astype(bf16)


def in_hbm(value):
    return pltpu.with_memory_space_constraint(value, pltpu.HBM)


def after(value, *others):
    return lax.optimization_barrier((value, *others))[0]


def at_index(value, i):
    return lax.dynamic_index_in_dim(value, i, 0, keepdims=False)


def body(
    tokens,
    routes,
    cotangent,
    attn_gain,
    query_weight,
    key_weight,
    value_weight,
    out_weight,
    moe_gain,
    router_weight,
    expert_gate,
    expert_up,
    expert_down,
):
    half, core, late = lax.axis_index("yh"), lax.axis_index("c"), lax.axis_index("yl")
    place = lax.axis_index("x") * 4 + lax.axis_index("z")
    pos = jnp.stack([half, core, late, half * 16 + place, (late * 16 + place) * 2 + core, lax.axis_index("x"), lax.axis_index("z")]).astype(jnp.int32)
    cos, sin = rotary_tables()

    (packed,) = call(
        pack_kernel,
        [((16, 16, PACK), bf16)],
        [
            pos, query_weight, key_weight, value_weight, out_weight, router_weight,
            attn_gain.reshape(1, 16), moe_gain.reshape(1, 16),
        ],
        us=0,
    )
    w_a = plane(packed)
    tok_oth = swap(tokens, "yh")
    cot_oth = swap(cotangent, "yh")

    experts = jnp.stack([expert_gate, expert_up, expert_down])
    experts = experts.reshape(3, 16, 2, 16, 2, 128).transpose(3, 2, 0, 4, 1, 5).reshape(16, 192, 128)
    tab, tab_t, mask = call(
        route_kernel,
        [((SLOTS, SEQ), bf16), ((SEQ, SLOTS), bf16), ((SEQ, 128), f32)],
        [pos, routes],
        scratch=[pltpu.VMEM((128, SEQ), f32)],
        us=0,
    )
    grad, cot_sent = call(
        dispatch_kernel,
        [((SEQ, D), bf16), ((16, ROWS + 192, 128), bf16)],
        [pos, tab, cotangent, cot_oth, experts],
        us=3,
    )
    w_a = after(w_a, experts, cot_sent, tok_oth)
    w_b = swap(w_a, "yl")
    w_c = swap(w_a, "c")
    w_d = swap(w_b, "c")
    cot_slots = plane(after(cot_sent, w_c))

    e_own = lax.dynamic_slice_in_dim(cot_slots, ROWS + 96 * half, 96, 1)
    e_oth = lax.dynamic_slice_in_dim(cot_slots, ROWS + 96 * (1 - half), 96, 1)
    pieces = [e_own, swap(e_own, "yl"), swap(e_oth, "yh"), swap(e_oth, "diag")]
    pieces = pieces + [swap(piece, "c") for piece in pieces]
    w_gate, w_up, w_down = call(weights_kernel, [((D, 512), bf16)] * 3, [pos] + pieces, us=4, vmem=PART_BYTES)

    kept = [
        ((SEQ, D), bf16), ((128, D), f32), ((SEQ, D), bf16), ((SEQ, 512), bf16), ((SEQ, 512), bf16),
        ((SEQ, 512), bf16), ((SEQ, 512), bf16), ((4, 512, 128), f32),
    ]
    part, rows, aux, attn_in, q, k, v, ctx, lse = call(
        attn_kernel,
        [((SEQ, D), bf16)] + kept,
        [pos, tokens, tok_oth, cos, sin, w_a, w_b, w_c, w_d],
        late_from=5,
        late_outs=8,
        scratch=[pltpu.VMEM(shape, kind) for shape, kind in kept]
        + [pltpu.VMEM((2, 16, 2, 16, PACK), bf16), pltpu.SemaphoreType.DMA((12,))],
        us=7,
    )
    part_oth = swap(part, "yh")
    kept = [((SEQ, D), f32), ((SEQ, D), bf16), ((16, ROWS + 16, 128), bf16)]
    gates, middle, moe_in, x_sent = call(
        mid_kernel,
        [((SEQ, 128), f32)] + kept,
        [pos, rows, part, part_oth, aux, tab, mask],
        late_outs=3,
        scratch=[pltpu.VMEM((128, SEQ), f32)]
        + [pltpu.VMEM(shape, kind) for shape, kind in kept]
        + [pltpu.SemaphoreType.DMA((7,))],
        us=3,
    )
    x_slots = plane(x_sent)

    whole = pl.BlockSpec((D, 512), lambda i, *pos: (0, 0))
    by_row = pl.BlockSpec((4 * CAP, 512), lambda i, *pos: (i, 0))
    by_peer = lambda rows: pl.BlockSpec((4, rows, 128), lambda i, *pos: (i, 0, 0))
    dx, gate_g, up_g, scaled = call(
        expert_kernel,
        [((16, ROWS + 16, 128), bf16), ((SLOTS, 512), bf16), ((SLOTS, 512), bf16), ((SLOTS, 512), bf16)],
        [pos, in_hbm(x_slots), in_hbm(cot_slots), w_gate, w_up, w_down],
        scratch=[pltpu.VMEM((4 * CAP, D), bf16), pltpu.VMEM((4 * CAP, D), bf16)],
        grid=(4,),
        in_specs=[by_peer(ROWS + 16), by_peer(ROWS), whole, whole, whole],
        out_specs=[by_peer(ROWS + 16), by_row, by_row, by_row],
        us=12,
        hbm=True,
        vmem=PART_BYTES,
    )
    dx_back = plane(dx)

    full = pl.BlockSpec((SLOTS, 512), lambda i, *pos: (0, 0))
    by_col = pl.BlockSpec((16, 2 * CAP, 128), lambda i, *pos: (0, i, 0))
    by_owner = pl.BlockSpec((1, 2, 8, 96, 128), lambda i, pos: ((i // 2 + pos[2]) % 2, 0, i % 2, 0, 0))
    e_mine, e_sent = call(
        expert_grad_kernel,
        [((2, 2, 16, 96, 128), bf16), ((2, 2, 16, 96, 128), bf16)],
        [pos, x_slots, cot_slots, gate_g, up_g, scaled],
        scratch=[
            pltpu.VMEM((SLOTS, 256), bf16), pltpu.VMEM((SLOTS, 256), bf16), pltpu.VMEM((256, 512), bf16),
        ],
        grid=(4,),
        in_specs=[by_col, by_col, full, full, full],
        out_specs=[by_owner, by_owner],
        us=0,
        prefetch=True,
    )


    e_got = swap(e_sent, "c")
    e_yl, e_yh, e_diag = (
        swap(added(e_mine[i, j], e_got[i, j]), axis) for i, j, axis in ((1, 0, "yl"), (0, 1, "yh"), (1, 1, "diag"))
    )
    (y,) = call(
        expert_out_kernel,
        [((16, ROWS, 128), bf16)],
        [pos, after(scaled, e_got), w_down],
        grid=(4,),
        in_specs=[full, pl.BlockSpec((256, 512), lambda i, *pos: (i, 0))],
        out_specs=[by_col],
        us=0,
    )
    dx_back = after(dx_back, e_yl, y)
    (comb,) = call(
        combine_kernel, [((SEQ, EXT), bf16)], [pos, tab_t, dx_back],
        scratch=[pltpu.VMEM((SLOTS, EXT), bf16)], us=0,
    )
    comb = after(comb, e_yh, e_diag)
    comb_oth = swap(comb, "yh")
    y_back = plane(y)
    by_first = pl.BlockSpec((1, 1, 16, 96, 128), lambda i, *pos: (0, 0, 0, 0, 0))
    by_third = pl.BlockSpec((16, 96, 128), lambda i, *pos: (0, 0, 0))
    (e_cat,) = call(
        expert_sum_kernel,
        [((16, 192, 128), bf16)],
        [pos, after(e_mine, comb), e_got, e_yl, e_yh, e_diag],
        grid=(1,),
        in_specs=[by_first, by_first, by_third, by_third, by_third],
        out_specs=[pl.BlockSpec((16, 192, 128), lambda i, *pos: (0, 0, 0))],
        us=0,
    )
    comb_oth = after(comb_oth, e_cat)
    part_sent, gains, mg_own, part_own, a_mine, a_sent = call(
        back_kernel,
        [
            ((HALF, D), bf16), ((8, 128), f32), ((HALF, D), f32), ((HALF, D), f32),
            ((2, 16, 16, PACK), bf16), ((2, 16, 16, PACK), bf16),
        ],
        [
            pos, comb, comb_oth, middle, moe_in, gates, aux, grad,
            w_a, w_b, w_c, w_d, ctx, q, k, v, lse, cos, sin, attn_in, rows,
        ],
        late_from=8,
        late_outs=4,
        scratch=[
            pltpu.VMEM((2, 16, 2, 16, PACK), bf16), pltpu.VMEM((SEQ, 512), bf16), pltpu.VMEM((SEQ, 512), bf16),
            pltpu.VMEM((SEQ, 512), bf16), pltpu.VMEM((SEQ, 512), bf16), pltpu.VMEM((4, 512, 128), f32),
            pltpu.VMEM((SEQ, 256), f32), pltpu.VMEM((SEQ, 256), f32), pltpu.VMEM((SEQ, D), bf16),
            pltpu.VMEM((SEQ, D), bf16), pltpu.SemaphoreType.DMA((19,)),
            pltpu.VMEM((SEQ, D), f32), pltpu.VMEM((SEQ, D), bf16), pltpu.VMEM((2, 16, 2, 16, PACK), bf16),
            pltpu.VMEM((SEQ, 512), bf16), pltpu.VMEM((SEQ, D), f32), pltpu.VMEM((SEQ, D), f32),
        ],
        us=0,
    )

    a_got = swap(a_sent, "c")
    block = pltpu.VMEM((16, 16, PACK), bf16)
    wide = pltpu.VMEM((16, 16, PACK + 128), bf16)
    a_move, gains = call(
        move_kernel,
        [((16, 16, PACK + 128), bf16), ((16, 128), f32)],
        [pos, gains] + [swap(gains, axis) for axis in ("yh", "c", "twist")] + [a_mine, a_got],
        late_from=5,
        scratch=[block, block, pltpu.SemaphoreType.DMA((4,))],
        us=0,
    )
    a_yl = swap(a_move, "yl")
    e_back = plane(after(e_cat, y_back))
    out_own, out_sent = call(
        finish_kernel,
        [((HALF, D), f32), ((2, HALF, D), bf16)],
        [pos, tab_t, middle, after(y_back, a_move), part_sent],
        scratch=[pltpu.VMEM((SLOTS, D), bf16), pltpu.VMEM((SEQ, D), f32)],
        us=0,
    )
    a_yl = after(a_yl, out_sent)
    (a_sum,) = call(
        sum_kernel,
        [((16, 16, PACK + 128), bf16)],
        [pos, gains, a_mine, a_got, a_yl],
        late_from=2,
        scratch=[block, block, wide, pltpu.SemaphoreType.DMA((6,))],
        us=0,
    )
    total = plane(after(a_sum, e_back))
    grad_gate, grad_up, grad_down = call(
        expert_final_kernel, [((16, EXPERTS, 256), f32)] * 3, [pos, after(e_back, a_sum)], us=0
    )

    rows_oth = swap(after(out_sent, a_sum), "yh")
    w_query, w_key, w_value, w_out, w_router, gain_two, gain_one = call(
        final_kernel,
        [((16, n), f32) for n in (512, 256, 256, 512, 32)] + [((1, 16), f32)] * 2,
        [pos, total],
        us=0,
    )
    rows_oth = after(rows_oth, grad_gate, w_query)
    input_grad, output = call(
        rows_kernel,
        [((HALF, D), bf16), ((HALF, D), bf16)],
        [pos, tokens, aux, mg_own, part_own, out_own, rows_oth],
        us=0,
    )

    return (
        output,
        input_grad,
        gain_one.reshape(16),
        w_query,
        w_key,
        w_value,
        w_out,
        gain_two.reshape(16),
        w_router,
        grad_gate,
        grad_up,
        grad_down,
    )


def solution(mesh):
    fine = Mesh(mesh.devices.reshape(2, 4, 4, 2, 2), ("yl", "x", "z", "c", "yh"))
    dp, every = ("yl", "x", "z", "c"), ("yl", "x", "z", "c", "yh")
    in_specs = (
        P(every, None),
        P(dp, None),
        P(every, None),
        P(dp),
        P(dp, "yh"),
        P(dp, "yh"),
        P(dp, "yh"),
        P(dp, "yh"),
        P(dp),
        P(dp, None),
        P(dp, None, "yh"),
        P(dp, None, "yh"),
        P(dp, None, "yh"),
    )
    out_specs = (
        P(every, None),
        P(every, None),
        P(dp),
        P(dp, "yh"),
        P(dp, "yh"),
        P(dp, "yh"),
        P(dp, "yh"),
        P(dp),
        P(dp, None),
        P(dp, None, "yh"),
        P(dp, None, "yh"),
        P(dp, None, "yh"),
    )
    return jax.shard_map(body, mesh=fine, in_specs=in_specs, out_specs=out_specs, check_vma=False)
```
